32 devices in a mesh: dp: 8 (over z, y), rows: 4 (over x, core).
Axes of the slice: x: 2, y: 2, z: 4, core: 2. Of those that a mesh axis runs over, the one named last changes fastest.
Arguments:
- tokens: bfloat16 [32, 64, 64, 512], P('dp', 'rows'), may hold values from -6 to 6
- frame_level: int32 [32], P('dp'), may hold values from 0 to 2, as said below
- ln1_gain: bfloat16 [512], P(('dp', 'rows')), may hold values from 0.25 to 1.75
- ln1_bias: bfloat16 [512], P(('dp', 'rows')), may hold values from -1.5 to 1.5
- qkv_weight: bfloat16 [512, 1536], P(('dp', 'rows')), may hold values from -0.25 to 0.25
- qv_bias: bfloat16 [1024], P(('dp', 'rows')), may hold values from -2.5 to 2.5
- proj_weight: bfloat16 [512, 512], P(('dp', 'rows')), may hold values from -1 to 1
- proj_bias: bfloat16 [512], P(('dp', 'rows')), may hold values from -1.5 to 1.5
- ln2_gain: bfloat16 [512], P(('dp', 'rows')), may hold values from 0.25 to 1.75
- ln2_bias: bfloat16 [512], P(('dp', 'rows')), may hold values from -1.5 to 1.5
- fc1_weight: bfloat16 [512, 2048], P(('dp', 'rows')), may hold values from -0.25 to 0.25
- fc1_bias: bfloat16 [2048], P(('dp', 'rows')), may hold values from -2.5 to 2.5
- fc2_weight: bfloat16 [2048, 512], P(('dp', 'rows')), may hold values from -0.1875 to 0.1875
- fc2_bias: bfloat16 [512], P(('dp', 'rows')), may hold values from -1.5 to 1.5
- d_out: bfloat16 [32, 64, 64, 512], P('dp', 'rows'), may hold values from -6 to 6
Outputs:
- mixed: bfloat16 [32, 64, 64, 512], P('dp', 'rows')
- grad_tokens: bfloat16 [32, 64, 64, 512], P('dp', 'rows')
- grad_ln1_gain: float32 [512], P(('dp', 'rows'))
- grad_ln1_bias: float32 [512], P(('dp', 'rows'))
- grad_qkv_weight: float32 [512, 1536], P(('dp', 'rows'))
- grad_qv_bias: float32 [1024], P(('dp', 'rows'))
- grad_proj_weight: float32 [512, 512], P(('dp', 'rows'))
- grad_proj_bias: float32 [512], P(('dp', 'rows'))
- grad_ln2_gain: float32 [512], P(('dp', 'rows'))
- grad_ln2_bias: float32 [512], P(('dp', 'rows'))
- grad_fc1_weight: float32 [512, 2048], P(('dp', 'rows'))
- grad_fc1_bias: float32 [2048], P(('dp', 'rows'))
- grad_fc2_weight: float32 [2048, 512], P(('dp', 'rows'))
- grad_fc2_bias: float32 [512], P(('dp', 'rows'))
The draws below stay inside these ranges and needn't reach their ends.
Inputs may be any that keep to these rules, and one draw needn't show every extreme that they name: `frame_level`: in each aligned block of 4 frames, at least one frame has level 2.
All inputs are finite; a program needn't handle non-finite values.
Results may differ from the reference program's by a relative error of at most 0.012.
Values may be sent and summed in bfloat16 or wider, within the bound.
No kernel may reach another device: no remote copies, remote signals or barrier semaphores. Data moves between devices by JAX's collectives and lax.ppermute only.
A program may use at most 256 MiB of HBM per device.

```python
import jax
import jax.numpy as jnp
from jax import lax

HEADS = 8
HEAD_DIM = 64
D = 512
FF = 2048
WIN = 8
FRAME_H = 64
COLS = 64
FRAMES_DEV = 4
FRAMES = 32


def draw_frame_level(key, part):
    key = jax.random.fold_in(key, 7)
    first_key, second_key = jax.random.split(key)
    raw_levels = jax.random.randint(first_key, (FRAMES,), 0, 3)
    chosen = jax.random.randint(second_key, (FRAMES // FRAMES_DEV,), 0, FRAMES_DEV)
    position = jnp.arange(FRAMES, dtype=jnp.int32) % FRAMES_DEV
    forced = position == jnp.repeat(chosen, FRAMES_DEV, total_repeat_length=FRAMES)
    return jnp.where(forced, 2, raw_levels).astype(jnp.int32)


def with_spikes(values, key, source, target, blocks, factor):
    def block_of(dim):
        return (jnp.arange(values.shape[dim]) // (values.shape[dim] // blocks)).reshape((-1,) + (1,) * (values.ndim - 1 - dim))

    first = jax.random.permutation(key, blocks)[block_of(target)]
    second = (block_of(target) + blocks // 2) % blocks
    return jnp.where((block_of(source) == first) | (block_of(source) == second), factor * values, values)


def level_of(stream_key, dims, shards, low, top_value):
    gain, own = 1.0, jax.random.fold_in(stream_key, 6)
    for dim, shards_of in shards:
        draws = jnp.exp(jax.random.uniform(jax.random.fold_in(own, dim), (shards_of,), jnp.float32, low / len(shards), top_value / len(shards)))
        gain = gain * jnp.repeat(draws, dims[dim] // shards_of).reshape([-1 if axis == dim else 1 for axis in range(len(dims))])
    return gain


def noise(rng, dims, scale, most, pieces=(), held_as=jnp.bfloat16):
    entries = scale * jax.random.normal(rng, dims, jnp.float32)
    if pieces:
        entries = entries * level_of(rng, dims, pieces, -0.22, 0.18)
    return jnp.clip(entries, -most, most).astype(held_as)


def heavy_noise(stream_key, dims, width, reach, cuts, heavy, kind=jnp.bfloat16):
    values = width * jax.random.normal(stream_key, dims, jnp.float32)
    if cuts:
        values = values * level_of(stream_key, dims, cuts, -0.22, 0.18)
    return jnp.clip(with_spikes(values, jax.random.fold_in(stream_key, 3), *heavy), -reach, reach).astype(kind)


def setup_inputs(seed: int = 0) -> dict:
    seeds = jax.random.split(jax.random.key(seed), 16)
    return {
        "tokens": noise(seeds[0], (FRAMES, FRAME_H, COLS, D), 1.0, 6.0, ((0, 8), (1, 4))),
        "frame_level": draw_frame_level(jax.random.fold_in(seeds[15], 71), 0),
        "ln1_gain": jnp.clip(1.0 + 0.15 * jax.random.normal(seeds[2], (D,), jnp.float32), 0.25, 1.75).astype(jnp.bfloat16),
        "ln1_bias": noise(seeds[3], (D,), 0.3, 1.5, ((0, 32),)),
        "qkv_weight": noise(seeds[4], (D, 3 * D), D ** -0.5, 0.25, ((0, 32),)),
        "qv_bias": noise(seeds[5], (2 * D,), 0.5, 2.5, ((0, 32),)),
        "proj_weight": noise(seeds[6], (D, D), (D // 16) ** -0.5, 1.0, ((0, 32),)),
        "proj_bias": noise(seeds[7], (D,), 0.3, 1.5, ((0, 32),)),
        "ln2_gain": jnp.clip(1.0 + 0.15 * jax.random.normal(seeds[8], (D,), jnp.float32), 0.25, 1.75).astype(jnp.bfloat16),
        "ln2_bias": noise(seeds[9], (D,), 0.3, 1.5, ((0, 32),)),
        "fc1_weight": noise(seeds[10], (D, FF), D ** -0.5, 0.25, ((0, 32),)),
        "fc1_bias": noise(seeds[11], (FF,), 0.5, 2.5, ((0, 32),)),
        "fc2_weight": noise(seeds[12], (FF, D), (FF // 2) ** -0.5, 0.1875, ((0, 32),)),
        "fc2_bias": noise(seeds[13], (D,), 0.3, 1.5, ((0, 32),)),
        "d_out": heavy_noise(seeds[14], (FRAMES, FRAME_H, COLS, D), 1.0, 6.0, ((0, 8), (1, 4)), (0, 3, 8, 2.0)),
    }


@jax.custom_vjp
def low(v):
    return lax.optimization_barrier(v.astype(jnp.bfloat16)).astype(jnp.float32)

@jax.custom_vjp
def low_back(v):
    return v

def low_keep(v):
    return (low(v), None)

def low_pass(kept, grad):
    return (grad,)

def back_keep(v):
    return (v, None)

def back_low(kept, grad):
    return (low(grad),)
low.defvjp(low_keep, low_pass)
low_back.defvjp(back_keep, back_low)
HIGH = lax.Precision.HIGHEST

def normalize(values):
    center = values - lax.optimization_barrier(jnp.mean(values, axis=-1, keepdims=True))
    return center * lax.rsqrt(lax.optimization_barrier(jnp.mean(center * center, axis=-1, keepdims=True)) + 1e-05)

def to_windows(grid):
    leading = grid.shape[0]
    depth = grid.shape[-1]
    divided = grid.reshape(leading, FRAME_H // WIN, WIN, COLS // WIN, WIN, depth)
    return divided.transpose(0, 1, 3, 2, 4, 5).reshape(leading, FRAME_H // WIN, COLS // WIN, WIN * WIN, depth)

def from_windows(blocks):
    leading = blocks.shape[0]
    depth = blocks.shape[-1]
    divided = blocks.reshape(leading, FRAME_H // WIN, COLS // WIN, WIN, WIN, depth)
    return divided.transpose(0, 1, 3, 2, 4, 5).reshape(leading, FRAME_H, COLS, depth)

def region_of(index, length):
    return (index >= length - WIN).astype(jnp.int32) + (index >= length - WIN // 2).astype(jnp.int32)

def window_mask(levels):
    half_win = WIN // 2
    rolled_rows = jnp.arange(FRAME_H, dtype=jnp.int32)
    rolled_cols = jnp.arange(COLS, dtype=jnp.int32)
    factor = 1 + (levels >= 1).astype(jnp.int32) + 2 * (levels >= 2).astype(jnp.int32)
    row_valid = (rolled_rows + half_win) % FRAME_H < (FRAME_H * factor // 4)[:, None]
    col_valid = (rolled_cols + half_win) % COLS < (COLS * factor // 4)[:, None]
    usable = (row_valid[:, :, None] & col_valid[:, None, :]).astype(jnp.int32)[..., None]
    regions = (region_of(rolled_rows, FRAME_H)[:, None] * 3 + region_of(rolled_cols, COLS)[None, :])[None, :, :, None]
    usable_win = to_windows(usable)[..., 0]
    region_win = to_windows(regions)[..., 0]
    allowed = (region_win[..., :, None] == region_win[..., None, :]) & (usable_win[..., None, :] > 0)
    return jnp.where(allowed, 0.0, -100.0).astype(jnp.float32)[:, :, :, None]

def attend(query, keys, values, levels):
    half_win = WIN // 2
    groups = query.shape[0]

    def split_heads(grid):
        rolled = jnp.roll(grid, (-half_win, -half_win), axis=(1, 2))
        return to_windows(rolled).reshape(groups, FRAME_H // WIN, COLS // WIN, WIN * WIN, HEADS, HEAD_DIM)
    query_heads = split_heads(query)
    key_heads = split_heads(keys)
    value_heads = split_heads(values)
    scores = jnp.einsum('gabqhd,gabkhd->gabhqk', query_heads, key_heads, precision=HIGH) * HEAD_DIM ** (-0.5)
    scores = low_back(scores + window_mask(levels))
    probs = low(jax.nn.softmax(scores, axis=-1))
    result = jnp.einsum('gabhqk,gabkhd->gabqhd', probs, value_heads, precision=HIGH)
    result = result.reshape(groups, FRAME_H // WIN, COLS // WIN, WIN * WIN, D)
    return jnp.roll(from_windows(result), (half_win, half_win), axis=(1, 2))

def layer_block(params, inputs, levels):
    gain_one, bias_one, weight_qkv, bias_qv, weight_proj, bias_proj, gain_two, bias_two, weight_up, bias_up, weight_down, bias_down = params
    hidden_one = low(normalize(inputs) * gain_one + bias_one)
    projected = jnp.einsum('ghwc,ce->ghwe', hidden_one, weight_qkv, precision=HIGH)
    query = low(low_back(projected[..., :D] + bias_qv[:D]))
    keys = low(low_back(projected[..., D:2 * D]))
    values = low(low_back(projected[..., 2 * D:] + bias_qv[D:]))
    attended = low(low_back(attend(query, keys, values, levels)))
    branch = low_back(jnp.einsum('ghwc,ce->ghwe', attended, weight_proj, precision=HIGH) + bias_proj)
    middle = inputs + branch
    hidden_two = low(normalize(middle) * gain_two + bias_two)
    upward = low_back(jnp.einsum('ghwc,cf->ghwf', hidden_two, weight_up, precision=HIGH) + bias_up)
    gelu_out = low(jax.nn.gelu(upward, approximate=False))
    return middle + jnp.einsum('ghwf,fc->ghwc', gelu_out, weight_down, precision=HIGH) + bias_down

def reference(tokens, frame_level, ln1_gain, ln1_bias, qkv_weight, qv_bias, proj_weight, proj_bias, ln2_gain, ln2_bias, fc1_weight, fc1_bias, fc2_weight, fc2_bias, d_out):
    params = tuple((item.astype(jnp.float32) for item in (ln1_gain, ln1_bias, qkv_weight, qv_bias, proj_weight, proj_bias, ln2_gain, ln2_bias, fc1_weight, fc1_bias, fc2_weight, fc2_bias)))
    inputs = tokens.astype(jnp.float32)
    level_groups = frame_level.reshape(FRAMES, 1)
    checked = jax.checkpoint(layer_block)

    def forward(weights, frames_in):
        stacked = frames_in.reshape(FRAMES, 1, FRAME_H, COLS, D)

        def scan_step(carry, item):
            return (carry, checked(weights, item[0], item[1]))
        unused, outputs = lax.scan(scan_step, None, (stacked, level_groups))
        return outputs.reshape(FRAMES, FRAME_H, COLS, D)
    result, pullback = jax.vjp(forward, params, inputs)
    grad_params, grad_inputs = pullback(d_out.astype(jnp.float32))
    return (result.astype(jnp.bfloat16), grad_inputs.astype(jnp.bfloat16), grad_params[0], grad_params[1], grad_params[2], grad_params[3], grad_params[4], grad_params[5], grad_params[6], grad_params[7], grad_params[8], grad_params[9], grad_params[10], grad_params[11])
```

```python
import functools

import jax
import jax.numpy as jnp
from jax import lax
from jax.experimental import pallas as pl
from jax.experimental.pallas import tpu as pltpu
from jax.sharding import PartitionSpec as P

HEAD_DIM = 64
WIN = 8
HALF = WIN // 2
CELLS = WIN * WIN
LANES = 4 * HEAD_DIM
EPSILON = 1e-05
INV_ROOT_TWO = 0.7071067811865476
INV_ROOT_TWO_PI = 0.3989422804014327
F32 = jnp.float32
BF16 = jnp.bfloat16
VMEM_LIMIT = 60 * 1024 * 1024


def from_behind(x, axis, by):
    devices = lax.axis_size(axis)
    return lax.ppermute(x, axis, [(i, (i + by) % devices) for i in range(devices)])


def dot(a, b):
    return jnp.dot(a, b, preferred_element_type=F32)


def dot_t(a, b):
    return lax.dot_general(a, b, (((1,), (1,)), ((), ())), preferred_element_type=F32)


def to_window_order(x, columns):
    depth = x.shape[-1]
    grid = pltpu.roll(x.reshape(WIN, columns, depth), columns - HALF, 1)
    grid = grid.reshape(WIN, columns // WIN, WIN, depth).swapaxes(0, 1)
    return grid.reshape(WIN * columns, depth)


def from_window_order(x, columns):
    depth = x.shape[-1]
    grid = x.reshape(columns // WIN, WIN, WIN, depth).swapaxes(0, 1)
    grid = pltpu.roll(grid.reshape(WIN, columns, depth), HALF, 1)
    return grid.reshape(WIN * columns, depth)


def normalize(values):
    center = values - jnp.mean(values, axis=-1, keepdims=True)
    inverse = lax.rsqrt(jnp.mean(center * center, axis=-1, keepdims=True) + EPSILON)
    return center * inverse, inverse


def norm_back(grad, normed, inverse):
    return inverse * (
        grad
        - jnp.mean(grad, axis=-1, keepdims=True)
        - normed * jnp.mean(grad * normed, axis=-1, keepdims=True)
    )


def block_diag(x):
    lane_head = lax.broadcasted_iota(jnp.int32, x.shape, 1) // HEAD_DIM
    zero = jnp.zeros_like(x)
    return jnp.concatenate(
        [jnp.where(lane_head == head, x, zero) for head in range(LANES // HEAD_DIM)], axis=0
    )


def stacked_identity():
    row = lax.broadcasted_iota(jnp.int32, (CELLS, LANES), 0)
    lane = lax.broadcasted_iota(jnp.int32, (CELLS, LANES), 1)
    return jnp.where(row == lane % CELLS, 1.0, 0.0).astype(BF16)


def flip(x):
    return dot_t(stacked_identity(), block_diag(x)).astype(BF16)


def window_bias(info, frames, step, win, columns, height, rows_here):
    frame = lax.rem(step, frames)
    level = info[frame]
    factor = jnp.where(level >= 2, 4, jnp.where(level >= 1, 2, 1))
    base = info[frames] * rows_here + (step // frames) * WIN
    row_limit, col_limit = height * factor // 4, columns * factor // 4
    last_row = (base + WIN >= height).astype(jnp.int32)
    last_col = jnp.int32(win == columns // WIN - 1)
    key = lax.broadcasted_iota(jnp.int32, (CELLS, LANES), 0)
    query = lax.broadcasted_iota(jnp.int32, (CELLS, LANES), 1) % CELLS
    row = base + key // WIN + HALF
    col = win * WIN + key % WIN + HALF
    row = jnp.where(row >= height, row - height, row)
    col = jnp.where(col >= columns, col - columns, col)
    differ = key ^ query
    bad = (differ // (HALF * WIN) % 2) * last_row + (differ // HALF % 2) * last_col
    bad = bad + (row >= row_limit).astype(jnp.int32) + (col >= col_limit).astype(jnp.int32)
    return jnp.where(bad > 0, -100.0, 0.0)


def attend_kernel(
    frames, columns, height, rows_here,
    info, top, own, halo, weight, gain, bias, bias_q, bias_v,
    q_out, k_out, v_out, p_out, o_out, q_s, k_s, v_s,
):
    step = pl.program_id(0)
    width = top.shape[-1]
    bottom = jnp.where(step < frames, own[...], halo[...])
    x = jnp.concatenate([top[...], bottom], axis=0).astype(F32)
    normed, _ = normalize(to_window_order(x, columns))
    hidden = (normed * gain[...] + bias[...]).astype(BF16)
    q = (dot(hidden, weight[:, :width]) + bias_q[...]).astype(BF16) * 0.125
    k = dot(hidden, weight[:, width : 2 * width]).astype(BF16)
    v = (dot(hidden, weight[:, 2 * width :]) + bias_v[...]).astype(BF16)
    q_s[...] = q
    k_s[...] = k
    v_s[...] = v
    q_out[...] = q
    k_out[...] = k
    v_out[...] = v

    def one_window(win, carry):
        rows = pl.ds(pl.multiple_of(win * CELLS, CELLS), CELLS)
        mask = window_bias(info, frames, step, win, columns, height, rows_here)
        for group in range(width // LANES):
            lanes = slice(group * LANES, (group + 1) * LANES)
            scores = dot_t(k_s[rows, lanes], block_diag(q_s[rows, lanes])) + mask
            exponent = jnp.exp(scores - jnp.max(scores, axis=0, keepdims=True))
            probs = exponent * (1.0 / jnp.sum(exponent, axis=0, keepdims=True))
            probs = probs.astype(BF16)
            p_out[rows, lanes] = probs
            out = dot(flip(probs), block_diag(v_s[rows, lanes]))
            o_out[rows, lanes] = out.astype(BF16)
        return carry

    lax.fori_loop(0, columns // WIN, one_window, 0, unroll=2)


def middle_kernel(
    frames, columns, chunk,
    top, own, halo, dtop, down, dhalo, o_in, w_proj, w_up, w_down,
    b_proj, g_two, b_two, b_up, b_down,
    m_top, m_own, m_halo, dx_out, do_out, dw_proj, dw_up, dw_down_t, small,
):
    step = pl.program_id(0)
    width = top.shape[-1]
    hidden_width = w_up.shape[-1]

    @pl.when(step == 0)
    def _():
        dw_proj[...] = jnp.zeros_like(dw_proj)
        dw_up[...] = jnp.zeros_like(dw_up)
        dw_down_t[...] = jnp.zeros_like(dw_down_t)
        small[...] = jnp.zeros_like(small)

    bottom = jnp.where(step < frames, own[...], halo[...])
    dbottom = jnp.where(step < frames, down[...], dhalo[...])
    x = to_window_order(jnp.concatenate([top[...], bottom], axis=0).astype(F32), columns)
    dy = to_window_order(jnp.concatenate([dtop[...], dbottom], axis=0).astype(F32), columns)
    dy_low = dy.astype(BF16)
    x2 = x + dot(o_in[...], w_proj[...]) + b_proj[...]
    normed, inverse = normalize(x2)
    h2 = (normed * g_two[...] + b_two[...]).astype(BF16)
    h2_t = h2.T
    dy_t = dy_low.T
    total = x2 + b_down[...]
    dh2 = jnp.zeros_like(x2)
    for start in range(0, hidden_width, chunk):
        part = slice(start, start + chunk)
        u = dot(h2, w_up[:, part]) + b_up[:, part]
        dg = dot_t(dy_low, w_down[part, :])
        phi = 0.5 * (1.0 + lax.erf(u * INV_ROOT_TWO))
        g = (u * phi).astype(BF16)
        slope = phi + u * jnp.exp(-0.5 * u * u) * INV_ROOT_TWO_PI
        du_full = dg * slope
        du = du_full.astype(BF16)
        total += dot(g, w_down[part, :])
        dh2 += dot_t(du, w_up[:, part])
        dw_up[:, part] += dot(h2_t, du)
        dw_down_t[:, part] += dot(dy_t, g)
        small[0:1, part] += jnp.sum(du_full, axis=0, keepdims=True)
    mixed = from_window_order(total, columns).astype(BF16)
    half = mixed.shape[0] // 2
    m_top[...] = mixed[:half]

    @pl.when(step < frames)
    def _():
        m_own[...] = mixed[half:]

    @pl.when(step >= frames)
    def _():
        m_halo[...] = mixed[half:]

    small[1:2, :width] += jnp.sum(dy, axis=0, keepdims=True)
    small[2:3, :width] += jnp.sum(dh2 * normed, axis=0, keepdims=True)
    small[3:4, :width] += jnp.sum(dh2, axis=0, keepdims=True)
    dx2 = dy + norm_back(dh2 * g_two[...], normed, inverse)
    da = dx2.astype(BF16)
    small[4:5, :width] += jnp.sum(dx2, axis=0, keepdims=True)
    dx_out[...] = dx2
    dw_proj[...] += dot(o_in[...].T, da)
    do_out[...] = dot_t(da, w_proj[...]).astype(BF16)


def back_kernel(
    frames, columns,
    top, own, halo, q_in, k_in, v_in, p_in, do_in, dx_in, weight, gain, bias,
    g_top, g_own, g_halo, dw, small, d_s,
):
    step = pl.program_id(0)
    width = top.shape[-1]

    @pl.when(step == 0)
    def _():
        dw[...] = jnp.zeros_like(dw)
        small[...] = jnp.zeros_like(small)

    def one_window(win, carry):
        rows = pl.ds(pl.multiple_of(win * CELLS, CELLS), CELLS)
        for group in range(width // LANES):
            at = group * LANES
            lanes = slice(at, at + LANES)
            probs = p_in[rows, lanes]
            full = probs.astype(F32)
            do_diag = block_diag(do_in[rows, lanes])
            dv = dot(probs, do_diag)
            dp = dot_t(v_in[rows, lanes], do_diag)
            ds = full * (dp - jnp.sum(dp * full, axis=0, keepdims=True))
            ds = ds.astype(BF16)
            dk = dot(ds, block_diag(q_in[rows, lanes]))
            dq = dot(flip(ds), block_diag(k_in[rows, lanes])) * 0.125
            d_s[rows, at : at + LANES] = dq.astype(BF16)
            d_s[rows, width + at : width + at + LANES] = dk.astype(BF16)
            d_s[rows, 2 * width + at : 2 * width + at + LANES] = dv.astype(BF16)
        return carry

    lax.fori_loop(0, columns // WIN, one_window, 0, unroll=2)
    bottom = jnp.where(step < frames, own[...], halo[...])
    x = jnp.concatenate([top[...], bottom], axis=0).astype(F32)
    normed, inverse = normalize(to_window_order(x, columns))
    hidden = (normed * gain[...] + bias[...]).astype(BF16)
    d = d_s[...]
    dw[...] += dot(hidden.T, d)
    small[0:1, :] += jnp.sum(d.astype(F32), axis=0, keepdims=True)
    dh = dot_t(d, weight[...])
    small[1:2, :width] += jnp.sum(dh * normed, axis=0, keepdims=True)
    small[2:3, :width] += jnp.sum(dh, axis=0, keepdims=True)
    grad = dx_in[...] + norm_back(dh * gain[...], normed, inverse)
    grad = from_window_order(grad, columns).astype(BF16)
    half = grad.shape[0] // 2
    g_top[...] = grad[:half]

    @pl.when(step < frames)
    def _():
        g_own[...] = grad[half:]

    @pl.when(step >= frames)
    def _():
        g_halo[...] = grad[half:]


def whole(array):
    zeros = (0,) * array.ndim
    return pl.BlockSpec(array.shape, lambda s, *_: zeros, pipeline_mode=pl.Buffered(1))


def whole_out(shape):
    zeros = (0,) * len(shape)
    return pl.BlockSpec(shape, lambda s, *_: zeros)


def grid_specs(frames, cells, width):
    top = pl.BlockSpec((None, None, cells, width), lambda s, *_: (s % frames, 1 + 2 * (s // frames), 0, 0))
    own = pl.BlockSpec(
        (None, None, cells, width), lambda s, *_: (jnp.minimum(s, frames - 1), 2, 0, 0)
    )
    halo = pl.BlockSpec((None, cells, width), lambda s, *_: (jnp.maximum(s - frames, 0), 0, 0))
    return [top, own, halo]


def out_specs_of(frames, cells, width):
    top = pl.BlockSpec((None, None, cells, width), lambda s, *_: (s // frames, s % frames, 0, 0))
    own = pl.BlockSpec((None, cells, width), lambda s, *_: (jnp.minimum(s, frames - 1), 0, 0))
    halo = pl.BlockSpec((None, cells, width), lambda s, *_: (jnp.maximum(s - frames, 0), 0, 0))
    return [top, own, halo]


def params(name_vmem=VMEM_LIMIT):
    return pltpu.CompilerParams(vmem_limit_bytes=name_vmem, dimension_semantics=("arbitrary",))


def attend(info, tokens4, halo, weight, gain, bias, bias_q, bias_v, height, columns):
    frames, groups, cells, width = tokens4.shape
    steps, block = 2 * frames, 2 * cells
    row = pl.BlockSpec((None, block, width), lambda s, *_: (s, 0, 0))
    shape = jax.ShapeDtypeStruct((steps, block, width), BF16)
    vectors = (gain, bias, bias_q, bias_v)
    return pl.pallas_call(
        functools.partial(attend_kernel, frames, columns, height, groups * HALF),
        out_shape=[shape] * 5,
        grid_spec=pltpu.PrefetchScalarGridSpec(
            num_scalar_prefetch=1,
            grid=(steps,),
            in_specs=grid_specs(frames, cells, width) + [whole(weight)] + [whole(v) for v in vectors],
            out_specs=[row] * 5,
            scratch_shapes=[pltpu.VMEM((block, width), BF16)] * 3,
        ),
        compiler_params=params(),
        name="attend",
    )(info, tokens4, tokens4, halo, weight, *vectors)


def middle(tokens4, halo, d4, dhalo, o, w_proj, w_up, w_down, vectors, columns, chunk=512):
    frames, groups, cells, width = tokens4.shape
    steps, block = 2 * frames, 2 * cells
    hidden_width = w_up.shape[-1]
    row = pl.BlockSpec((None, block, width), lambda s, *_: (s, 0, 0))
    ins = grid_specs(frames, cells, width)
    return pl.pallas_call(
        functools.partial(middle_kernel, frames, columns, chunk),
        out_shape=[
            jax.ShapeDtypeStruct((2, frames, cells, width), BF16),
            jax.ShapeDtypeStruct((frames, cells, width), BF16),
            jax.ShapeDtypeStruct((frames, cells, width), BF16),
            jax.ShapeDtypeStruct((steps, block, width), F32),
            jax.ShapeDtypeStruct((steps, block, width), BF16),
            jax.ShapeDtypeStruct((width, width), F32),
            jax.ShapeDtypeStruct((width, hidden_width), F32),
            jax.ShapeDtypeStruct((width, hidden_width), F32),
            jax.ShapeDtypeStruct((8, hidden_width), F32),
        ],
        grid=(steps,),
        in_specs=ins + ins + [row] + [whole(w) for w in (w_proj, w_up, w_down)] + [whole(v) for v in vectors],
        out_specs=out_specs_of(frames, cells, width)
        + [row, row]
        + [
            whole_out((width, width)),
            whole_out((width, hidden_width)),
            whole_out((width, hidden_width)),
            whole_out((8, hidden_width)),
        ],
        compiler_params=params(),
        name="middle",
    )(tokens4, tokens4, halo, d4, d4, dhalo, o, w_proj, w_up, w_down, *vectors)


def back(tokens4, halo, q, k, v, p, do, dx, weight, gain, bias, columns):
    frames, groups, cells, width = tokens4.shape
    steps, block = 2 * frames, 2 * cells
    row = pl.BlockSpec((None, block, width), lambda s, *_: (s, 0, 0))
    return pl.pallas_call(
        functools.partial(back_kernel, frames, columns),
        out_shape=[
            jax.ShapeDtypeStruct((2, frames, cells, width), BF16),
            jax.ShapeDtypeStruct((frames, cells, width), BF16),
            jax.ShapeDtypeStruct((frames, cells, width), BF16),
            jax.ShapeDtypeStruct((width, 3 * width), F32),
            jax.ShapeDtypeStruct((8, 3 * width), F32),
        ],
        grid=(steps,),
        in_specs=grid_specs(frames, cells, width) + [row] * 6 + [whole(weight), whole(gain), whole(bias)],
        out_specs=out_specs_of(frames, cells, width)
        + [whole_out((width, 3 * width)), whole_out((8, 3 * width))],
        scratch_shapes=[pltpu.VMEM((block, 3 * width), BF16)],
        compiler_params=params(),
        name="back",
    )(tokens4, tokens4, halo, q, k, v, p, do, dx, weight, gain, bias)


def per_device(
    tokens, frame_level, ln1_gain, ln1_bias, qkv_weight, qv_bias, proj_weight, proj_bias,
    ln2_gain, ln2_bias, fc1_weight, fc1_bias, fc2_weight, fc2_bias, d_out,
):
    frames, rows_here, columns, width = tokens.shape
    height = rows_here * lax.axis_size("rows")
    axes = ("dp", "rows")
    cells = HALF * columns
    grouped = (frames, rows_here // HALF, cells, width)
    tokens4, d4 = tokens.reshape(grouped), d_out.reshape(grouped)
    halo = from_behind(tokens4[:, 0], "rows", -1)
    dhalo = from_behind(d4[:, 0], "rows", -1)
    gather = lambda w: lax.all_gather(w, axes, axis=0, tiled=True)
    w_qkv, w_proj, w_up, w_down = (gather(w) for w in (qkv_weight, proj_weight, fc1_weight, fc2_weight))
    vec = lambda v: gather(v).astype(F32)[None, :]
    gain_one, bias_one, bias_qv = vec(ln1_gain), vec(ln1_bias), vec(qv_bias)
    info = jnp.concatenate([frame_level, lax.axis_index("rows").astype(jnp.int32)[None]])
    q, k, v, p, o = attend(
        info, tokens4, halo, w_qkv, gain_one, bias_one, bias_qv[:, :width], bias_qv[:, width:],
        height, columns,
    )
    vectors = tuple(vec(v) for v in (proj_bias, ln2_gain, ln2_bias, fc1_bias, fc2_bias))
    m_top, m_own, m_halo, dx, do, dw_proj, dw_up, dw_down_t, small = middle(
        tokens4, halo, d4, dhalo, o, w_proj, w_up, w_down, vectors, columns
    )
    g_top, g_own, g_halo, dw_qkv, small_back = back(
        tokens4, halo, q, k, v, p, do, dx, w_qkv, gain_one, bias_one, columns
    )

    def assemble(top, own, back_rows):
        returned = from_behind(back_rows, "rows", 1)
        return jnp.stack([returned, top[0], own, top[1]], axis=1).reshape(tokens.shape)

    scatter = lambda g: lax.psum_scatter(g, axes, scatter_dimension=0, tiled=True)
    return (
        assemble(m_top, m_own, m_halo),
        assemble(g_top, g_own, g_halo),
        scatter(small_back[1, :width]),
        scatter(small_back[2, :width]),
        scatter(dw_qkv),
        scatter(jnp.concatenate([small_back[0, :width], small_back[0, 2 * width :]])),
        scatter(dw_proj),
        scatter(small[4, :width]),
        scatter(small[2, :width]),
        scatter(small[3, :width]),
        scatter(dw_up),
        scatter(small[0]),
        scatter(dw_down_t.T),
        scatter(small[1, :width]),
    )


def solution(mesh):
    both = ("dp", "rows")
    frame, vector, matrix = P("dp", "rows", None, None), P(both), P(both, None)
    return jax.shard_map(
        per_device,
        mesh=mesh,
        in_specs=(
            frame, P("dp"), vector, vector, matrix, vector, matrix, vector,
            vector, vector, matrix, vector, matrix, vector, frame,
        ),
        out_specs=(
            frame, frame, vector, vector, matrix, vector, matrix, vector,
            vector, vector, matrix, vector, matrix, vector,
        ),
        check_vma=False,
    )
```

```python
import functools

import jax
import jax.numpy as jnp
from jax import lax
from jax.experimental import pallas as pl
from jax.experimental.pallas import tpu as pltpu
from jax.sharding import PartitionSpec as P

HEAD_DIM = 64
WIN = 8
HALF = WIN // 2
CELLS = WIN * WIN
LANES = 4 * HEAD_DIM
LANE = 128
ROWS = 16
EPSILON = 1e-05
INV_ROOT_TWO = 0.7071067811865476
INV_ROOT_TWO_PI = 0.3989422804014327
F32 = jnp.float32
BF16 = jnp.bfloat16
VMEM_LIMIT = 60 * 1024 * 1024


def from_behind(x, axis, by):
    devices = lax.axis_size(axis)
    return lax.ppermute(x, axis, [(i, (i + by) % devices) for i in range(devices)])


def dot(a, b):
    return jnp.dot(a, b, preferred_element_type=F32)


def dot_t(a, b):
    return lax.dot_general(a, b, (((1,), (1,)), ((), ())), preferred_element_type=F32)


def to_window_order(x, columns):
    depth = x.shape[-1]
    grid = pltpu.roll(x.reshape(WIN, columns, depth), columns - HALF, 1)
    grid = grid.reshape(WIN, columns // WIN, WIN, depth).swapaxes(0, 1)
    return grid.reshape(WIN * columns, depth)


def from_window_order(x, columns):
    depth = x.shape[-1]
    grid = x.reshape(columns // WIN, WIN, WIN, depth).swapaxes(0, 1)
    grid = pltpu.roll(grid.reshape(WIN, columns, depth), HALF, 1)
    return grid.reshape(WIN * columns, depth)


def normalize(values):
    center = values - jnp.mean(values, axis=-1, keepdims=True)
    inverse = lax.rsqrt(jnp.mean(center * center, axis=-1, keepdims=True) + EPSILON)
    return center * inverse, inverse


def norm_back(grad, normed, inverse):
    return inverse * (
        grad
        - jnp.mean(grad, axis=-1, keepdims=True)
        - normed * jnp.mean(grad * normed, axis=-1, keepdims=True)
    )


def block_diag(x):
    lane_head = lax.broadcasted_iota(jnp.int32, x.shape, 1) // HEAD_DIM
    zero = jnp.zeros_like(x)
    return jnp.concatenate(
        [jnp.where(lane_head == head, x, zero) for head in range(LANES // HEAD_DIM)], axis=0
    )


def stacked_identity():
    row = lax.broadcasted_iota(jnp.int32, (CELLS, LANES), 0)
    lane = lax.broadcasted_iota(jnp.int32, (CELLS, LANES), 1)
    return jnp.where(row == lane % CELLS, 1.0, 0.0).astype(BF16)


def flip(x):
    return dot_t(stacked_identity(), block_diag(x)).astype(BF16)


def window_bias(info, frames, step, win, columns, height, rows_here):
    frame = lax.rem(step, frames)
    level = info[frame]
    factor = jnp.where(level >= 2, 4, jnp.where(level >= 1, 2, 1))
    base = info[frames] * rows_here + (step // frames) * WIN
    row_limit, col_limit = height * factor // 4, columns * factor // 4
    last_row = (base + WIN >= height).astype(jnp.int32)
    last_col = jnp.int32(win == columns // WIN - 1)
    key = lax.broadcasted_iota(jnp.int32, (CELLS, LANES), 0)
    query = lax.broadcasted_iota(jnp.int32, (CELLS, LANES), 1) % CELLS
    row = base + key // WIN + HALF
    col = win * WIN + key % WIN + HALF
    row = jnp.where(row >= height, row - height, row)
    col = jnp.where(col >= columns, col - columns, col)
    differ = key ^ query
    bad = (differ // (HALF * WIN) % 2) * last_row + (differ // HALF % 2) * last_col
    bad = bad + (row >= row_limit).astype(jnp.int32) + (col >= col_limit).astype(jnp.int32)
    return jnp.where(bad > 0, -100.0, 0.0)


def place(info, at, mine, theirs, targets, vec, sem, vec_sem):
    copies = []
    for core, source in enumerate((mine, theirs)):
        for j in range(source.shape[0]):
            block = info[at] ^ (bits_of(j) | core)
            for lane, lanes, rows, target in targets:
                for sub in range(rows // ROWS):
                    row = pl.multiple_of(block * rows + sub * ROWS, ROWS)
                    copies.append(
                        pltpu.make_async_copy(
                            source.at[j, :, pl.ds(lane + sub * lanes, lanes)],
                            target.at[pl.ds(row, ROWS), :],
                            sem,
                        )
                    )
        lanes = vec.shape[-1]
        blocks = source.shape[0]
        copies.append(
            pltpu.make_async_copy(
                source.at[:, :, pl.ds(source.shape[-1] - lanes, lanes)],
                vec.at[pl.ds(core * blocks, blocks)],
                vec_sem,
            )
        )
    for copy in copies:
        copy.start()


def wait_bytes(targets, sem):
    for target in targets:
        pltpu.make_async_copy(target, target, sem).wait()


def bits_of(j):
    return (j % 4) * 8 + (j // 8) * 4 + (j // 4 % 2) * 2


def natural_rows(vec):
    total = jnp.sum(vec[...].astype(F32), axis=0)
    return [total[r : r + 1, :] for r in range(total.shape[0])]


def hand_over(info, at, sources, tail, keep, send):
    for core, out in enumerate((keep, send)):
        for j in range(out.shape[0]):
            block = info[at] ^ (bits_of(j) | core)
            for lane, lanes, rows, source in sources:
                for sub in range(rows // ROWS):
                    row = pl.multiple_of(block * rows + sub * ROWS, ROWS)
                    start = lane + sub * lanes
                    out[j, :, start : start + lanes] = source[pl.ds(row, ROWS), :].astype(out.dtype)
            out[j, :, out.shape[-1] - tail.shape[-1] :] = tail.astype(out.dtype)


def attend_kernel(
    frames, columns, height, rows_here, first,
    info, top, own, halo, mine, theirs, *rest,
):
    q_out, k_out, v_out, p_out, o_out, q_s, k_s, v_s, weight, vec, lines, sem = rest[-12:]
    step = pl.program_id(0) + first
    width = top.shape[-1]

    @pl.when(pl.program_id(0) == 0)
    def _():
        place(info, frames + 1, mine, theirs, [(0, 3 * width, ROWS, weight)], vec, sem.at[0], sem.at[1])
        wait_bytes([weight], sem.at[0])
        wait_bytes([vec], sem.at[1])
        pieces = natural_rows(vec)
        per = width // LANE
        for line in range(lines.shape[0]):
            lines[line : line + 1, :] = jnp.concatenate(pieces[line * per : (line + 1) * per], axis=1)

    gain, bias, bias_q, bias_v = (lines.at[i : i + 1] for i in range(4))
    bottom = jnp.where(step < frames, own[...], halo[...])
    x = jnp.concatenate([top[...], bottom], axis=0).astype(F32)
    normed, _ = normalize(to_window_order(x, columns))
    hidden = (normed * gain[...] + bias[...]).astype(BF16)
    q = (dot(hidden, weight[:, :width]) + bias_q[...]).astype(BF16) * 0.125
    k = dot(hidden, weight[:, width : 2 * width]).astype(BF16)
    v = (dot(hidden, weight[:, 2 * width :]) + bias_v[...]).astype(BF16)
    q_s[...] = q
    k_s[...] = k
    v_s[...] = v
    q_out[...] = q
    k_out[...] = k
    v_out[...] = v

    def one_window(win, carry):
        rows = pl.ds(pl.multiple_of(win * CELLS, CELLS), CELLS)
        mask = window_bias(info, frames, step, win, columns, height, rows_here)
        for group in range(width // LANES):
            lanes = slice(group * LANES, (group + 1) * LANES)
            scores = dot_t(k_s[rows, lanes], block_diag(q_s[rows, lanes])) + mask
            exponent = jnp.exp(scores - jnp.max(scores, axis=0, keepdims=True))
            probs = exponent * (1.0 / jnp.sum(exponent, axis=0, keepdims=True))
            probs = probs.astype(BF16)
            p_out[rows, lanes] = probs
            out = dot(flip(probs), block_diag(v_s[rows, lanes]))
            o_out[rows, lanes] = out.astype(BF16)
        return carry

    lax.fori_loop(0, columns // WIN, one_window, 0, unroll=2)


def middle_kernel(
    frames, columns, chunk,
    info, top, own, halo, dtop, down, dhalo, o_in, mine, theirs,
    m_top, m_own, m_halo, dx_out, do_out, keep, send,
    w_proj, w_up, w_down, vec, lines, b_up, dw_proj, dw_up, dw_down_t, dw_down, small, sem,
):
    step = pl.program_id(0)
    width = top.shape[-1]
    hidden_width = w_up.shape[-1]
    b_proj, g_two, b_two, b_down = (lines.at[i : i + 1] for i in range(4))

    @pl.when(step == 0)
    def _():
        targets = [
            (0, width, ROWS, w_proj),
            (width, hidden_width, ROWS, w_up),
            (width + hidden_width, width, w_down.shape[0] // 32, w_down),
        ]
        place(info, frames + 1, mine, theirs, targets, vec, sem.at[0], sem.at[1])
        wait_bytes([w_proj, w_up, w_down], sem.at[0])
        wait_bytes([vec], sem.at[1])
        pieces = natural_rows(vec)
        per = width // pieces[0].shape[-1]
        for line in range(4):
            lines[line : line + 1, :] = jnp.concatenate(pieces[line * per : (line + 1) * per], axis=1)
        b_up[...] = jnp.concatenate(pieces[4 * per :], axis=1)
        dw_proj[...] = jnp.zeros_like(dw_proj)
        dw_up[...] = jnp.zeros_like(dw_up)
        dw_down_t[...] = jnp.zeros_like(dw_down_t)
        small[...] = jnp.zeros_like(small)

    bottom = jnp.where(step < frames, own[...], halo[...])
    dbottom = jnp.where(step < frames, down[...], dhalo[...])
    x = to_window_order(jnp.concatenate([top[...], bottom], axis=0).astype(F32), columns)
    dy = to_window_order(jnp.concatenate([dtop[...], dbottom], axis=0).astype(F32), columns)
    dy_low = dy.astype(BF16)
    x2 = x + dot(o_in[...], w_proj[...]) + b_proj[...]
    normed, inverse = normalize(x2)
    h2 = (normed * g_two[...] + b_two[...]).astype(BF16)
    h2_t = h2.T
    dy_t = dy_low.T
    total = x2 + b_down[...]
    dh2 = jnp.zeros_like(x2)
    for start in range(0, hidden_width, chunk):
        part = slice(start, start + chunk)
        u = dot(h2, w_up[:, part]) + b_up[:, part]
        dg = dot_t(dy_low, w_down[part, :])
        phi = 0.5 * (1.0 + lax.erf(u * INV_ROOT_TWO))
        g = (u * phi).astype(BF16)
        slope = phi + u * jnp.exp(-0.5 * u * u) * INV_ROOT_TWO_PI
        du_full = dg * slope
        du = du_full.astype(BF16)
        total += dot(g, w_down[part, :])
        dh2 += dot_t(du, w_up[:, part])
        dw_up[:, part] += dot(h2_t, du)
        dw_down_t[:, part] += dot(dy_t, g)
        small[0:1, part] += jnp.sum(du_full, axis=0, keepdims=True)
    mixed = from_window_order(total, columns).astype(BF16)
    half = mixed.shape[0] // 2
    m_top[...] = mixed[:half]

    @pl.when(step < frames)
    def _():
        m_own[...] = mixed[half:]

    @pl.when(step >= frames)
    def _():
        m_halo[...] = mixed[half:]

    small[1:2, :width] += jnp.sum(dy, axis=0, keepdims=True)
    small[2:3, :width] += jnp.sum(dh2 * normed, axis=0, keepdims=True)
    small[3:4, :width] += jnp.sum(dh2, axis=0, keepdims=True)
    dx2 = dy + norm_back(dh2 * g_two[...], normed, inverse)
    da = dx2.astype(BF16)
    small[4:5, :width] += jnp.sum(dx2, axis=0, keepdims=True)
    dx_out[...] = dx2
    dw_proj[...] += dot(o_in[...].T, da)
    do_out[...] = dot_t(da, w_proj[...]).astype(BF16)

    @pl.when(step == pl.num_programs(0) - 1)
    def _():
        for lane in range(0, hidden_width, LANE):
            dw_down[lane : lane + LANE, :] = dw_down_t[:, lane : lane + LANE].T
        order = (4, 2, 3, 1)
        flat = jnp.concatenate([small[r : r + 1, :width] for r in order] + [small[0:1, :]], axis=1)
        lines_of = keep.shape[-1] - width - 2 * hidden_width
        tail = jnp.concatenate(
            [flat[:, i * lines_of : (i + 1) * lines_of] for i in range(ROWS)], axis=0
        )
        sources = [
            (0, width, ROWS, dw_proj),
            (width, hidden_width, ROWS, dw_up),
            (width + hidden_width, width, dw_down.shape[0] // 32, dw_down),
        ]
        hand_over(info, frames + 1, sources, tail, keep, send)


def back_kernel(
    frames, columns,
    info, top, own, halo, q_in, k_in, v_in, p_in, do_in, dx_in, mine, theirs,
    g_top, g_own, g_halo, keep, send, d_s, weight, vec, lines, dw, small, sem,
):
    step = pl.program_id(0)
    width = top.shape[-1]
    gain, bias = (lines.at[i : i + 1] for i in range(2))

    @pl.when(step == 0)
    def _():
        place(info, frames + 1, mine, theirs, [(0, 3 * width, ROWS, weight)], vec, sem.at[0], sem.at[1])
        wait_bytes([weight], sem.at[0])
        wait_bytes([vec], sem.at[1])
        pieces = natural_rows(vec)
        per = width // LANE
        for line in range(lines.shape[0]):
            lines[line : line + 1, :] = jnp.concatenate(pieces[line * per : (line + 1) * per], axis=1)
        dw[...] = jnp.zeros_like(dw)
        small[...] = jnp.zeros_like(small)

    def one_window(win, carry):
        rows = pl.ds(pl.multiple_of(win * CELLS, CELLS), CELLS)
        for group in range(width // LANES):
            at = group * LANES
            lanes = slice(at, at + LANES)
            probs = p_in[rows, lanes]
            full = probs.astype(F32)
            do_diag = block_diag(do_in[rows, lanes])
            dv = dot(probs, do_diag)
            dp = dot_t(v_in[rows, lanes], do_diag)
            ds = full * (dp - jnp.sum(dp * full, axis=0, keepdims=True))
            ds = ds.astype(BF16)
            dk = dot(ds, block_diag(q_in[rows, lanes]))
            dq = dot(flip(ds), block_diag(k_in[rows, lanes])) * 0.125
            d_s[rows, at : at + LANES] = dq.astype(BF16)
            d_s[rows, width + at : width + at + LANES] = dk.astype(BF16)
            d_s[rows, 2 * width + at : 2 * width + at + LANES] = dv.astype(BF16)
        return carry

    lax.fori_loop(0, columns // WIN, one_window, 0, unroll=2)
    bottom = jnp.where(step < frames, own[...], halo[...])
    x = jnp.concatenate([top[...], bottom], axis=0).astype(F32)
    normed, inverse = normalize(to_window_order(x, columns))
    hidden = (normed * gain[...] + bias[...]).astype(BF16)
    d = d_s[...]
    dw[...] += dot(hidden.T, d)
    small[0:1, :] += jnp.sum(d.astype(F32), axis=0, keepdims=True)
    dh = dot_t(d, weight[...])
    small[1:2, :width] += jnp.sum(dh * normed, axis=0, keepdims=True)
    small[2:3, :width] += jnp.sum(dh, axis=0, keepdims=True)
    grad = dx_in[...] + norm_back(dh * gain[...], normed, inverse)
    grad = from_window_order(grad, columns).astype(BF16)
    half = grad.shape[0] // 2
    g_top[...] = grad[:half]

    @pl.when(step < frames)
    def _():
        g_own[...] = grad[half:]

    @pl.when(step >= frames)
    def _():
        g_halo[...] = grad[half:]

    @pl.when(step == pl.num_programs(0) - 1)
    def _():
        pieces = [small[1:2, :width], small[2:3, :width], small[0:1, :width], small[0:1, 2 * width :]]
        flat = jnp.concatenate(pieces, axis=1)
        tail = jnp.concatenate([flat[:, i * LANE : (i + 1) * LANE] for i in range(ROWS)], axis=0)
        hand_over(info, frames + 1, [(0, 3 * width, ROWS, dw)], tail, keep, send)


def grid_specs(frames, cells, width, first=0):
    top = pl.BlockSpec(
        (None, None, cells, width),
        lambda s, *_: ((s + first) % frames, 1 + 2 * ((s + first) // frames), 0, 0),
    )
    own = pl.BlockSpec(
        (None, None, cells, width), lambda s, *_: (jnp.minimum(s + first, frames - 1), 2, 0, 0)
    )
    halo = pl.BlockSpec(
        (None, cells, width), lambda s, *_: (jnp.maximum(s + first - frames, 0), 0, 0)
    )
    return [top, own, halo]


def out_specs_of(frames, cells, width):
    top = pl.BlockSpec((None, None, cells, width), lambda s, *_: (s // frames, s % frames, 0, 0))
    own = pl.BlockSpec((None, cells, width), lambda s, *_: (jnp.minimum(s, frames - 1), 0, 0))
    halo = pl.BlockSpec((None, cells, width), lambda s, *_: (jnp.maximum(s - frames, 0), 0, 0))
    return [top, own, halo]


def whole_out(shape):
    zeros = (0,) * len(shape)
    return pl.BlockSpec(shape, lambda s, *_: zeros, pipeline_mode=pl.Buffered(1))


ANYWHERE = pl.BlockSpec(memory_space=pl.ANY)


def params():
    return pltpu.CompilerParams(vmem_limit_bytes=VMEM_LIMIT, dimension_semantics=("arbitrary",))


def attend(info, tokens4, halo, blocks, previous, first, height, columns):
    frames, groups, cells, width = tokens4.shape
    steps, block = 2 * frames, 2 * cells
    row = pl.BlockSpec((None, block, width), lambda s, *_: (s + first, 0, 0))
    shape = jax.ShapeDtypeStruct((steps, block, width), BF16)
    held = 6
    return pl.pallas_call(
        functools.partial(attend_kernel, frames, columns, height, groups * HALF, first),
        out_shape=[shape] * 5,
        grid_spec=pltpu.PrefetchScalarGridSpec(
            num_scalar_prefetch=1,
            grid=(frames,),
            in_specs=grid_specs(frames, cells, width, first) + [ANYWHERE] * (2 + len(previous)),
            out_specs=[row] * 5,
            scratch_shapes=[pltpu.VMEM((block, width), BF16)] * 3
            + [
                pltpu.VMEM((width, 3 * width), BF16),
                pltpu.VMEM((32, ROWS, LANE), BF16),
                pltpu.VMEM((4, width), F32),
                pltpu.SemaphoreType.DMA((2,)),
            ],
        ),
        input_output_aliases={held + i: i for i in range(len(previous))},
        compiler_params=params(),
        cost_estimate=pl.CostEstimate(flops=3 * 10**10, bytes_accessed=2 * 10**7, transcendentals=10**6),
        name="attend",
    )(info, tokens4, tokens4, halo, *blocks, *previous)


def middle(info, tokens4, halo, d4, dhalo, o, blocks, hidden_width, columns, chunk=512):
    frames, groups, cells, width = tokens4.shape
    steps, block = 2 * frames, 2 * cells
    row = pl.BlockSpec((None, block, width), lambda s, *_: (s, 0, 0))
    ins = grid_specs(frames, cells, width)
    mine = blocks[0].shape
    return pl.pallas_call(
        functools.partial(middle_kernel, frames, columns, chunk),
        out_shape=[
            jax.ShapeDtypeStruct((2, frames, cells, width), BF16),
            jax.ShapeDtypeStruct((frames, cells, width), BF16),
            jax.ShapeDtypeStruct((frames, cells, width), BF16),
            jax.ShapeDtypeStruct((steps, block, width), F32),
            jax.ShapeDtypeStruct((steps, block, width), BF16),
            jax.ShapeDtypeStruct(mine, F32),
            jax.ShapeDtypeStruct(mine, BF16),
        ],
        grid_spec=pltpu.PrefetchScalarGridSpec(
            num_scalar_prefetch=1,
            grid=(steps,),
            in_specs=ins + ins + [row, ANYWHERE, ANYWHERE],
            out_specs=out_specs_of(frames, cells, width) + [row, row, whole_out(mine), whole_out(mine)],
            scratch_shapes=[
                pltpu.VMEM((width, width), BF16),
                pltpu.VMEM((width, hidden_width), BF16),
                pltpu.VMEM((hidden_width, width), BF16),
                pltpu.VMEM((32, ROWS, 2 * LANE), BF16),
                pltpu.VMEM((4, width), F32),
                pltpu.VMEM((1, hidden_width), F32),
                pltpu.VMEM((width, width), F32),
                pltpu.VMEM((width, hidden_width), F32),
                pltpu.VMEM((width, hidden_width), F32),
                pltpu.VMEM((hidden_width, width), F32),
                pltpu.VMEM((8, hidden_width), F32),
                pltpu.SemaphoreType.DMA((2,)),
            ],
        ),
        compiler_params=params(),
        cost_estimate=pl.CostEstimate(flops=8 * 10**10, bytes_accessed=4 * 10**7, transcendentals=10**7),
        name="middle",
    )(info, tokens4, tokens4, halo, d4, d4, dhalo, o, *blocks)


def back(info, tokens4, halo, q, k, v, p, do, dx, blocks, columns):
    frames, groups, cells, width = tokens4.shape
    steps, block = 2 * frames, 2 * cells
    row = pl.BlockSpec((None, block, width), lambda s, *_: (s, 0, 0))
    mine = blocks[0].shape
    return pl.pallas_call(
        functools.partial(back_kernel, frames, columns),
        out_shape=[
            jax.ShapeDtypeStruct((2, frames, cells, width), BF16),
            jax.ShapeDtypeStruct((frames, cells, width), BF16),
            jax.ShapeDtypeStruct((frames, cells, width), BF16),
            jax.ShapeDtypeStruct(mine, F32),
            jax.ShapeDtypeStruct(mine, BF16),
        ],
        grid_spec=pltpu.PrefetchScalarGridSpec(
            num_scalar_prefetch=1,
            grid=(steps,),
            in_specs=grid_specs(frames, cells, width) + [row] * 6 + [ANYWHERE, ANYWHERE],
            out_specs=out_specs_of(frames, cells, width) + [whole_out(mine), whole_out(mine)],
            scratch_shapes=[
                pltpu.VMEM((block, 3 * width), BF16),
                pltpu.VMEM((width, 3 * width), BF16),
                pltpu.VMEM((32, ROWS, LANE), BF16),
                pltpu.VMEM((4, width), F32),
                pltpu.VMEM((width, 3 * width), F32),
                pltpu.VMEM((8, 3 * width), F32),
                pltpu.SemaphoreType.DMA((2,)),
            ],
        ),
        compiler_params=params(),
        cost_estimate=pl.CostEstimate(flops=4 * 10**10, bytes_accessed=4 * 10**7, transcendentals=10**6),
        name="back",
    )(info, tokens4, tokens4, halo, q, k, v, p, do, dx, *blocks)


AXES = ("dp", "rows")


def flip_perm(axis, bits):
    return [(i, i ^ bits) for i in range(lax.axis_size(axis))]


def flipped(x, axis, bits):
    return lax.ppermute(x, axis, flip_perm(axis, bits))


def flipped_both(x, dp_bits, rows_bits):
    dp, rows = lax.axis_size("dp"), lax.axis_size("rows")
    pairs = [
        (d * rows + r, (d ^ dp_bits) * rows + (r ^ rows_bits)) for d in range(dp) for r in range(rows)
    ]
    return lax.ppermute(x, AXES, pairs)


def is_cube():
    return lax.axis_size("dp") == 8 and lax.axis_size("rows") == 4


def place_index():
    return lax.axis_index("dp") * lax.axis_size("rows") + lax.axis_index("rows")


def spread(shards):
    index = place_index()
    parts = []
    for shard in shards:
        count = shard.shape[0]
        whole_size = count * lax.axis_size("dp") * lax.axis_size("rows")
        zeros = jnp.zeros((whole_size,), shard.dtype)
        parts.append(lax.dynamic_update_slice(zeros, shard, (index * count,)))
    return jnp.concatenate(parts).reshape(ROWS, -1)


def gather_blocks(matrices, vectors):
    if is_cube():
        pieces = []
        for m in matrices:
            pieces += [m[i : i + ROWS] for i in range(0, m.shape[0], ROWS)]
        own = jnp.concatenate(pieces + [spread(vectors)], axis=1)
        column = jnp.stack([own] + [flipped(own, "dp", 2 * z) for z in (1, 2, 3)])
        plane = [column, flipped(column, "rows", 2), flipped(column, "dp", 1), flipped_both(column, 1, 2)]
        mine = jnp.concatenate(plane)
        return mine, flipped(mine, "rows", 1)
    full = [lax.all_gather(m, AXES, axis=0, tiled=True) for m in matrices]
    lanes = []
    for m in full:
        per = m.shape[0] // 32
        blocks = m.reshape(32, per // ROWS, ROWS, m.shape[1]).transpose(0, 2, 1, 3)
        lanes.append(blocks.reshape(32, ROWS, -1))
    flat = jnp.concatenate([lax.all_gather(v, AXES, axis=0, tiled=True) for v in vectors])
    tail = flat.reshape(1, ROWS, -1)
    lanes.append(jnp.concatenate([tail, jnp.zeros((31,) + tail.shape[1:], tail.dtype)]))
    natural = jnp.concatenate(lanes, axis=2)
    relative = natural.reshape(4, 2, 2, 2, ROWS, -1).transpose(3, 1, 2, 0, 4, 5)
    relative = relative.reshape(2, 16, ROWS, -1)
    return relative[0], relative[1]


def scatter_sums(keep, send, matrix_shapes, vector_sizes):
    shards = lax.axis_size("dp") * lax.axis_size("rows")
    matrices = []
    if is_cube():
        first = keep + flipped(send, "rows", 1).astype(F32)
        low = first[4:].astype(BF16)
        plane = (
            first[:4]
            + flipped(low[:4], "rows", 2).astype(F32)
            + flipped(low[4:8], "dp", 1).astype(F32)
            + flipped_both(low[8:], 1, 2).astype(F32)
        )
        low = plane[1:].astype(BF16)
        total = plane[0]
        for z in (1, 2, 3):
            total += flipped(low[z - 1], "dp", 2 * z).astype(F32)
        lane = 0
        for rows, lanes in matrix_shapes:
            per = rows // shards
            pieces = [total[:, lane + i * lanes : lane + (i + 1) * lanes] for i in range(per // ROWS)]
            matrices.append(jnp.concatenate(pieces, axis=0))
            lane += per // ROWS * lanes
        flat = total[:, lane:].reshape(-1)
    else:
        relative = jnp.stack([keep, send.astype(F32)]).reshape(2, 2, 2, 4, ROWS, -1)
        natural = relative.transpose(3, 1, 2, 0, 4, 5).reshape(32, ROWS, -1)
        lane = 0
        for rows, lanes in matrix_shapes:
            subs = rows // 32 // ROWS
            piece = natural[:, :, lane : lane + subs * lanes].reshape(32, ROWS, subs, lanes)
            whole_matrix = piece.transpose(0, 2, 1, 3).reshape(rows, lanes)
            matrices.append(lax.psum_scatter(whole_matrix, AXES, scatter_dimension=0, tiled=True))
            lane += subs * lanes
        flat = lax.psum(natural[0, :, lane:], AXES).reshape(-1)
    vectors, start = [], 0
    for size in vector_sizes:
        count = size // shards
        vectors.append(lax.dynamic_slice(flat, (start + place_index() * count,), (count,)))
        start += size
    return matrices, vectors


def per_device(
    tokens, frame_level, ln1_gain, ln1_bias, qkv_weight, qv_bias, proj_weight, proj_bias,
    ln2_gain, ln2_bias, fc1_weight, fc1_bias, fc2_weight, fc2_bias, d_out,
):
    frames, rows_here, columns, width = tokens.shape
    height = rows_here * lax.axis_size("rows")
    hidden_width = fc1_weight.shape[1]
    cells = HALF * columns
    grouped = (frames, rows_here // HALF, cells, width)
    tokens4, d4 = tokens.reshape(grouped), d_out.reshape(grouped)
    attend_blocks = gather_blocks((qkv_weight,), (ln1_gain, ln1_bias, qv_bias))
    halo = from_behind(tokens4[:, 0], "rows", -1)
    middle_blocks = gather_blocks(
        (proj_weight, fc1_weight, fc2_weight), (proj_bias, ln2_gain, ln2_bias, fc2_bias, fc1_bias)
    )
    dhalo = from_behind(d4[:, 0], "rows", -1)
    me = place_index() if is_cube() else 0
    info = jnp.concatenate(
        [frame_level, jnp.stack([lax.axis_index("rows"), jnp.int32(me)]).astype(jnp.int32)]
    )
    early = attend(info, tokens4, halo, attend_blocks, (), 0, height, columns)
    q, k, v, p, o = attend(info, tokens4, halo, attend_blocks, early, frames, height, columns)
    m_top, m_own, m_halo, dx, do, keep, send = middle(
        info, tokens4, halo, d4, dhalo, o, middle_blocks, hidden_width, columns
    )
    (dw_proj, dw_up, dw_down), (db_proj, dg_two, db_two, db_down, db_up) = scatter_sums(
        keep,
        send,
        ((width, width), (width, hidden_width), (hidden_width, width)),
        (width, width, width, width, hidden_width),
    )
    g_top, g_own, g_halo, keep, send = back(
        info, tokens4, halo, q, k, v, p, do, dx, attend_blocks, columns
    )
    (dw_qkv,), (dg_one, db_one, db_qv) = scatter_sums(
        keep, send, ((width, 3 * width),), (width, width, 2 * width)
    )

    def assemble(top, own, back_rows):
        returned = from_behind(back_rows, "rows", 1)
        return jnp.stack([returned, top[0], own, top[1]], axis=1).reshape(tokens.shape)

    return (
        assemble(m_top, m_own, m_halo),
        assemble(g_top, g_own, g_halo),
        dg_one, db_one, dw_qkv, db_qv, dw_proj, db_proj, dg_two, db_two, dw_up, db_up, dw_down, db_down,
    )


def solution(mesh):
    both = ("dp", "rows")
    frame, vector, matrix = P("dp", "rows", None, None), P(both), P(both, None)
    return jax.shard_map(
        per_device,
        mesh=mesh,
        in_specs=(
            frame, P("dp"), vector, vector, matrix, vector, matrix, vector,
            vector, vector, matrix, vector, matrix, vector, frame,
        ),
        out_specs=(
            frame, frame, vector, vector, matrix, vector, matrix, vector,
            vector, vector, matrix, vector, matrix, vector,
        ),
        check_vma=False,
    )
```

```python
import functools

import jax
import jax.numpy as jnp
from jax import lax
from jax.experimental import pallas as pl
from jax.experimental.pallas import tpu as pltpu
from jax.sharding import PartitionSpec as P

HEAD_DIM = 64
WIN = 8
HALF = WIN // 2
CELLS = WIN * WIN
LANES = 4 * HEAD_DIM
LANE = 128
ROWS = 16
EPSILON = 1e-05
INV_ROOT_TWO = 0.7071067811865476
INV_ROOT_TWO_PI = 0.3989422804014327
F32 = jnp.float32
BF16 = jnp.bfloat16
VMEM_LIMIT = 60 * 1024 * 1024


def from_behind(x, axis, by):
    devices = lax.axis_size(axis)
    return lax.ppermute(x, axis, [(i, (i + by) % devices) for i in range(devices)])


def dot(a, b):
    return jnp.dot(a, b, preferred_element_type=F32)


def dot_t(a, b):
    return lax.dot_general(a, b, (((1,), (1,)), ((), ())), preferred_element_type=F32)


def to_window_order(x, columns):
    depth = x.shape[-1]
    grid = pltpu.roll(x.reshape(WIN, columns, depth), columns - HALF, 1)
    grid = grid.reshape(WIN, columns // WIN, WIN, depth).swapaxes(0, 1)
    return grid.reshape(WIN * columns, depth)


def from_window_order(x, columns):
    depth = x.shape[-1]
    grid = x.reshape(columns // WIN, WIN, WIN, depth).swapaxes(0, 1)
    grid = pltpu.roll(grid.reshape(WIN, columns, depth), HALF, 1)
    return grid.reshape(WIN * columns, depth)


def normalize(values):
    center = values - jnp.mean(values, axis=-1, keepdims=True)
    inverse = lax.rsqrt(jnp.mean(center * center, axis=-1, keepdims=True) + EPSILON)
    return center * inverse, inverse


def norm_back(grad, normed, inverse):
    return inverse * (
        grad
        - jnp.mean(grad, axis=-1, keepdims=True)
        - normed * jnp.mean(grad * normed, axis=-1, keepdims=True)
    )


def block_diag(x):
    lane_head = lax.broadcasted_iota(jnp.int32, x.shape, 1) // HEAD_DIM
    zero = jnp.zeros_like(x)
    return jnp.concatenate(
        [jnp.where(lane_head == head, x, zero) for head in range(LANES // HEAD_DIM)], axis=0
    )


def dot_down(a, b):
    pair = 2 * HEAD_DIM
    first = lax.broadcasted_iota(jnp.int32, (CELLS, pair), 1) < HEAD_DIM
    out = []
    for lane in range(0, LANES, pair):
        both = lax.dot_general(
            a[:, lane : lane + pair],
            b[:, lane : lane + pair],
            (((0,), (0,)), ((), ())),
            preferred_element_type=F32,
        )
        out.append(jnp.where(first, both[:HEAD_DIM], both[HEAD_DIM:]))
    return jnp.concatenate(out, axis=1)


def window_bias(info, frames, step, win, columns, height, rows_here):
    frame = lax.rem(step, frames)
    level = info[frame]
    factor = jnp.where(level >= 2, 4, jnp.where(level >= 1, 2, 1))
    base = info[frames] * rows_here + (step // frames) * WIN
    row_limit, col_limit = height * factor // 4, columns * factor // 4
    last_row = (base + WIN >= height).astype(jnp.int32)
    last_col = jnp.int32(win == columns // WIN - 1)
    key = lax.broadcasted_iota(jnp.int32, (CELLS, LANES), 0)
    query = lax.broadcasted_iota(jnp.int32, (CELLS, LANES), 1) % CELLS
    row = base + key // WIN + HALF
    col = win * WIN + key % WIN + HALF
    row = jnp.where(row >= height, row - height, row)
    col = jnp.where(col >= columns, col - columns, col)
    differ = key ^ query
    bad = (differ // (HALF * WIN) % 2) * last_row + (differ // HALF % 2) * last_col
    bad = bad + (row >= row_limit).astype(jnp.int32) + (col >= col_limit).astype(jnp.int32)
    return jnp.where(bad > 0, -100.0, 0.0)


def place(info, at, mine, theirs, targets, vec, sem, vec_sem):
    copies = []
    for core, source in enumerate((mine, theirs)):
        for j in range(source.shape[0]):
            block = info[at] ^ (bits_of(j) | core)
            for lane, lanes, rows, target in targets:
                for sub in range(rows // ROWS):
                    row = pl.multiple_of(block * rows + sub * ROWS, ROWS)
                    copies.append(
                        pltpu.make_async_copy(
                            source.at[j, :, pl.ds(lane + sub * lanes, lanes)],
                            target.at[pl.ds(row, ROWS), :],
                            sem,
                        )
                    )
        lanes = vec.shape[-1]
        blocks = source.shape[0]
        copies.append(
            pltpu.make_async_copy(
                source.at[:, :, pl.ds(source.shape[-1] - lanes, lanes)],
                vec.at[pl.ds(core * blocks, blocks)],
                vec_sem,
            )
        )
    for copy in copies:
        copy.start()


def wait_bytes(targets, sem):
    for target in targets:
        pltpu.make_async_copy(target, target, sem).wait()


def bits_of(j):
    return (j % 4) * 8 + (j // 8) * 4 + (j // 4 % 2) * 2


def natural_rows(vec):
    total = jnp.sum(vec[...].astype(F32), axis=0)
    return [total[r : r + 1, :] for r in range(total.shape[0])]


def hand_over(info, at, sources, tail, keep, send):
    for core, out in enumerate((keep, send)):
        for j in range(out.shape[0]):
            block = info[at] ^ (bits_of(j) | core)
            for lane, lanes, rows, source in sources:
                for sub in range(rows // ROWS):
                    row = pl.multiple_of(block * rows + sub * ROWS, ROWS)
                    start = lane + sub * lanes
                    out[j, :, start : start + lanes] = source[pl.ds(row, ROWS), :].astype(out.dtype)
            out[j, :, out.shape[-1] - tail.shape[-1] :] = tail.astype(out.dtype)


def store_rows(out, halo, held, sem, local, total, step, frames, value):
    slot = lax.rem(local, 2)
    half = value.shape[0] // 2

    def finish(slot):
        for part in range(2):
            rows = held.at[slot, pl.ds(part * half, half)]
            pltpu.make_async_copy(rows, rows, sem.at[slot, part]).wait()

    @pl.when(local >= 2)
    def _():
        finish(slot)

    held[slot] = value
    frame, window_row = lax.rem(step, frames), step // frames
    top, bottom = (held.at[slot, pl.ds(part * half, half)] for part in range(2))
    pltpu.make_async_copy(top, out.at[frame, 1 + 2 * window_row], sem.at[slot, 0]).start()

    @pl.when(step < frames)
    def _():
        pltpu.make_async_copy(bottom, out.at[frame, 2], sem.at[slot, 1]).start()

    if halo is not None:

        @pl.when(step >= frames)
        def _():
            pltpu.make_async_copy(bottom, halo.at[frame], sem.at[slot, 1]).start()

    @pl.when(local == total - 1)
    def _():
        finish(slot)
        if total > 1:
            finish(1 - slot)


def attend_kernel(
    frames, columns, height, rows_here, first,
    info, top, own, halo, mine, theirs, *rest,
):
    q_out, k_out, v_out, p_out, o_out, weight, vec, lines, sem = rest[-9:]
    step = pl.program_id(0) + first
    width = top.shape[-1]

    @pl.when(pl.program_id(0) == 0)
    def _():
        place(info, frames + 1, mine, theirs, [(0, 3 * width, ROWS, weight)], vec, sem.at[0], sem.at[1])
        wait_bytes([weight], sem.at[0])
        wait_bytes([vec], sem.at[1])
        pieces = natural_rows(vec)
        per = width // LANE
        for line in range(lines.shape[0]):
            lines[line : line + 1, :] = jnp.concatenate(pieces[line * per : (line + 1) * per], axis=1)

    gain, bias, bias_q, bias_v = (lines.at[i : i + 1] for i in range(4))
    bottom = jnp.where(step < frames, own[...], halo[...])
    x = jnp.concatenate([top[...], bottom], axis=0).astype(F32)
    normed, _ = normalize(to_window_order(x, columns))
    hidden = (normed * gain[...] + bias[...]).astype(BF16)
    q_out[...] = (dot(hidden, weight[:, :width]) + bias_q[...]).astype(BF16) * 0.125
    k_out[...] = dot(hidden, weight[:, width : 2 * width]).astype(BF16)
    v_out[...] = (dot(hidden, weight[:, 2 * width :]) + bias_v[...]).astype(BF16)

    wins, groups = range(columns // WIN), range(width // LANES)
    items = [(w, slice(w * CELLS, (w + 1) * CELLS), slice(g * LANES, (g + 1) * LANES)) for w in wins for g in groups]
    masks = [window_bias(info, frames, step, w, columns, height, rows_here) for w in wins]
    scores = [dot_t(k_out[r, l], block_diag(q_out[r, l])) for _, r, l in items]
    exponents = []
    for (w, _, _), score in zip(items, scores):
        score = score + masks[w]
        exponents.append(jnp.exp(score - jnp.max(score, axis=0, keepdims=True)))
    probs = [(e * (1.0 / jnp.sum(e, axis=0, keepdims=True))).astype(BF16) for e in exponents]
    outs = [dot_down(p, v_out[r, l]).astype(BF16) for p, (_, r, l) in zip(probs, items)]
    for (_, r, l), p, out in zip(items, probs, outs):
        p_out[r, l] = p
        o_out[r, l] = out


def middle_kernel(
    frames, columns, chunk,
    info, top, own, halo, dtop, down, dhalo, o_in, mine, theirs,
    m_out, m_halo, dx_out, do_out, keep, send,
    w_proj, w_up, w_down, vec, lines, b_up, dw_proj, dw_up, dw_down_t, dw_down, small, g_s, du_s, held,
    sem, out_sem,
):
    step = pl.program_id(0)
    width = top.shape[-1]
    hidden_width = w_up.shape[-1]
    b_proj, g_two, b_two, b_down = (lines.at[i : i + 1] for i in range(4))

    @pl.when(step == 0)
    def _():
        targets = [
            (0, width, ROWS, w_proj),
            (width, hidden_width, ROWS, w_up),
            (width + hidden_width, width, w_down.shape[0] // 32, w_down),
        ]
        place(info, frames + 1, mine, theirs, targets, vec, sem.at[0], sem.at[1])
        wait_bytes([w_proj, w_up, w_down], sem.at[0])
        wait_bytes([vec], sem.at[1])
        pieces = natural_rows(vec)
        per = width // pieces[0].shape[-1]
        for line in range(4):
            lines[line : line + 1, :] = jnp.concatenate(pieces[line * per : (line + 1) * per], axis=1)
        b_up[...] = jnp.concatenate(pieces[4 * per :], axis=1)
        dw_proj[...] = jnp.zeros_like(dw_proj)
        dw_up[...] = jnp.zeros_like(dw_up)
        dw_down_t[...] = jnp.zeros_like(dw_down_t)
        small[...] = jnp.zeros_like(small)

    bottom = jnp.where(step < frames, own[...], halo[...])
    dbottom = jnp.where(step < frames, down[...], dhalo[...])
    x = to_window_order(jnp.concatenate([top[...], bottom], axis=0).astype(F32), columns)
    dy = to_window_order(jnp.concatenate([dtop[...], dbottom], axis=0).astype(F32), columns)
    dy_low = dy.astype(BF16)
    x2 = x + dot(o_in[...], w_proj[...]) + b_proj[...]
    normed, inverse = normalize(x2)
    h2 = (normed * g_two[...] + b_two[...]).astype(BF16)
    h2_t = h2.T
    dy_t = dy_low.T
    total = x2 + b_down[...]
    dh2 = jnp.zeros_like(x2)
    parts = [slice(start, start + chunk) for start in range(0, hidden_width, chunk)]

    def enter(part):
        return dot(h2, w_up[:, part]) + b_up[:, part], dot_t(dy_low, w_down[part, :])

    ahead = enter(parts[0])
    for index, part in enumerate(parts + [None]):
        if part is not None:
            u, dg = ahead
            if index + 1 < len(parts):
                ahead = enter(parts[index + 1])
            phi = 0.5 * (1.0 + lax.erf(u * INV_ROOT_TWO))
            g_s[:, part] = (u * phi).astype(BF16)
            du = dg * (phi + u * jnp.exp(-0.5 * u * u) * INV_ROOT_TWO_PI)
            du_s[:, part] = du.astype(BF16)
            small[0:1, part] += jnp.sum(du, axis=0, keepdims=True)
        if index > 0:
            old = parts[index - 1]
            total += dot(g_s[:, old], w_down[old, :])
            dh2 += dot_t(du_s[:, old], w_up[:, old])
            dw_up[:, old] += dot(h2_t, du_s[:, old])
            dw_down_t[:, old] += dot(dy_t, g_s[:, old])
    mixed = from_window_order(total, columns).astype(BF16)
    store_rows(m_out, m_halo, held, out_sem, step, pl.num_programs(0), step, frames, mixed)
    small[1:2, :width] += jnp.sum(dy, axis=0, keepdims=True)
    small[2:3, :width] += jnp.sum(dh2 * normed, axis=0, keepdims=True)
    small[3:4, :width] += jnp.sum(dh2, axis=0, keepdims=True)
    dx2 = dy + norm_back(dh2 * g_two[...], normed, inverse)
    da = dx2.astype(BF16)
    small[4:5, :width] += jnp.sum(dx2, axis=0, keepdims=True)
    dx_out[...] = dx2
    dw_proj[...] += dot(o_in[...].T, da)
    do_out[...] = dot_t(da, w_proj[...]).astype(BF16)

    @pl.when(step == pl.num_programs(0) - 1)
    def _():
        for lane in range(0, hidden_width, LANE):
            dw_down[lane : lane + LANE, :] = dw_down_t[:, lane : lane + LANE].T
        order = (4, 2, 3, 1)
        flat = jnp.concatenate([small[r : r + 1, :width] for r in order] + [small[0:1, :]], axis=1)
        lines_of = keep.shape[-1] - width - 2 * hidden_width
        tail = jnp.concatenate(
            [flat[:, i * lines_of : (i + 1) * lines_of] for i in range(ROWS)], axis=0
        )
        sources = [
            (0, width, ROWS, dw_proj),
            (width, hidden_width, ROWS, dw_up),
            (width + hidden_width, width, dw_down.shape[0] // 32, dw_down),
        ]
        hand_over(info, frames + 1, sources, tail, keep, send)


def back_kernel(
    frames, columns, first, count, with_halo, starts, ends,
    info, top, own, halo, q_in, k_in, v_in, p_in, do_in, dx_in, mine, theirs, *rest,
):
    if not starts:
        dw_before, small_before, *rest = rest[1 + with_halo :]
    *outs, d_s, weight, vec, lines, held, sem, out_sem = rest
    g_out, g_halo, dw, small = (outs[0], outs[1] if with_halo else None, outs[-2], outs[-1])
    local = pl.program_id(0)
    step = lax.rem(local + first, 2 * frames)
    width = top.shape[-1]
    gain, bias = (lines.at[i : i + 1] for i in range(2))

    @pl.when(local == 0)
    def _():
        place(info, frames + 1, mine, theirs, [(0, 3 * width, ROWS, weight)], vec, sem.at[0], sem.at[1])
        if starts:
            dw[...] = jnp.zeros_like(dw)
            small[...] = jnp.zeros_like(small)
        else:
            copies = [
                pltpu.make_async_copy(dw_before, dw, sem.at[2]),
                pltpu.make_async_copy(small_before, small, sem.at[3]),
            ]
            for copy in copies:
                copy.start()
            for copy in copies:
                copy.wait()
        wait_bytes([weight], sem.at[0])
        wait_bytes([vec], sem.at[1])
        pieces = natural_rows(vec)
        per = width // LANE
        for line in range(lines.shape[0]):
            lines[line : line + 1, :] = jnp.concatenate(pieces[line * per : (line + 1) * per], axis=1)

    items = [
        (slice(w * CELLS, (w + 1) * CELLS), g * LANES)
        for w in range(columns // WIN)
        for g in range(width // LANES)
    ]
    items = [(r, at, slice(at, at + LANES)) for r, at in items]
    diags = [block_diag(do_in[r, l]) for r, _, l in items]
    dps = [dot_t(v_in[r, l], diag) for (r, _, l), diag in zip(items, diags)]
    dvs = [dot(p_in[r, l], diag).astype(BF16) for (r, _, l), diag in zip(items, diags)]
    dss = []
    for (r, _, l), dp in zip(items, dps):
        full = p_in[r, l].astype(F32)
        dss.append((full * (dp - jnp.sum(dp * full, axis=0, keepdims=True))).astype(BF16))
    dks = [dot(ds, block_diag(q_in[r, l])).astype(BF16) for (r, _, l), ds in zip(items, dss)]
    dqs = [(dot_down(ds, k_in[r, l]) * 0.125).astype(BF16) for (r, _, l), ds in zip(items, dss)]
    for (r, at, _), dq, dk, dv in zip(items, dqs, dks, dvs):
        for part, grad in enumerate((dq, dk, dv)):
            d_s[r, part * width + at : part * width + at + LANES] = grad
    bottom = jnp.where(step < frames, own[...], halo[...])
    x = jnp.concatenate([top[...], bottom], axis=0).astype(F32)
    normed, inverse = normalize(to_window_order(x, columns))
    hidden = (normed * gain[...] + bias[...]).astype(BF16)
    d = d_s[...]
    dw[...] += dot(hidden.T, d)
    small[0:1, :] += jnp.sum(d.astype(F32), axis=0, keepdims=True)
    dh = dot_t(d, weight[...])
    small[1:2, :width] += jnp.sum(dh * normed, axis=0, keepdims=True)
    small[2:3, :width] += jnp.sum(dh, axis=0, keepdims=True)
    grad = dx_in[...] + norm_back(dh * gain[...], normed, inverse)
    grad = from_window_order(grad, columns).astype(BF16)
    store_rows(g_out, g_halo, held, out_sem, local, count, step, frames, grad)

    if ends:
        keep, send = outs[1 + with_halo : 3 + with_halo]

        @pl.when(local == count - 1)
        def _():
            pieces = [small[1:2, :width], small[2:3, :width], small[0:1, :width], small[0:1, 2 * width :]]
            flat = jnp.concatenate(pieces, axis=1)
            tail = jnp.concatenate([flat[:, i * LANE : (i + 1) * LANE] for i in range(ROWS)], axis=0)
            hand_over(info, frames + 1, [(0, 3 * width, ROWS, dw)], tail, keep, send)


def join_kernel(*refs):
    out = refs[-1]
    rows = refs[0].shape[0]
    for index, ref in enumerate(refs[:-1]):
        out[index * rows : (index + 1) * rows] = ref[...]


def join(*parts):
    shape = (len(parts) * parts[0].shape[0],) + parts[0].shape[1:]
    vmem = pl.BlockSpec(memory_space=pltpu.VMEM)
    return pl.pallas_call(
        join_kernel,
        out_shape=jax.ShapeDtypeStruct(shape, parts[0].dtype),
        in_specs=[vmem] * len(parts),
        out_specs=vmem,
        compiler_params=pltpu.CompilerParams(vmem_limit_bytes=VMEM_LIMIT),
        name="join",
    )(*parts)


def pack_kernel(index_ref, *refs):
    vectors, (qkv, proj, up, down, a_out, b_out) = refs[:-6], refs[-6:]
    index = index_ref[0]
    wide = 2 * LANE

    def spread_rows(sections, lanes):
        row = lax.broadcasted_iota(jnp.int32, (ROWS, wide), 0)
        total = jnp.zeros((ROWS, wide), F32)
        for ref, base in sections:
            count = ref.shape[0]
            at = base + index * count
            own = ref[...].astype(F32)[None, :]
            own = jnp.concatenate([own, jnp.zeros((1, wide - count), F32)], axis=1)
            moved = pltpu.roll(own, lax.rem(at, lanes), 1)
            total = total + jnp.where(row == at // lanes, moved, 0.0)
        return total[:, :lanes].astype(BF16)

    width = proj.shape[1]
    full = qkv.shape[1]
    a_out[:, :full] = qkv[...]
    sections = [(vectors[i], i * width) for i in range(3)]
    a_out[:, full:] = spread_rows(sections, a_out.shape[1] - full)
    hidden = up.shape[1]
    b_out[:, :width] = proj[...]
    b_out[:, width : width + hidden] = up[...]
    for i in range(down.shape[0] // ROWS):
        at = width + hidden + i * width
        b_out[:, at : at + width] = down[i * ROWS : (i + 1) * ROWS]
    full = width + 2 * hidden
    sections = [(vectors[3 + i], i * width) for i in range(5)]
    b_out[:, full:] = spread_rows(sections, b_out.shape[1] - full)


def pack(index, vectors, qkv, proj, up, down):
    lanes_a = qkv.shape[1] + LANE
    lanes_b = proj.shape[1] + 2 * up.shape[1] + 2 * LANE
    vmem = pl.BlockSpec(memory_space=pltpu.VMEM)
    return pl.pallas_call(
        pack_kernel,
        out_shape=[
            jax.ShapeDtypeStruct((ROWS, lanes_a), BF16),
            jax.ShapeDtypeStruct((ROWS, lanes_b), BF16),
        ],
        in_specs=[pl.BlockSpec(memory_space=pltpu.SMEM)] + [vmem] * (len(vectors) + 4),
        out_specs=[vmem, vmem],
        name="pack",
    )(index, *vectors, qkv, proj, up, down)


def grid_specs(frames, cells, width, first=0):
    top = pl.BlockSpec(
        (None, None, cells, width),
        lambda s, *_: ((s + first) % frames, 1 + 2 * ((s + first) % (2 * frames) // frames), 0, 0),
    )
    own = pl.BlockSpec(
        (None, None, cells, width),
        lambda s, *_: (jnp.minimum((s + first) % (2 * frames), frames - 1), 2, 0, 0),
    )
    halo = pl.BlockSpec(
        (None, cells, width), lambda s, *_: (jnp.maximum((s + first) % (2 * frames) - frames, 0), 0, 0)
    )
    return [top, own, halo]


def whole_out(shape):
    zeros = (0,) * len(shape)
    return pl.BlockSpec(shape, lambda s, *_: zeros, pipeline_mode=pl.Buffered(1))


ANYWHERE = pl.BlockSpec(memory_space=pl.ANY)


def params():
    return pltpu.CompilerParams(vmem_limit_bytes=VMEM_LIMIT, dimension_semantics=("arbitrary",))


def attend(info, tokens4, halo, blocks, previous, first, height, columns):
    frames, groups, cells, width = tokens4.shape
    steps, block = 2 * frames, 2 * cells
    row = pl.BlockSpec((None, block, width), lambda s, *_: (s + first, 0, 0))
    shape = jax.ShapeDtypeStruct((steps, block, width), BF16)
    held = 6
    return pl.pallas_call(
        functools.partial(attend_kernel, frames, columns, height, groups * HALF, first),
        out_shape=[shape] * 5,
        grid_spec=pltpu.PrefetchScalarGridSpec(
            num_scalar_prefetch=1,
            grid=(frames,),
            in_specs=grid_specs(frames, cells, width, first) + [ANYWHERE] * (2 + len(previous)),
            out_specs=[row] * 5,
            scratch_shapes=[
                pltpu.VMEM((width, 3 * width), BF16),
                pltpu.VMEM((32, ROWS, LANE), BF16),
                pltpu.VMEM((4, width), F32),
                pltpu.SemaphoreType.DMA((2,)),
            ],
        ),
        input_output_aliases={held + i: i for i in range(len(previous))},
        compiler_params=params(),
        cost_estimate=pl.CostEstimate(flops=3 * 10**10, bytes_accessed=2 * 10**7, transcendentals=10**6),
        name="attend",
    )(info, tokens4, tokens4, halo, *blocks, *previous)


def middle(info, tokens4, halo, d4, dhalo, o, blocks, hidden_width, columns, chunk=256):
    frames, groups, cells, width = tokens4.shape
    steps, block = 2 * frames, 2 * cells
    row = pl.BlockSpec((None, block, width), lambda s, *_: (s, 0, 0))
    ins = grid_specs(frames, cells, width)
    mine = blocks[0].shape
    return pl.pallas_call(
        functools.partial(middle_kernel, frames, columns, chunk),
        out_shape=[
            jax.ShapeDtypeStruct(tokens4.shape, BF16),
            jax.ShapeDtypeStruct(halo.shape, BF16),
            jax.ShapeDtypeStruct((steps, block, width), F32),
            jax.ShapeDtypeStruct((steps, block, width), BF16),
            jax.ShapeDtypeStruct(mine, BF16),
            jax.ShapeDtypeStruct(mine, BF16),
        ],
        grid_spec=pltpu.PrefetchScalarGridSpec(
            num_scalar_prefetch=1,
            grid=(steps,),
            in_specs=ins + ins + [row, ANYWHERE, ANYWHERE],
            out_specs=[ANYWHERE, ANYWHERE, row, row, whole_out(mine), whole_out(mine)],
            scratch_shapes=[
                pltpu.VMEM((width, width), BF16),
                pltpu.VMEM((width, hidden_width), BF16),
                pltpu.VMEM((hidden_width, width), BF16),
                pltpu.VMEM((32, ROWS, 2 * LANE), BF16),
                pltpu.VMEM((4, width), F32),
                pltpu.VMEM((1, hidden_width), F32),
                pltpu.VMEM((width, width), F32),
                pltpu.VMEM((width, hidden_width), F32),
                pltpu.VMEM((width, hidden_width), F32),
                pltpu.VMEM((hidden_width, width), F32),
                pltpu.VMEM((8, hidden_width), F32),
                pltpu.VMEM((block, hidden_width), BF16),
                pltpu.VMEM((block, hidden_width), BF16),
                pltpu.VMEM((2, block, width), BF16),
                pltpu.SemaphoreType.DMA((2,)),
                pltpu.SemaphoreType.DMA((2, 2)),
            ],
        ),
        compiler_params=params(),
        cost_estimate=pl.CostEstimate(flops=9 * 10**10, bytes_accessed=4 * 10**7, transcendentals=10**7),
        name="middle",
    )(info, tokens4, tokens4, halo, d4, d4, dhalo, o, *blocks)


def back(info, tokens4, halo, q, k, v, p, do, dx, blocks, columns, before, first, count, ends):
    frames, groups, cells, width = tokens4.shape
    steps, block = 2 * frames, 2 * cells
    row = pl.BlockSpec((None, block, width), lambda s, *_: ((s + first) % steps, 0, 0))
    mine = blocks[0].shape
    dw, small = (width, 3 * width), (8, 3 * width)
    handed = [jax.ShapeDtypeStruct(mine, BF16)] * 2
    sums = [jax.ShapeDtypeStruct(dw, F32), jax.ShapeDtypeStruct(small, F32)]
    held = 12
    with_halo = first + count > frames
    g_shapes = [jax.ShapeDtypeStruct(tokens4.shape, BF16), jax.ShapeDtypeStruct(halo.shape, BF16)]
    g_shapes = g_shapes[: 1 + with_halo]
    if before:
        before = (before[0], *(before[1:2] if with_halo else ()), *before[-2:])
    return pl.pallas_call(
        functools.partial(
            back_kernel, frames, columns, first, count, with_halo, not before, ends
        ),
        out_shape=g_shapes + (handed if ends else sums),
        grid_spec=pltpu.PrefetchScalarGridSpec(
            num_scalar_prefetch=1,
            grid=(count,),
            in_specs=grid_specs(frames, cells, width, first)
            + [row] * 6
            + [ANYWHERE] * (2 + len(before)),
            out_specs=[ANYWHERE] * len(g_shapes)
            + ([whole_out(mine)] * 2 if ends else [whole_out(dw), whole_out(small)]),
            scratch_shapes=([pltpu.VMEM(dw, F32), pltpu.VMEM(small, F32)] if ends else [])
            + [
                pltpu.VMEM((block, 3 * width), BF16),
                pltpu.VMEM((width, 3 * width), BF16),
                pltpu.VMEM((32, ROWS, LANE), BF16),
                pltpu.VMEM((4, width), F32),
                pltpu.VMEM((2, block, width), BF16),
                pltpu.SemaphoreType.DMA((4,)),
                pltpu.SemaphoreType.DMA((2, 2)),
            ],
        ),
        input_output_aliases={held + i: i for i in range(len(g_shapes))} if before else {},
        compiler_params=params(),
        cost_estimate=pl.CostEstimate(
            flops=6 * 10**9 * count, bytes_accessed=5 * 10**6 * count, transcendentals=10**5
        ),
        name="back",
    )(info, tokens4, tokens4, halo, q, k, v, p, do, dx, *blocks, *before)


AXES = ("dp", "rows")


def flip_perm(axis, bits):
    return [(i, i ^ bits) for i in range(lax.axis_size(axis))]


def flipped(x, axis, bits):
    return lax.ppermute(x, axis, flip_perm(axis, bits))


def flipped_both(x, dp_bits, rows_bits):
    dp, rows = lax.axis_size("dp"), lax.axis_size("rows")
    pairs = [
        (d * rows + r, (d ^ dp_bits) * rows + (r ^ rows_bits)) for d in range(dp) for r in range(rows)
    ]
    return lax.ppermute(x, AXES, pairs)


def is_cube():
    return lax.axis_size("dp") == 8 and lax.axis_size("rows") == 4


def place_index():
    return lax.axis_index("dp") * lax.axis_size("rows") + lax.axis_index("rows")


def after(value, *others):
    return lax.optimization_barrier((value,) + others)[0]


def along_z(own):
    return [flipped(own, "dp", 2 * z) for z in (1, 2, 3)]


def over_plane(column):
    return [flipped(column, "rows", 2), flipped(column, "dp", 1), flipped_both(column, 1, 2)]


def gather_blocks(matrices, vectors):
    full = [lax.all_gather(m, AXES, axis=0, tiled=True) for m in matrices]
    lanes = []
    for m in full:
        per = m.shape[0] // 32
        blocks = m.reshape(32, per // ROWS, ROWS, m.shape[1]).transpose(0, 2, 1, 3)
        lanes.append(blocks.reshape(32, ROWS, -1))
    flat = jnp.concatenate([lax.all_gather(v, AXES, axis=0, tiled=True) for v in vectors])
    tail = flat.reshape(1, ROWS, -1)
    lanes.append(jnp.concatenate([tail, jnp.zeros((31,) + tail.shape[1:], tail.dtype)]))
    natural = jnp.concatenate(lanes, axis=2)
    relative = natural.reshape(4, 2, 2, 2, ROWS, -1).transpose(3, 1, 2, 0, 4, 5)
    relative = relative.reshape(2, 16, ROWS, -1)
    return relative[0], relative[1]


def own_rows(total, matrix_shapes, shards):
    matrices, lane = [], 0
    for rows, lanes in matrix_shapes:
        subs = rows // shards // ROWS
        pieces = [total[:, lane + i * lanes : lane + (i + 1) * lanes] for i in range(subs)]
        matrices.append(jnp.concatenate(pieces, axis=0))
        lane += subs * lanes
    return matrices, total[:, lane:].reshape(-1)


def wide(x):
    return x.astype(F32)


def sum_cores(keep, send):
    first = wide(keep) + wide(flipped(send, "rows", 1))
    return first[:4], first[4:].astype(BF16)


def sum_plane(kept, low):
    plane = (
        kept
        + wide(flipped(low[:4], "rows", 2))
        + wide(flipped(low[4:8], "dp", 1))
        + wide(flipped_both(low[8:], 1, 2))
    )
    return plane[0], plane[1:].astype(BF16)


def sum_line(kept, low):
    for z in (1, 2, 3):
        kept += wide(flipped(low[z - 1], "dp", 2 * z))
    return kept


def own_vectors(flat, vector_sizes):
    shards = lax.axis_size("dp") * lax.axis_size("rows")
    vectors, start = [], 0
    for size in vector_sizes:
        count = size // shards
        vectors.append(lax.dynamic_slice(flat, (start + place_index() * count,), (count,)))
        start += size
    return vectors


def scatter_sums(keep, send, matrix_shapes):
    matrices = []
    relative = jnp.stack([wide(keep), wide(send)]).reshape(2, 2, 2, 4, ROWS, -1)
    natural = relative.transpose(3, 1, 2, 0, 4, 5).reshape(32, ROWS, -1)
    lane = 0
    for rows, lanes in matrix_shapes:
        subs = rows // 32 // ROWS
        piece = natural[:, :, lane : lane + subs * lanes].reshape(32, ROWS, subs, lanes)
        whole_matrix = piece.transpose(0, 2, 1, 3).reshape(rows, lanes)
        matrices.append(lax.psum_scatter(whole_matrix, AXES, scatter_dimension=0, tiled=True))
        lane += subs * lanes
    flat = lax.psum(natural[0, :, lane:], AXES).reshape(-1)
    return matrices, flat


def per_device(
    tokens, frame_level, ln1_gain, ln1_bias, qkv_weight, qv_bias, proj_weight, proj_bias,
    ln2_gain, ln2_bias, fc1_weight, fc1_bias, fc2_weight, fc2_bias, d_out,
):
    frames, rows_here, columns, width = tokens.shape
    height = rows_here * lax.axis_size("rows")
    hidden_width = fc1_weight.shape[1]
    cells = HALF * columns
    grouped = (frames, rows_here // HALF, cells, width)
    tokens4, d4 = tokens.reshape(grouped), d_out.reshape(grouped)
    if is_cube():
        me = place_index().astype(jnp.int32)
        vectors = (
            ln1_gain, ln1_bias, qv_bias, proj_bias, ln2_gain, ln2_bias, fc2_bias, fc1_bias
        )
        own_a, own_b = pack(me[None], vectors, qkv_weight, proj_weight, fc1_weight, fc2_weight)
        z_a = along_z(own_a)
        own_b = after(own_b, *z_a)
        z_b = along_z(own_b)
        column_a = join(own_a[None], *(z[None] for z in z_a))
        halo = from_behind(after(tokens4[:, 0], column_a), "rows", -1)
        plane_a = over_plane(column_a)
        mine_a = join(column_a, *plane_a)
        attend_blocks = (mine_a, flipped(mine_a, "rows", 1))
        column_b = join(own_b[None], *(z[None] for z in z_b))
        column_b = after(column_b, mine_a)
        plane_b = over_plane(column_b)
        dhalo = from_behind(after(d4[:, 0], mine_a), "rows", -1)
    else:
        me = jnp.int32(0)
        attend_blocks = gather_blocks((qkv_weight,), (ln1_gain, ln1_bias, qv_bias))
        middle_blocks = gather_blocks(
            (proj_weight, fc1_weight, fc2_weight), (proj_bias, ln2_gain, ln2_bias, fc2_bias, fc1_bias)
        )
        halo = from_behind(tokens4[:, 0], "rows", -1)
        dhalo = from_behind(d4[:, 0], "rows", -1)
    info = jnp.concatenate([frame_level, jnp.stack([lax.axis_index("rows").astype(jnp.int32), me])])
    early = attend(info, tokens4, halo, attend_blocks, (), 0, height, columns)
    if is_cube():
        plane_b = lax.optimization_barrier((*plane_b, early[0]))[:3]
        mine_b = join(column_b, *plane_b)
        middle_blocks = (mine_b, flipped(mine_b, "rows", 1))
    q, k, v, p, o = attend(info, tokens4, halo, attend_blocks, early, frames, height, columns)
    m_out, m_halo, dx, do, keep, send = middle(
        info, tokens4, halo, d4, dhalo, o, middle_blocks, hidden_width, columns
    )
    m_back = from_behind(m_halo, "rows", 1)
    states = (info, tokens4, halo, q, k, v, p, do, dx, attend_blocks, columns)
    shapes_b = ((width, width), (width, hidden_width), (hidden_width, width))
    shapes_a = ((width, 3 * width),)
    if is_cube():
        shards = lax.axis_size("dp") * lax.axis_size("rows")
        cores_b = sum_cores(keep, send)
        before = back(*states, (), frames, 2, False)
        *before, cores_b, m_back = lax.optimization_barrier((*before, cores_b, m_back))
        plane_b = sum_plane(*cores_b)
        before = back(*states, before, frames + 2, frames, False)
        g_back = from_behind(before[1], "rows", 1)
        g_out, keep, send = back(*states, before, 2, frames - 2, True)
        plane_b, send = lax.optimization_barrier((plane_b, send))
        cores_a = sum_cores(keep, send)
        sums_b, flat_b = own_rows(sum_line(*plane_b), shapes_b, shards)
        cores_a, g_back = lax.optimization_barrier((cores_a, g_back))
        sums_a, flat_a = own_rows(sum_line(*sum_plane(*cores_a)), shapes_a, shards)
    else:
        sums_b, flat_b = scatter_sums(keep, send, shapes_b)
        before = back(*states, (), frames, frames, False)
        g_back = from_behind(before[1], "rows", 1)
        g_out, keep, send = back(*states, before, 0, frames, True)
        sums_a, flat_a = scatter_sums(keep, send, shapes_a)
    dw_proj, dw_up, dw_down = sums_b
    db_proj, dg_two, db_two, db_down, db_up = own_vectors(
        flat_b, (width, width, width, width, hidden_width)
    )
    (dw_qkv,) = sums_a
    dg_one, db_one, db_qv = own_vectors(flat_a, (width, width, 2 * width))
    return (
        m_out.at[:, 0].set(m_back).reshape(tokens.shape),
        g_out.at[:, 0].set(g_back).reshape(tokens.shape),
        dg_one, db_one, dw_qkv, db_qv, dw_proj, db_proj, dg_two, db_two, dw_up, db_up, dw_down, db_down,
    )


def solution(mesh):
    both = ("dp", "rows")
    frame, vector, matrix = P("dp", "rows", None, None), P(both), P(both, None)
    return jax.shard_map(
        per_device,
        mesh=mesh,
        in_specs=(
            frame, P("dp"), vector, vector, matrix, vector, matrix, vector,
            vector, vector, matrix, vector, matrix, vector, frame,
        ),
        out_specs=(
            frame, frame, vector, vector, matrix, vector, matrix, vector,
            vector, vector, matrix, vector, matrix, vector,
        ),
        check_vma=False,
    )
```

```python
import functools

import jax
import jax.numpy as jnp
from jax import lax
from jax.experimental import pallas as pl
from jax.experimental.pallas import tpu as pltpu
from jax.sharding import PartitionSpec as P

HEAD_DIM = 64
WIN = 8
HALF = WIN // 2
CELLS = WIN * WIN
LANES = 4 * HEAD_DIM
LANE = 128
ROWS = 16
EPSILON = 1e-05
INV_ROOT_TWO = 0.7071067811865476
INV_ROOT_TWO_PI = 0.3989422804014327
F32 = jnp.float32
BF16 = jnp.bfloat16
VMEM_LIMIT = 60 * 1024 * 1024


def from_behind(x, axis, by):
    devices = lax.axis_size(axis)
    return lax.ppermute(x, axis, [(i, (i + by) % devices) for i in range(devices)])


def dot(a, b):
    return jnp.dot(a, b, preferred_element_type=F32)


def dot_t(a, b):
    return lax.dot_general(a, b, (((1,), (1,)), ((), ())), preferred_element_type=F32)


def to_window_order(x, columns):
    depth = x.shape[-1]
    grid = pltpu.roll(x.reshape(WIN, columns, depth), columns - HALF, 1)
    grid = grid.reshape(WIN, columns // WIN, WIN, depth).swapaxes(0, 1)
    return grid.reshape(WIN * columns, depth)


def from_window_order(x, columns):
    depth = x.shape[-1]
    grid = x.reshape(columns // WIN, WIN, WIN, depth).swapaxes(0, 1)
    grid = pltpu.roll(grid.reshape(WIN, columns, depth), HALF, 1)
    return grid.reshape(WIN * columns, depth)


def normalize(values):
    center = values - jnp.mean(values, axis=-1, keepdims=True)
    inverse = lax.rsqrt(jnp.mean(center * center, axis=-1, keepdims=True) + EPSILON)
    return center * inverse, inverse


def norm_back(grad, normed, inverse):
    return inverse * (
        grad
        - jnp.mean(grad, axis=-1, keepdims=True)
        - normed * jnp.mean(grad * normed, axis=-1, keepdims=True)
    )


def block_diag(x):
    lane_head = lax.broadcasted_iota(jnp.int32, x.shape, 1) // HEAD_DIM
    zero = jnp.zeros_like(x)
    return jnp.concatenate(
        [jnp.where(lane_head == head, x, zero) for head in range(LANES // HEAD_DIM)], axis=0
    )


def dot_down(a, b):
    pair = 2 * HEAD_DIM
    first = lax.broadcasted_iota(jnp.int32, (CELLS, pair), 1) < HEAD_DIM
    out = []
    for lane in range(0, LANES, pair):
        both = lax.dot_general(
            a[:, lane : lane + pair],
            b[:, lane : lane + pair],
            (((0,), (0,)), ((), ())),
            preferred_element_type=F32,
        )
        out.append(jnp.where(first, both[:HEAD_DIM], both[HEAD_DIM:]))
    return jnp.concatenate(out, axis=1)


def window_bias(info, frames, step, win, columns, height, rows_here):
    frame = lax.rem(step, frames)
    level = info[frame]
    factor = jnp.where(level >= 2, 4, jnp.where(level >= 1, 2, 1))
    base = info[frames] * rows_here + (step // frames) * WIN
    row_limit, col_limit = height * factor // 4, columns * factor // 4
    last_row = (base + WIN >= height).astype(jnp.int32)
    last_col = jnp.int32(win == columns // WIN - 1)
    key = lax.broadcasted_iota(jnp.int32, (CELLS, LANES), 0)
    query = lax.broadcasted_iota(jnp.int32, (CELLS, LANES), 1) % CELLS
    row = base + key // WIN + HALF
    col = win * WIN + key % WIN + HALF
    row = jnp.where(row >= height, row - height, row)
    col = jnp.where(col >= columns, col - columns, col)
    differ = key ^ query
    bad = (differ // (HALF * WIN) % 2) * last_row + (differ // HALF % 2) * last_col
    bad = bad + (row >= row_limit).astype(jnp.int32) + (col >= col_limit).astype(jnp.int32)
    return jnp.where(bad > 0, -100.0, 0.0)


def place(info, at, pieces, targets, vec, vec_sem):
    blocks = [
        (source, k, core, i)
        for core, sources in enumerate(pieces)
        for i, (source, k) in enumerate((s, k) for s in sources for k in range(s.shape[0]))
    ]
    lanes = vec.shape[-1]
    start = 0
    for sources in pieces:
        for source in sources:
            count = source.shape[0]
            tail = source.at[:, :, pl.ds(source.shape[-1] - lanes, lanes)]
            pltpu.make_async_copy(tail, vec.at[pl.ds(start, count)], vec_sem).start()
            start += count
    for lane, lanes, rows, target, sem in targets:
        for source, k, core, i in blocks:
            block = info[at] ^ (bits_of(i) | core)
            for sub in range(rows // ROWS):
                row = pl.multiple_of(block * rows + sub * ROWS, ROWS)
                pltpu.make_async_copy(
                    source.at[k, :, pl.ds(lane + sub * lanes, lanes)], target.at[pl.ds(row, ROWS), :], sem
                ).start()


def halves(pieces):
    return pieces[: len(pieces) // 2], pieces[len(pieces) // 2 :]


def wait_bytes(target, sem):
    pltpu.make_async_copy(target, target, sem).wait()


def bits_of(j):
    return (j % 4) * 8 + (j // 8) * 4 + (j // 4 % 2) * 2


def natural_rows(vec):
    total = jnp.sum(vec[...].astype(F32), axis=0)
    return [total[r : r + 1, :] for r in range(total.shape[0])]


def hand_over(info, at, sources, tail, keep, send):
    for core, out in enumerate((keep, send)):
        for j in range(out.shape[0]):
            block = info[at] ^ (bits_of(j) | core)
            for lane, lanes, rows, source in sources:
                for sub in range(rows // ROWS):
                    row = pl.multiple_of(block * rows + sub * ROWS, ROWS)
                    start = lane + sub * lanes
                    out[j, :, start : start + lanes] = source[pl.ds(row, ROWS), :].astype(out.dtype)
            out[j, :, out.shape[-1] - tail.shape[-1] :] = tail.astype(out.dtype)


def store_rows(out, halo, held, sem, local, total, step, frames, value):
    slot = lax.rem(local, 2)
    half = value.shape[0] // 2

    def finish(slot):
        for part in range(2):
            rows = held.at[slot, pl.ds(part * half, half)]
            pltpu.make_async_copy(rows, rows, sem.at[slot, part]).wait()

    @pl.when(local >= 2)
    def _():
        finish(slot)

    held[slot] = value
    frame, window_row = lax.rem(step, frames), step // frames
    top, bottom = (held.at[slot, pl.ds(part * half, half)] for part in range(2))
    pltpu.make_async_copy(top, out.at[frame, 1 + 2 * window_row], sem.at[slot, 0]).start()

    @pl.when(step < frames)
    def _():
        pltpu.make_async_copy(bottom, out.at[frame, 2], sem.at[slot, 1]).start()

    if halo is not None:

        @pl.when(step >= frames)
        def _():
            pltpu.make_async_copy(bottom, halo.at[frame], sem.at[slot, 1]).start()

    @pl.when(local == total - 1)
    def _():
        finish(slot)
        if total > 1:
            finish(1 - slot)


def attend_kernel(
    frames, columns, height, rows_here,
    info, top, own, halo, *rest,
):
    q_out, k_out, v_out, p_out, o_out, weight, vec, lines, sem = rest[-9:]
    step = pl.program_id(0)
    width = top.shape[-1]

    @pl.when(step == 0)
    def _():
        place(
            info, frames + 1, halves(rest[:-9]), [(0, 3 * width, ROWS, weight, sem.at[0])], vec, sem.at[1]
        )
        wait_bytes(weight, sem.at[0])
        wait_bytes(vec, sem.at[1])
        pieces = natural_rows(vec)
        per = width // LANE
        for line in range(lines.shape[0]):
            lines[line : line + 1, :] = jnp.concatenate(pieces[line * per : (line + 1) * per], axis=1)

    gain, bias, bias_q, bias_v = (lines.at[i : i + 1] for i in range(4))
    bottom = jnp.where(step < frames, own[...], halo[...])
    x = jnp.concatenate([top[...], bottom], axis=0).astype(F32)
    normed, _ = normalize(to_window_order(x, columns))
    hidden = (normed * gain[...] + bias[...]).astype(BF16)
    q_out[...] = (dot(hidden, weight[:, :width]) + bias_q[...]).astype(BF16) * 0.125
    k_out[...] = dot(hidden, weight[:, width : 2 * width]).astype(BF16)
    v_out[...] = (dot(hidden, weight[:, 2 * width :]) + bias_v[...]).astype(BF16)

    wins, groups = range(columns // WIN), range(width // LANES)
    items = [(w, slice(w * CELLS, (w + 1) * CELLS), slice(g * LANES, (g + 1) * LANES)) for w in wins for g in groups]
    masks = [window_bias(info, frames, step, w, columns, height, rows_here) for w in wins]
    scores = [dot_t(k_out[r, l], block_diag(q_out[r, l])) for _, r, l in items]
    exponents = []
    for (w, _, _), score in zip(items, scores):
        score = score + masks[w]
        exponents.append(jnp.exp(score - jnp.max(score, axis=0, keepdims=True)))
    probs = [(e * (1.0 / jnp.sum(e, axis=0, keepdims=True))).astype(BF16) for e in exponents]
    outs = [dot_down(p, v_out[r, l]).astype(BF16) for p, (_, r, l) in zip(probs, items)]
    for (_, r, l), p, out in zip(items, probs, outs):
        p_out[r, l] = p
        o_out[r, l] = out


def middle_kernel(
    frames, columns, chunk,
    info, top, own, halo, dtop, down, dhalo, o_in, *rest,
):
    (
        m_out, m_halo, dx_out, do_out, keep, send,
        w_proj, w_up, w_down, vec, lines, b_up, dw_proj, dw_up, dw_down_t, dw_down, small, g_s, du_s, held,
        sem, out_sem,
    ) = rest[-22:]
    step = pl.program_id(0)
    width = top.shape[-1]
    hidden_width = w_up.shape[-1]
    b_proj, g_two, b_two, b_down = (lines.at[i : i + 1] for i in range(4))

    @pl.when(step == 0)
    def _():
        targets = [
            (0, width, ROWS, w_proj, sem.at[0]),
            (width, hidden_width, ROWS, w_up, sem.at[1]),
            (width + hidden_width, width, w_down.shape[0] // 32, w_down, sem.at[2]),
        ]
        place(info, frames + 1, halves(rest[:-22]), targets, vec, sem.at[3])
        wait_bytes(vec, sem.at[3])
        pieces = natural_rows(vec)
        per = width // pieces[0].shape[-1]
        for line in range(4):
            lines[line : line + 1, :] = jnp.concatenate(pieces[line * per : (line + 1) * per], axis=1)
        b_up[...] = jnp.concatenate(pieces[4 * per :], axis=1)
        for target, copied in ((w_proj, sem.at[0]), (w_up, sem.at[1]), (w_down, sem.at[2])):
            wait_bytes(target, copied)
        dw_proj[...] = jnp.zeros_like(dw_proj)
        dw_up[...] = jnp.zeros_like(dw_up)
        dw_down_t[...] = jnp.zeros_like(dw_down_t)
        small[...] = jnp.zeros_like(small)

    bottom = jnp.where(step < frames, own[...], halo[...])
    dbottom = jnp.where(step < frames, down[...], dhalo[...])
    x = to_window_order(jnp.concatenate([top[...], bottom], axis=0).astype(F32), columns)
    dy = to_window_order(jnp.concatenate([dtop[...], dbottom], axis=0).astype(F32), columns)
    dy_low = dy.astype(BF16)
    x2 = x + dot(o_in[...], w_proj[...]) + b_proj[...]
    normed, inverse = normalize(x2)
    h2 = (normed * g_two[...] + b_two[...]).astype(BF16)
    h2_t = h2.T
    dy_t = dy_low.T
    total = x2 + b_down[...]
    dh2 = jnp.zeros_like(x2)
    parts = [slice(start, start + chunk) for start in range(0, hidden_width, chunk)]

    def enter(part):
        return dot(h2, w_up[:, part]) + b_up[:, part], dot_t(dy_low, w_down[part, :])

    ahead = enter(parts[0])
    for index, part in enumerate(parts + [None]):
        if part is not None:
            u, dg = ahead
            if index + 1 < len(parts):
                ahead = enter(parts[index + 1])
            phi = 0.5 * (1.0 + lax.erf(u * INV_ROOT_TWO))
            g_s[:, part] = (u * phi).astype(BF16)
            du = dg * (phi + u * jnp.exp(-0.5 * u * u) * INV_ROOT_TWO_PI)
            du_s[:, part] = du.astype(BF16)
            small[0:1, part] += jnp.sum(du, axis=0, keepdims=True)
        if index > 0:
            old = parts[index - 1]
            total += dot(g_s[:, old], w_down[old, :])
            dh2 += dot_t(du_s[:, old], w_up[:, old])
            dw_up[:, old] += dot(h2_t, du_s[:, old])
            dw_down_t[:, old] += dot(dy_t, g_s[:, old])
    mixed = from_window_order(total, columns).astype(BF16)
    store_rows(m_out, m_halo, held, out_sem, step, pl.num_programs(0), step, frames, mixed)
    small[1:2, :width] += jnp.sum(dy, axis=0, keepdims=True)
    small[2:3, :width] += jnp.sum(dh2 * normed, axis=0, keepdims=True)
    small[3:4, :width] += jnp.sum(dh2, axis=0, keepdims=True)
    dx2 = dy + norm_back(dh2 * g_two[...], normed, inverse)
    da = dx2.astype(BF16)
    small[4:5, :width] += jnp.sum(dx2, axis=0, keepdims=True)
    dx_out[...] = dx2
    dw_proj[...] += dot(o_in[...].T, da)
    do_out[...] = dot_t(da, w_proj[...]).astype(BF16)

    @pl.when(step == pl.num_programs(0) - 1)
    def _():
        for lane in range(0, hidden_width, LANE):
            dw_down[lane : lane + LANE, :] = dw_down_t[:, lane : lane + LANE].T
        order = (4, 2, 3, 1)
        flat = jnp.concatenate([small[r : r + 1, :width] for r in order] + [small[0:1, :]], axis=1)
        lines_of = keep.shape[-1] - width - 2 * hidden_width
        tail = jnp.concatenate(
            [flat[:, i * lines_of : (i + 1) * lines_of] for i in range(ROWS)], axis=0
        )
        sources = [
            (0, width, ROWS, dw_proj),
            (width, hidden_width, ROWS, dw_up),
            (width + hidden_width, width, dw_down.shape[0] // 32, dw_down),
        ]
        hand_over(info, frames + 1, sources, tail, keep, send)


def back_kernel(
    frames, columns, first, count, with_halo, n_blocks, n_before, ends,
    info, top, own, halo, q_in, k_in, v_in, p_in, do_in, dx_in, *rest,
):
    blocks, rest = rest[:n_blocks], rest[n_blocks:]
    earlier = rest[1 + with_halo : n_before] if n_before else ()
    *outs, d_s, weight, vec, lines, held, sem, out_sem = rest[n_before:]
    g_out, g_halo = outs[0], outs[1] if with_halo else None
    if ends:
        keep, send, dw, small, *loaded = outs[1 + with_halo :]
    else:
        dw, small = outs[1 + with_halo :]
    local = pl.program_id(0)
    step = lax.rem(local + first, 2 * frames)
    width = top.shape[-1]
    gain, bias = (lines.at[i : i + 1] for i in range(2))

    @pl.when(local == 0)
    def _():
        place(
            info, frames + 1, halves(blocks), [(0, 3 * width, ROWS, weight, sem.at[0])], vec, sem.at[1]
        )
        dw[...] = jnp.zeros_like(dw)
        small[...] = jnp.zeros_like(small)
        if ends:
            for i, (source, target) in enumerate(zip(earlier, loaded)):
                pltpu.make_async_copy(source, target, sem.at[2 + i]).start()

    items = [
        (slice(w * CELLS, (w + 1) * CELLS), g * LANES)
        for w in range(columns // WIN)
        for g in range(width // LANES)
    ]
    items = [(r, at, slice(at, at + LANES)) for r, at in items]
    diags = [block_diag(do_in[r, l]) for r, _, l in items]
    dps = [dot_t(v_in[r, l], diag) for (r, _, l), diag in zip(items, diags)]
    dvs = [dot(p_in[r, l], diag).astype(BF16) for (r, _, l), diag in zip(items, diags)]
    dss = []
    for (r, _, l), dp in zip(items, dps):
        full = p_in[r, l].astype(F32)
        dss.append((full * (dp - jnp.sum(dp * full, axis=0, keepdims=True))).astype(BF16))
    dks = [dot(ds, block_diag(q_in[r, l])).astype(BF16) for (r, _, l), ds in zip(items, dss)]
    dqs = [(dot_down(ds, k_in[r, l]) * 0.125).astype(BF16) for (r, _, l), ds in zip(items, dss)]
    for (r, at, _), dq, dk, dv in zip(items, dqs, dks, dvs):
        for part, grad in enumerate((dq, dk, dv)):
            d_s[r, part * width + at : part * width + at + LANES] = grad

    @pl.when(local == 0)
    def _():
        wait_bytes(weight, sem.at[0])
        wait_bytes(vec, sem.at[1])
        pieces = natural_rows(vec)
        per = width // LANE
        for line in range(lines.shape[0]):
            lines[line : line + 1, :] = jnp.concatenate(pieces[line * per : (line + 1) * per], axis=1)

    bottom = jnp.where(step < frames, own[...], halo[...])
    x = jnp.concatenate([top[...], bottom], axis=0).astype(F32)
    normed, inverse = normalize(to_window_order(x, columns))
    hidden = (normed * gain[...] + bias[...]).astype(BF16)
    d = d_s[...]
    dw[...] += dot(hidden.T, d)
    small[0:1, :] += jnp.sum(d.astype(F32), axis=0, keepdims=True)
    dh = dot_t(d, weight[...])
    small[1:2, :width] += jnp.sum(dh * normed, axis=0, keepdims=True)
    small[2:3, :width] += jnp.sum(dh, axis=0, keepdims=True)
    grad = dx_in[...] + norm_back(dh * gain[...], normed, inverse)
    grad = from_window_order(grad, columns).astype(BF16)
    store_rows(g_out, g_halo, held, out_sem, local, count, step, frames, grad)

    if ends:

        @pl.when(local == count - 1)
        def _():
            for i, target in enumerate(loaded):
                wait_bytes(target, sem.at[2 + i])
                total = dw if i % 2 == 0 else small
                total[...] += target[...]
            pieces = [small[1:2, :width], small[2:3, :width], small[0:1, :width], small[0:1, 2 * width :]]
            flat = jnp.concatenate(pieces, axis=1)
            tail = jnp.concatenate([flat[:, i * LANE : (i + 1) * LANE] for i in range(ROWS)], axis=0)
            hand_over(info, frames + 1, [(0, 3 * width, ROWS, dw)], tail, keep, send)


def join_kernel(*refs):
    out = refs[-1]
    rows = refs[0].shape[0]
    for index, ref in enumerate(refs[:-1]):
        out[index * rows : (index + 1) * rows] = ref[...]


def join(*parts):
    shape = (len(parts) * parts[0].shape[0],) + parts[0].shape[1:]
    vmem = pl.BlockSpec(memory_space=pltpu.VMEM)
    return pl.pallas_call(
        join_kernel,
        out_shape=jax.ShapeDtypeStruct(shape, parts[0].dtype),
        in_specs=[vmem] * len(parts),
        out_specs=vmem,
        compiler_params=pltpu.CompilerParams(vmem_limit_bytes=VMEM_LIMIT),
        name="join",
    )(*parts)


def pack_kernel(index_ref, *refs):
    vectors, (qkv, proj, up, down, a_out, b_out) = refs[:-6], refs[-6:]
    index = index_ref[0]
    wide = 2 * LANE

    def spread_rows(sections, lanes):
        row = lax.broadcasted_iota(jnp.int32, (ROWS, wide), 0)
        total = jnp.zeros((ROWS, wide), F32)
        for ref, base in sections:
            count = ref.shape[0]
            at = base + index * count
            own = ref[...].astype(F32)[None, :]
            own = jnp.concatenate([own, jnp.zeros((1, wide - count), F32)], axis=1)
            moved = pltpu.roll(own, lax.rem(at, lanes), 1)
            total = total + jnp.where(row == at // lanes, moved, 0.0)
        return total[:, :lanes].astype(BF16)

    width = proj.shape[1]
    full = qkv.shape[1]
    a_out[:, :full] = qkv[...]
    sections = [(vectors[i], i * width) for i in range(3)]
    a_out[:, full:] = spread_rows(sections, a_out.shape[1] - full)
    hidden = up.shape[1]
    b_out[:, :width] = proj[...]
    b_out[:, width : width + hidden] = up[...]
    for i in range(down.shape[0] // ROWS):
        at = width + hidden + i * width
        b_out[:, at : at + width] = down[i * ROWS : (i + 1) * ROWS]
    full = width + 2 * hidden
    sections = [(vectors[3 + i], i * width) for i in range(5)]
    b_out[:, full:] = spread_rows(sections, b_out.shape[1] - full)


def pack(index, vectors, qkv, proj, up, down):
    lanes_a = qkv.shape[1] + LANE
    lanes_b = proj.shape[1] + 2 * up.shape[1] + 2 * LANE
    vmem = pl.BlockSpec(memory_space=pltpu.VMEM)
    return pl.pallas_call(
        pack_kernel,
        out_shape=[
            jax.ShapeDtypeStruct((ROWS, lanes_a), BF16),
            jax.ShapeDtypeStruct((ROWS, lanes_b), BF16),
        ],
        in_specs=[pl.BlockSpec(memory_space=pltpu.SMEM)] + [vmem] * (len(vectors) + 4),
        out_specs=[vmem, vmem],
        name="pack",
    )(index, *vectors, qkv, proj, up, down)


def grid_specs(frames, cells, width, first=0, which=0):
    top = pl.BlockSpec(
        (None, None, cells, width),
        lambda s, *_: ((s + first) % frames, 1 + 2 * ((s + first) % (2 * frames) // frames), 0, 0),
    )
    own = pl.BlockSpec(
        (None, None, cells, width),
        lambda s, *_: (jnp.minimum((s + first) % (2 * frames), frames - 1), 2, 0, 0),
    )
    halo = pl.BlockSpec(
        (None, None, cells, width),
        lambda s, *_: (which, jnp.maximum((s + first) % (2 * frames) - frames, 0), 0, 0),
    )
    return [top, own, halo]


def whole_out(shape):
    zeros = (0,) * len(shape)
    return pl.BlockSpec(shape, lambda s, *_: zeros, pipeline_mode=pl.Buffered(1))


ANYWHERE = pl.BlockSpec(memory_space=pl.ANY)


def params():
    return pltpu.CompilerParams(vmem_limit_bytes=VMEM_LIMIT, dimension_semantics=("arbitrary",))


def attend(info, tokens4, halo, blocks, height, columns):
    frames, groups, cells, width = tokens4.shape
    steps, block = 2 * frames, 2 * cells
    row = pl.BlockSpec((None, block, width), lambda s, *_: (s, 0, 0))
    shape = jax.ShapeDtypeStruct((steps, block, width), BF16)
    return pl.pallas_call(
        functools.partial(attend_kernel, frames, columns, height, groups * HALF),
        out_shape=[shape] * 5,
        grid_spec=pltpu.PrefetchScalarGridSpec(
            num_scalar_prefetch=1,
            grid=(steps,),
            in_specs=grid_specs(frames, cells, width) + [ANYWHERE] * len(blocks),
            out_specs=[row] * 5,
            scratch_shapes=[
                pltpu.VMEM((width, 3 * width), BF16),
                pltpu.VMEM((32, ROWS, LANE), BF16),
                pltpu.VMEM((4, width), F32),
                pltpu.SemaphoreType.DMA((2,)),
            ],
        ),
        compiler_params=params(),
        cost_estimate=pl.CostEstimate(flops=3 * 10**10, bytes_accessed=3 * 10**7, transcendentals=10**6),
        name="attend",
    )(info, tokens4, tokens4, halo, *blocks)


def middle(info, tokens4, halo, d4, o, blocks, hidden_width, columns, chunk=256):
    frames, groups, cells, width = tokens4.shape
    steps, block = 2 * frames, 2 * cells
    row = pl.BlockSpec((None, block, width), lambda s, *_: (s, 0, 0))
    ins = grid_specs(frames, cells, width) + grid_specs(frames, cells, width, which=1)
    mine = (16,) + blocks[0].shape[1:]
    return pl.pallas_call(
        functools.partial(middle_kernel, frames, columns, chunk),
        out_shape=[
            jax.ShapeDtypeStruct(tokens4.shape, BF16),
            jax.ShapeDtypeStruct(halo.shape[1:], BF16),
            jax.ShapeDtypeStruct((steps, block, width), F32),
            jax.ShapeDtypeStruct((steps, block, width), BF16),
            jax.ShapeDtypeStruct(mine, BF16),
            jax.ShapeDtypeStruct(mine, BF16),
        ],
        grid_spec=pltpu.PrefetchScalarGridSpec(
            num_scalar_prefetch=1,
            grid=(steps,),
            in_specs=ins + [row] + [ANYWHERE] * len(blocks),
            out_specs=[ANYWHERE, ANYWHERE, row, row, whole_out(mine), whole_out(mine)],
            scratch_shapes=[
                pltpu.VMEM((width, width), BF16),
                pltpu.VMEM((width, hidden_width), BF16),
                pltpu.VMEM((hidden_width, width), BF16),
                pltpu.VMEM((32, ROWS, 2 * LANE), BF16),
                pltpu.VMEM((4, width), F32),
                pltpu.VMEM((1, hidden_width), F32),
                pltpu.VMEM((width, width), F32),
                pltpu.VMEM((width, hidden_width), F32),
                pltpu.VMEM((width, hidden_width), F32),
                pltpu.VMEM((hidden_width, width), F32),
                pltpu.VMEM((8, hidden_width), F32),
                pltpu.VMEM((block, hidden_width), BF16),
                pltpu.VMEM((block, hidden_width), BF16),
                pltpu.VMEM((2, block, width), BF16),
                pltpu.SemaphoreType.DMA((4,)),
                pltpu.SemaphoreType.DMA((2, 2)),
            ],
        ),
        compiler_params=params(),
        cost_estimate=pl.CostEstimate(flops=9 * 10**10, bytes_accessed=4 * 10**7, transcendentals=10**7),
        name="middle",
    )(info, tokens4, tokens4, halo, d4, d4, halo, o, *blocks)


def back(info, tokens4, halo, q, k, v, p, do, dx, blocks, columns, before, first, count, ends):
    frames, groups, cells, width = tokens4.shape
    steps, block = 2 * frames, 2 * cells
    row = pl.BlockSpec((None, block, width), lambda s, *_: ((s + first) % steps, 0, 0))
    mine = (16,) + blocks[0].shape[1:]
    dw, small = (width, 3 * width), (8, 3 * width)
    handed = [jax.ShapeDtypeStruct(mine, BF16)] * 2
    sums = [jax.ShapeDtypeStruct(dw, F32), jax.ShapeDtypeStruct(small, F32)]
    in_vmem = [pltpu.VMEM(dw, F32), pltpu.VMEM(small, F32)]
    held = 10 + len(blocks)
    with_halo = first + count > frames
    g_shapes = [jax.ShapeDtypeStruct(tokens4.shape, BF16), jax.ShapeDtypeStruct(halo.shape[1:], BF16)]
    g_shapes = g_shapes[: 1 + with_halo]
    return pl.pallas_call(
        functools.partial(
            back_kernel, frames, columns, first, count, with_halo, len(blocks), len(before), ends
        ),
        out_shape=g_shapes + (handed if ends else sums),
        grid_spec=pltpu.PrefetchScalarGridSpec(
            num_scalar_prefetch=1,
            grid=(count,),
            in_specs=grid_specs(frames, cells, width, first)
            + [row] * 6
            + [ANYWHERE] * (len(blocks) + len(before)),
            out_specs=[ANYWHERE] * len(g_shapes)
            + ([whole_out(mine)] * 2 if ends else [whole_out(dw), whole_out(small)]),
            scratch_shapes=(in_vmem * ((len(before) - len(g_shapes)) // 2 + 1) if ends else [])
            + [
                pltpu.VMEM((block, 3 * width), BF16),
                pltpu.VMEM((width, 3 * width), BF16),
                pltpu.VMEM((32, ROWS, LANE), BF16),
                pltpu.VMEM((4, width), F32),
                pltpu.VMEM((2, block, width), BF16),
                pltpu.SemaphoreType.DMA((8,)),
                pltpu.SemaphoreType.DMA((2, 2)),
            ],
        ),
        input_output_aliases={held + i: i for i in range(len(g_shapes))} if before else {},
        compiler_params=params(),
        cost_estimate=pl.CostEstimate(
            flops=6 * 10**9 * count, bytes_accessed=5 * 10**6 * count, transcendentals=10**5
        ),
        name="back",
    )(info, tokens4, tokens4, halo, q, k, v, p, do, dx, *blocks, *before)


AXES = ("dp", "rows")


def flip_perm(axis, bits):
    return [(i, i ^ bits) for i in range(lax.axis_size(axis))]


def flipped(x, axis, bits):
    return lax.ppermute(x, axis, flip_perm(axis, bits))


def flipped_both(x, dp_bits, rows_bits):
    dp, rows = lax.axis_size("dp"), lax.axis_size("rows")
    pairs = [
        (d * rows + r, (d ^ dp_bits) * rows + (r ^ rows_bits)) for d in range(dp) for r in range(rows)
    ]
    return lax.ppermute(x, AXES, pairs)


def is_cube():
    return lax.axis_size("dp") == 8 and lax.axis_size("rows") == 4


def place_index():
    return lax.axis_index("dp") * lax.axis_size("rows") + lax.axis_index("rows")


def after(value, *others):
    return lax.optimization_barrier((value,) + others)[0]


def along_z(own):
    return [flipped(own, "dp", 2 * z) for z in (1, 2, 3)]


def over_plane(column):
    return [flipped(column, "rows", 2), flipped(column, "dp", 1), flipped_both(column, 1, 2)]


def gather_blocks(matrices, vectors):
    full = [lax.all_gather(m, AXES, axis=0, tiled=True) for m in matrices]
    lanes = []
    for m in full:
        per = m.shape[0] // 32
        blocks = m.reshape(32, per // ROWS, ROWS, m.shape[1]).transpose(0, 2, 1, 3)
        lanes.append(blocks.reshape(32, ROWS, -1))
    flat = jnp.concatenate([lax.all_gather(v, AXES, axis=0, tiled=True) for v in vectors])
    tail = flat.reshape(1, ROWS, -1)
    lanes.append(jnp.concatenate([tail, jnp.zeros((31,) + tail.shape[1:], tail.dtype)]))
    natural = jnp.concatenate(lanes, axis=2)
    relative = natural.reshape(4, 2, 2, 2, ROWS, -1).transpose(3, 1, 2, 0, 4, 5)
    relative = relative.reshape(2, 16, ROWS, -1)
    return relative[0], relative[1]


def own_rows(total, matrix_shapes, shards):
    matrices, lane = [], 0
    for rows, lanes in matrix_shapes:
        subs = rows // shards // ROWS
        pieces = [total[:, lane + i * lanes : lane + (i + 1) * lanes] for i in range(subs)]
        matrices.append(jnp.concatenate(pieces, axis=0))
        lane += subs * lanes
    return matrices, total[:, lane:].reshape(-1)


def wide(x):
    return x.astype(F32)


def sum_cores(keep, send):
    first = wide(keep) + wide(flipped(send, "rows", 1))
    return first[:4], first[4:].astype(BF16)


def sum_plane(kept, low):
    plane = (
        kept
        + wide(flipped(low[:4], "rows", 2))
        + wide(flipped(low[4:8], "dp", 1))
        + wide(flipped_both(low[8:], 1, 2))
    )
    return plane[0], plane[1:].astype(BF16)


def sum_line(kept, low):
    for z in (1, 2, 3):
        kept += wide(flipped(low[z - 1], "dp", 2 * z))
    return kept


def own_vectors(flat, vector_sizes):
    shards = lax.axis_size("dp") * lax.axis_size("rows")
    vectors, start = [], 0
    for size in vector_sizes:
        count = size // shards
        vectors.append(lax.dynamic_slice(flat, (start + place_index() * count,), (count,)))
        start += size
    return vectors


def scatter_sums(keep, send, matrix_shapes):
    matrices = []
    relative = jnp.stack([wide(keep), wide(send)]).reshape(2, 2, 2, 4, ROWS, -1)
    natural = relative.transpose(3, 1, 2, 0, 4, 5).reshape(32, ROWS, -1)
    lane = 0
    for rows, lanes in matrix_shapes:
        subs = rows // 32 // ROWS
        piece = natural[:, :, lane : lane + subs * lanes].reshape(32, ROWS, subs, lanes)
        whole_matrix = piece.transpose(0, 2, 1, 3).reshape(rows, lanes)
        matrices.append(lax.psum_scatter(whole_matrix, AXES, scatter_dimension=0, tiled=True))
        lane += subs * lanes
    flat = lax.psum(natural[0, :, lane:], AXES).reshape(-1)
    return matrices, flat


def per_device(
    tokens, frame_level, ln1_gain, ln1_bias, qkv_weight, qv_bias, proj_weight, proj_bias,
    ln2_gain, ln2_bias, fc1_weight, fc1_bias, fc2_weight, fc2_bias, d_out,
):
    frames, rows_here, columns, width = tokens.shape
    height = rows_here * lax.axis_size("rows")
    hidden_width = fc1_weight.shape[1]
    cells = HALF * columns
    grouped = (frames, rows_here // HALF, cells, width)
    tokens4, d4 = tokens.reshape(grouped), d_out.reshape(grouped)
    if is_cube():
        me = place_index().astype(jnp.int32)
        vectors = (
            ln1_gain, ln1_bias, qv_bias, proj_bias, ln2_gain, ln2_bias, fc2_bias, fc1_bias
        )
        own_a, own_b = pack(me[None], vectors, qkv_weight, proj_weight, fc1_weight, fc2_weight)
        z_a = along_z(own_a)
        halo = from_behind(jnp.stack([tokens4[:, 0], d4[:, 0]]), "rows", -1)
        column_a = join(own_a[None], *(z[None] for z in z_a))
        z_b = along_z(after(own_b, *z_a))
        mine_a = (column_a, *over_plane(column_a))
        column_b = join(own_b[None], *(z[None] for z in z_b))
        *mine_a, column_b = lax.optimization_barrier((*mine_a, column_b))
        attend_blocks = (*mine_a, *(flipped(piece, "rows", 1) for piece in mine_a))
        mine_b = (column_b, *over_plane(column_b))
    else:
        me = jnp.int32(0)
        attend_blocks = gather_blocks((qkv_weight,), (ln1_gain, ln1_bias, qv_bias))
        middle_blocks = gather_blocks(
            (proj_weight, fc1_weight, fc2_weight), (proj_bias, ln2_gain, ln2_bias, fc2_bias, fc1_bias)
        )
        halo = from_behind(jnp.stack([tokens4[:, 0], d4[:, 0]]), "rows", -1)
    info = jnp.concatenate([frame_level, jnp.stack([lax.axis_index("rows").astype(jnp.int32), me])])
    q, k, v, p, o = attend(info, tokens4, halo, attend_blocks, height, columns)
    if is_cube():
        *mine_b, o = lax.optimization_barrier((*mine_b, o))
        middle_blocks = (*mine_b, *(flipped(piece, "rows", 1) for piece in mine_b))
    m_out, m_halo, dx, do, keep, send = middle(
        info, tokens4, halo, d4, o, middle_blocks, hidden_width, columns
    )
    m_back = from_behind(m_halo, "rows", 1)
    states = (info, tokens4, halo, q, k, v, p, do, dx, attend_blocks, columns)
    shapes_b = ((width, width), (width, hidden_width), (hidden_width, width))
    shapes_a = ((width, 3 * width),)
    if is_cube():
        shards = lax.axis_size("dp") * lax.axis_size("rows")
        cores_b = sum_cores(keep, send)
        part_a = back(*states, (), frames, 2, False)
        *part_a, cores_b, m_back = lax.optimization_barrier((*part_a, cores_b, m_back))
        plane_b = sum_plane(*cores_b)
        part_b = back(*states, part_a[:2], frames + 2, frames, False)
        g_back = from_behind(part_b[1], "rows", 1)
        sums = (*part_a[2:], *part_b[2:])
        g_out, keep, send = back(*states, (part_b[0], *sums), 2, frames - 2, True)
        plane_b, send = lax.optimization_barrier((plane_b, send))
        plane_a = sum_plane(*sum_cores(keep, send))
        line_b = [flipped(plane_b[1][z - 1], "dp", 2 * z) for z in (1, 2, 3)]
        line_b, plane_a = lax.optimization_barrier((line_b, plane_a))
        sums_b, flat_b = own_rows(plane_b[0] + sum(wide(x) for x in line_b), shapes_b, shards)
        sums_a, flat_a = own_rows(sum_line(*plane_a), shapes_a, shards)
    else:
        sums_b, flat_b = scatter_sums(keep, send, shapes_b)
        before = back(*states, (), frames, frames, False)
        g_back = from_behind(before[1], "rows", 1)
        g_out, keep, send = back(*states, (before[0], *before[2:]), 0, frames, True)
        sums_a, flat_a = scatter_sums(keep, send, shapes_a)
    dw_proj, dw_up, dw_down = sums_b
    db_proj, dg_two, db_two, db_down, db_up = own_vectors(
        flat_b, (width, width, width, width, hidden_width)
    )
    (dw_qkv,) = sums_a
    dg_one, db_one, db_qv = own_vectors(flat_a, (width, width, 2 * width))
    return (
        m_out.at[:, 0].set(m_back).reshape(tokens.shape),
        g_out.at[:, 0].set(g_back).reshape(tokens.shape),
        dg_one, db_one, dw_qkv, db_qv, dw_proj, db_proj, dg_two, db_two, dw_up, db_up, dw_down, db_down,
    )


def solution(mesh):
    both = ("dp", "rows")
    frame, vector, matrix = P("dp", "rows", None, None), P(both), P(both, None)
    return jax.shard_map(
        per_device,
        mesh=mesh,
        in_specs=(
            frame, P("dp"), vector, vector, matrix, vector, matrix, vector,
            vector, vector, matrix, vector, matrix, vector, frame,
        ),
        out_specs=(
            frame, frame, vector, vector, matrix, vector, matrix, vector,
            vector, vector, matrix, vector, matrix, vector,
        ),
        check_vma=False,
    )
```

```python
import functools

import jax
import jax.numpy as jnp
from jax import lax
from jax.experimental import pallas as pl
from jax.experimental.pallas import tpu as pltpu
from jax.sharding import PartitionSpec as P

HEAD_DIM = 64
WIN = 8
HALF = WIN // 2
CELLS = WIN * WIN
LANES = 4 * HEAD_DIM
LANE = 128
ROWS = 16
EPSILON = 1e-05
INV_ROOT_TWO = 0.7071067811865476
INV_ROOT_TWO_PI = 0.3989422804014327
F32 = jnp.float32
BF16 = jnp.bfloat16
VMEM_LIMIT = 60 * 1024 * 1024


def from_behind(x, axis, by):
    devices = lax.axis_size(axis)
    return lax.ppermute(x, axis, [(i, (i + by) % devices) for i in range(devices)])


def dot(a, b):
    return jnp.dot(a, b, preferred_element_type=F32)


def dot_t(a, b):
    return lax.dot_general(a, b, (((1,), (1,)), ((), ())), preferred_element_type=F32)


def to_window_order(x, columns):
    depth = x.shape[-1]
    grid = pltpu.roll(x.reshape(WIN, columns, depth), columns - HALF, 1)
    grid = grid.reshape(WIN, columns // WIN, WIN, depth).swapaxes(0, 1)
    return grid.reshape(WIN * columns, depth)


def from_window_order(x, columns):
    depth = x.shape[-1]
    grid = x.reshape(columns // WIN, WIN, WIN, depth).swapaxes(0, 1)
    grid = pltpu.roll(grid.reshape(WIN, columns, depth), HALF, 1)
    return grid.reshape(WIN * columns, depth)


def normalize(values):
    center = values - jnp.mean(values, axis=-1, keepdims=True)
    inverse = lax.rsqrt(jnp.mean(center * center, axis=-1, keepdims=True) + EPSILON)
    return center * inverse, inverse


def norm_back(grad, normed, inverse):
    return inverse * (
        grad
        - jnp.mean(grad, axis=-1, keepdims=True)
        - normed * jnp.mean(grad * normed, axis=-1, keepdims=True)
    )


def block_diag(x):
    lane_head = lax.broadcasted_iota(jnp.int32, x.shape, 1) // HEAD_DIM
    zero = jnp.zeros_like(x)
    return jnp.concatenate(
        [jnp.where(lane_head == head, x, zero) for head in range(LANES // HEAD_DIM)], axis=0
    )


def dot_down(a, b):
    pair = 2 * HEAD_DIM
    first = lax.broadcasted_iota(jnp.int32, (CELLS, pair), 1) < HEAD_DIM
    out = []
    for lane in range(0, LANES, pair):
        both = lax.dot_general(
            a[:, lane : lane + pair],
            b[:, lane : lane + pair],
            (((0,), (0,)), ((), ())),
            preferred_element_type=F32,
        )
        out.append(jnp.where(first, both[:HEAD_DIM], both[HEAD_DIM:]))
    return jnp.concatenate(out, axis=1)


def window_bias(info, frames, step, win, columns, height, rows_here):
    frame = lax.rem(step, frames)
    level = info[frame]
    factor = jnp.where(level >= 2, 4, jnp.where(level >= 1, 2, 1))
    base = info[frames] * rows_here + (step // frames) * WIN
    row_limit, col_limit = height * factor // 4, columns * factor // 4
    last_row = (base + WIN >= height).astype(jnp.int32)
    last_col = jnp.int32(win == columns // WIN - 1)
    key = lax.broadcasted_iota(jnp.int32, (CELLS, LANES), 0)
    query = lax.broadcasted_iota(jnp.int32, (CELLS, LANES), 1) % CELLS
    row = base + key // WIN + HALF
    col = win * WIN + key % WIN + HALF
    row = jnp.where(row >= height, row - height, row)
    col = jnp.where(col >= columns, col - columns, col)
    differ = key ^ query
    bad = (differ // (HALF * WIN) % 2) * last_row + (differ // HALF % 2) * last_col
    bad = bad + (row >= row_limit).astype(jnp.int32) + (col >= col_limit).astype(jnp.int32)
    return jnp.where(bad > 0, -100.0, 0.0)


def place(info, at, pieces, targets, vec, vec_sem):
    blocks = [
        (source, k, core, i)
        for core, sources in enumerate(pieces)
        for i, (source, k) in enumerate((s, k) for s in sources for k in range(s.shape[0]))
    ]
    lanes = vec.shape[-1]
    start = 0
    for sources in pieces:
        for source in sources:
            count = source.shape[0]
            tail = source.at[:, :, pl.ds(source.shape[-1] - lanes, lanes)]
            pltpu.make_async_copy(tail, vec.at[pl.ds(start, count)], vec_sem).start()
            start += count
    for lane, lanes, rows, target, sem in targets:
        for source, k, core, i in blocks:
            block = info[at] ^ (bits_of(i) | core)
            for sub in range(rows // ROWS):
                row = pl.multiple_of(block * rows + sub * ROWS, ROWS)
                pltpu.make_async_copy(
                    source.at[k, :, pl.ds(lane + sub * lanes, lanes)], target.at[pl.ds(row, ROWS), :], sem
                ).start()


def halves(pieces):
    return pieces[: len(pieces) // 2], pieces[len(pieces) // 2 :]


def wait_bytes(target, sem):
    pltpu.make_async_copy(target, target, sem).wait()


def bits_of(j):
    return (j % 4) * 8 + (j // 8) * 4 + (j // 4 % 2) * 2


def natural_rows(vec):
    total = jnp.sum(vec[...].astype(F32), axis=0)
    return [total[r : r + 1, :] for r in range(total.shape[0])]


def hand_over(info, at, sources, tail, keep, send):
    for core, out in enumerate((keep, send)):
        for j in range(out.shape[0]):
            block = info[at] ^ (bits_of(j) | core)
            for lane, lanes, rows, source in sources:
                for sub in range(rows // ROWS):
                    row = pl.multiple_of(block * rows + sub * ROWS, ROWS)
                    start = lane + sub * lanes
                    out[j, :, start : start + lanes] = source[pl.ds(row, ROWS), :].astype(out.dtype)
            out[j, :, out.shape[-1] - tail.shape[-1] :] = tail.astype(out.dtype)


def store_rows(out, halo, held, sem, local, total, window_row, frame, value):
    slot = lax.rem(local, 2)
    half = out.shape[2]
    count = value.shape[0] // (2 * half)

    def finish(slot):
        for part in range(2 * count):
            rows = held.at[slot, pl.ds(part * half, half)]
            pltpu.make_async_copy(rows, rows, sem.at[slot, part]).wait()

    @pl.when(local >= 2)
    def _():
        finish(slot)

    held[slot] = value
    for i in range(count):
        at = frame + i
        top, bottom = (held.at[slot, pl.ds((2 * i + part) * half, half)] for part in range(2))
        top_sem, bottom_sem = sem.at[slot, 2 * i], sem.at[slot, 2 * i + 1]
        pltpu.make_async_copy(top, out.at[at, 1 + 2 * window_row], top_sem).start()

        @pl.when(window_row == 0)
        def _():
            pltpu.make_async_copy(bottom, out.at[at, 2], bottom_sem).start()

        if halo is not None:

            @pl.when(window_row == 1)
            def _():
                pltpu.make_async_copy(bottom, halo.at[at], bottom_sem).start()

    @pl.when(local == total - 1)
    def _():
        finish(slot)
        if total > 1:
            finish(1 - slot)


def attend_kernel(
    frames, columns, height, rows_here,
    info, top, own, halo, *rest,
):
    q_out, k_out, v_out, p_out, o_out, weight, vec, lines, sem = rest[-9:]
    step = pl.program_id(0)
    width = top.shape[-1]

    @pl.when(step == 0)
    def _():
        place(
            info, frames + 1, halves(rest[:-9]), [(0, 3 * width, ROWS, weight, sem.at[0])], vec, sem.at[1]
        )
        wait_bytes(weight, sem.at[0])
        wait_bytes(vec, sem.at[1])
        pieces = natural_rows(vec)
        per = width // LANE
        for line in range(lines.shape[0]):
            lines[line : line + 1, :] = jnp.concatenate(pieces[line * per : (line + 1) * per], axis=1)

    gain, bias, bias_q, bias_v = (lines.at[i : i + 1] for i in range(4))
    bottom = jnp.where(step < frames, own[...], halo[...])
    x = jnp.concatenate([top[...], bottom], axis=0).astype(F32)
    normed, _ = normalize(to_window_order(x, columns))
    hidden = (normed * gain[...] + bias[...]).astype(BF16)
    q_out[...] = (dot(hidden, weight[:, :width]) + bias_q[...]).astype(BF16) * 0.125
    k_out[...] = dot(hidden, weight[:, width : 2 * width]).astype(BF16)
    v_out[...] = (dot(hidden, weight[:, 2 * width :]) + bias_v[...]).astype(BF16)

    wins, groups = range(columns // WIN), range(width // LANES)
    items = [(w, slice(w * CELLS, (w + 1) * CELLS), slice(g * LANES, (g + 1) * LANES)) for w in wins for g in groups]
    masks = [window_bias(info, frames, step, w, columns, height, rows_here) for w in wins]
    scores = [dot_t(k_out[r, l], block_diag(q_out[r, l])) for _, r, l in items]
    exponents = []
    for (w, _, _), score in zip(items, scores):
        score = score + masks[w]
        exponents.append(jnp.exp(score - jnp.max(score, axis=0, keepdims=True)))
    probs = [(e * (1.0 / jnp.sum(e, axis=0, keepdims=True))).astype(BF16) for e in exponents]
    outs = [dot_down(p, v_out[r, l]).astype(BF16) for p, (_, r, l) in zip(probs, items)]
    for (_, r, l), p, out in zip(items, probs, outs):
        p_out[r, l] = p
        o_out[r, l] = out


def middle_kernel(
    frames, columns, chunk,
    info, top, own, halo, dtop, down, dhalo, o_in, *rest,
):
    (
        m_out, m_halo, dx_out, do_out, keep, send,
        w_proj, w_up, w_down, vec, lines, b_up, dw_proj, dw_up, dw_down_t, dw_down, small, g_s, du_s, held,
        sem, out_sem,
    ) = rest[-22:]
    step = pl.program_id(0)
    width = top.shape[-1]
    hidden_width = w_up.shape[-1]
    b_proj, g_two, b_two, b_down = (lines.at[i : i + 1] for i in range(4))

    @pl.when(step == 0)
    def _():
        targets = [
            (0, width, ROWS, w_proj, sem.at[0]),
            (width, hidden_width, ROWS, w_up, sem.at[1]),
            (width + hidden_width, width, w_down.shape[0] // 32, w_down, sem.at[2]),
        ]
        place(info, frames + 1, halves(rest[:-22]), targets, vec, sem.at[3])
        wait_bytes(vec, sem.at[3])
        pieces = natural_rows(vec)
        per = width // pieces[0].shape[-1]
        for line in range(4):
            lines[line : line + 1, :] = jnp.concatenate(pieces[line * per : (line + 1) * per], axis=1)
        b_up[...] = jnp.concatenate(pieces[4 * per :], axis=1)
        for target, copied in ((w_proj, sem.at[0]), (w_up, sem.at[1]), (w_down, sem.at[2])):
            wait_bytes(target, copied)
        dw_proj[...] = jnp.zeros_like(dw_proj)
        dw_up[...] = jnp.zeros_like(dw_up)
        dw_down_t[...] = jnp.zeros_like(dw_down_t)
        small[...] = jnp.zeros_like(small)

    count = top.shape[0]
    pairs = frames // count
    window_row = step // pairs

    def rows_of(top, own, halo):
        out = []
        for i in range(count):
            bottom = jnp.where(window_row == 0, own[i], halo[i])
            rows = jnp.concatenate([top[i], bottom], axis=0).astype(F32)
            out.append(to_window_order(rows, columns))
        return jnp.concatenate(out, axis=0)

    dy = rows_of(dtop, down, dhalo)
    dy_low = dy.astype(BF16)
    o_rows = o_in[...].reshape(-1, width)
    x2 = rows_of(top, own, halo) + dot(o_rows, w_proj[...]) + b_proj[...]
    parts = [slice(start, start + chunk) for start in range(0, hidden_width, chunk)]
    dgs = {0: dot_t(dy_low, w_down[parts[0], :])}
    normed, inverse = normalize(x2)
    h2 = (normed * g_two[...] + b_two[...]).astype(BF16)
    h2_t = h2.T
    dy_t = dy_low.T
    total = x2 + b_down[...]
    dh2 = jnp.zeros_like(x2)

    def enter(index):
        if index not in dgs:
            dgs[index] = dot_t(dy_low, w_down[parts[index], :])
        return dot(h2, w_up[:, parts[index]]) + b_up[:, parts[index]]

    ahead = enter(0)
    for index in range(len(parts) + 1):
        if index < len(parts):
            u, part = ahead, parts[index]
            if index + 1 < len(parts):
                ahead = enter(index + 1)
            phi = 0.5 * (1.0 + lax.erf(u * INV_ROOT_TWO))
            g_s[index % 2] = (u * phi).astype(BF16)
            du = dgs[index] * (phi + u * jnp.exp(-0.5 * u * u) * INV_ROOT_TWO_PI)
            du_s[index % 2] = du.astype(BF16)
            small[0:1, part] += jnp.sum(du, axis=0, keepdims=True)
        if index > 0:
            old, slot = parts[index - 1], (index - 1) % 2
            total += dot(g_s[slot], w_down[old, :])
            dh2 += dot_t(du_s[slot], w_up[:, old])
            dw_up[:, old] += dot(h2_t, du_s[slot])
            dw_down_t[:, old] += dot(dy_t, g_s[slot])
    block = total.shape[0] // count
    mixed = [from_window_order(total[i * block : (i + 1) * block], columns) for i in range(count)]
    mixed = jnp.concatenate(mixed, axis=0).astype(BF16)
    store_rows(
        m_out, m_halo, held, out_sem, step, pl.num_programs(0), window_row, lax.rem(step, pairs) * count, mixed
    )
    small[1:2, :width] += jnp.sum(dy, axis=0, keepdims=True)
    small[2:3, :width] += jnp.sum(dh2 * normed, axis=0, keepdims=True)
    small[3:4, :width] += jnp.sum(dh2, axis=0, keepdims=True)
    dx2 = dy + norm_back(dh2 * g_two[...], normed, inverse)
    da = dx2.astype(BF16)
    small[4:5, :width] += jnp.sum(dx2, axis=0, keepdims=True)
    dx_out[...] = dx2.reshape(dx_out.shape)
    dw_proj[...] += dot(o_rows.T, da)
    do_out[...] = dot_t(da, w_proj[...]).astype(BF16).reshape(do_out.shape)

    @pl.when(step == pl.num_programs(0) - 1)
    def _():
        for lane in range(0, hidden_width, LANE):
            dw_down[lane : lane + LANE, :] = dw_down_t[:, lane : lane + LANE].astype(BF16).T
        order = (4, 2, 3, 1)
        flat = jnp.concatenate([small[r : r + 1, :width] for r in order] + [small[0:1, :]], axis=1)
        lines_of = keep.shape[-1] - width - 2 * hidden_width
        tail = jnp.concatenate(
            [flat[:, i * lines_of : (i + 1) * lines_of] for i in range(ROWS)], axis=0
        )
        sources = [
            (0, width, ROWS, dw_proj),
            (width, hidden_width, ROWS, dw_up),
            (width + hidden_width, width, dw_down.shape[0] // 32, dw_down),
        ]
        hand_over(info, frames + 1, sources, tail, keep, send)


def back_kernel(
    frames, columns, first, count, with_halo, n_blocks, n_before, ends,
    info, top, own, halo, q_in, k_in, v_in, p_in, do_in, dx_in, *rest,
):
    blocks, rest = rest[:n_blocks], rest[n_blocks:]
    earlier = rest[1 + with_halo : n_before] if n_before else ()
    *outs, d_s, weight, vec, lines, held, sem, out_sem = rest[n_before:]
    g_out, g_halo = outs[0], outs[1] if with_halo else None
    if ends:
        keep, send, dw, small, *loaded = outs[1 + with_halo :]
    else:
        dw, small = outs[1 + with_halo :]
    local = pl.program_id(0)
    step = lax.rem(local + first, 2 * frames)
    width = top.shape[-1]
    gain, bias = (lines.at[i : i + 1] for i in range(2))

    @pl.when(local == 0)
    def _():
        place(
            info, frames + 1, halves(blocks), [(0, 3 * width, ROWS, weight, sem.at[0])], vec, sem.at[1]
        )
        dw[...] = jnp.zeros_like(dw)
        small[...] = jnp.zeros_like(small)
        if ends:
            for i, (source, target) in enumerate(zip(earlier, loaded)):
                pltpu.make_async_copy(source, target, sem.at[2 + i]).start()

    items = [
        (slice(w * CELLS, (w + 1) * CELLS), g * LANES)
        for w in range(columns // WIN)
        for g in range(width // LANES)
    ]
    items = [(r, at, slice(at, at + LANES)) for r, at in items]
    diags = [block_diag(do_in[r, l]) for r, _, l in items]
    dps = [dot_t(v_in[r, l], diag) for (r, _, l), diag in zip(items, diags)]
    dvs = [dot(p_in[r, l], diag).astype(BF16) for (r, _, l), diag in zip(items, diags)]
    dss = []
    for (r, _, l), dp in zip(items, dps):
        full = p_in[r, l].astype(F32)
        dss.append((full * (dp - jnp.sum(dp * full, axis=0, keepdims=True))).astype(BF16))
    dks = [dot(ds, block_diag(q_in[r, l])).astype(BF16) for (r, _, l), ds in zip(items, dss)]
    dqs = [(dot_down(ds, k_in[r, l]) * 0.125).astype(BF16) for (r, _, l), ds in zip(items, dss)]
    for (r, at, _), dq, dk, dv in zip(items, dqs, dks, dvs):
        for part, grad in enumerate((dq, dk, dv)):
            d_s[r, part * width + at : part * width + at + LANES] = grad

    @pl.when(local == 0)
    def _():
        wait_bytes(weight, sem.at[0])
        wait_bytes(vec, sem.at[1])
        pieces = natural_rows(vec)
        per = width // LANE
        for line in range(lines.shape[0]):
            lines[line : line + 1, :] = jnp.concatenate(pieces[line * per : (line + 1) * per], axis=1)

    bottom = jnp.where(step < frames, own[...], halo[...])
    x = jnp.concatenate([top[...], bottom], axis=0).astype(F32)
    normed, inverse = normalize(to_window_order(x, columns))
    hidden = (normed * gain[...] + bias[...]).astype(BF16)
    d = d_s[...]
    dw[...] += dot(hidden.T, d)
    small[0:1, :] += jnp.sum(d.astype(F32), axis=0, keepdims=True)
    dh = dot_t(d, weight[...])
    small[1:2, :width] += jnp.sum(dh * normed, axis=0, keepdims=True)
    small[2:3, :width] += jnp.sum(dh, axis=0, keepdims=True)
    grad = dx_in[...] + norm_back(dh * gain[...], normed, inverse)
    grad = from_window_order(grad, columns).astype(BF16)
    store_rows(
        g_out, g_halo, held, out_sem, local, count, step // frames, lax.rem(step, frames), grad
    )

    if ends:

        @pl.when(local == count - 1)
        def _():
            for i, target in enumerate(loaded):
                wait_bytes(target, sem.at[2 + i])
                total = dw if i % 2 == 0 else small
                total[...] += target[...]
            pieces = [small[1:2, :width], small[2:3, :width], small[0:1, :width], small[0:1, 2 * width :]]
            flat = jnp.concatenate(pieces, axis=1)
            tail = jnp.concatenate([flat[:, i * LANE : (i + 1) * LANE] for i in range(ROWS)], axis=0)
            hand_over(info, frames + 1, [(0, 3 * width, ROWS, dw)], tail, keep, send)


def join_kernel(*refs):
    out = refs[-1]
    rows = refs[0].shape[0]
    for index, ref in enumerate(refs[:-1]):
        out[index * rows : (index + 1) * rows] = ref[...]


def join(*parts):
    shape = (len(parts) * parts[0].shape[0],) + parts[0].shape[1:]
    vmem = pl.BlockSpec(memory_space=pltpu.VMEM)
    return pl.pallas_call(
        join_kernel,
        out_shape=jax.ShapeDtypeStruct(shape, parts[0].dtype),
        in_specs=[vmem] * len(parts),
        out_specs=vmem,
        compiler_params=pltpu.CompilerParams(vmem_limit_bytes=VMEM_LIMIT),
        name="join",
    )(*parts)


def pack_kernel(index_ref, *refs):
    vectors, (qkv, proj, up, down, a_out, b_out) = refs[:-6], refs[-6:]
    index = index_ref[0]
    wide = 2 * LANE

    def spread_rows(sections, lanes):
        row = lax.broadcasted_iota(jnp.int32, (ROWS, wide), 0)
        total = jnp.zeros((ROWS, wide), F32)
        for ref, base in sections:
            count = ref.shape[0]
            at = base + index * count
            own = ref[...].astype(F32)[None, :]
            own = jnp.concatenate([own, jnp.zeros((1, wide - count), F32)], axis=1)
            moved = pltpu.roll(own, lax.rem(at, lanes), 1)
            total = total + jnp.where(row == at // lanes, moved, 0.0)
        return total[:, :lanes].astype(BF16)

    width = proj.shape[1]
    full = qkv.shape[1]
    a_out[:, :full] = qkv[...]
    sections = [(vectors[i], i * width) for i in range(3)]
    a_out[:, full:] = spread_rows(sections, a_out.shape[1] - full)
    hidden = up.shape[1]
    b_out[:, :width] = proj[...]
    b_out[:, width : width + hidden] = up[...]
    for i in range(down.shape[0] // ROWS):
        at = width + hidden + i * width
        b_out[:, at : at + width] = down[i * ROWS : (i + 1) * ROWS]
    full = width + 2 * hidden
    sections = [(vectors[3 + i], i * width) for i in range(5)]
    b_out[:, full:] = spread_rows(sections, b_out.shape[1] - full)


def pack(index, vectors, qkv, proj, up, down):
    lanes_a = qkv.shape[1] + LANE
    lanes_b = proj.shape[1] + 2 * up.shape[1] + 2 * LANE
    vmem = pl.BlockSpec(memory_space=pltpu.VMEM)
    return pl.pallas_call(
        pack_kernel,
        out_shape=[
            jax.ShapeDtypeStruct((ROWS, lanes_a), BF16),
            jax.ShapeDtypeStruct((ROWS, lanes_b), BF16),
        ],
        in_specs=[pl.BlockSpec(memory_space=pltpu.SMEM)] + [vmem] * (len(vectors) + 4),
        out_specs=[vmem, vmem],
        name="pack",
    )(index, *vectors, qkv, proj, up, down)


def grid_specs(frames, cells, width, first=0, which=0, count=None):
    turns = frames // (count or 1)
    at = lambda s: (s + first) % (2 * turns)
    top = pl.BlockSpec(
        (count, None, cells, width), lambda s, *_: (at(s) % turns, 1 + 2 * (at(s) // turns), 0, 0)
    )
    own = pl.BlockSpec(
        (count, None, cells, width), lambda s, *_: (jnp.minimum(at(s), turns - 1), 2, 0, 0)
    )
    halo = pl.BlockSpec(
        (None, count, cells, width), lambda s, *_: (which, jnp.maximum(at(s) - turns, 0), 0, 0)
    )
    return [top, own, halo]


def whole_out(shape):
    zeros = (0,) * len(shape)
    return pl.BlockSpec(shape, lambda s, *_: zeros, pipeline_mode=pl.Buffered(1))


ANYWHERE = pl.BlockSpec(memory_space=pl.ANY)


def params():
    return pltpu.CompilerParams(vmem_limit_bytes=VMEM_LIMIT, dimension_semantics=("arbitrary",))


def attend(info, tokens4, halo, blocks, height, columns):
    frames, groups, cells, width = tokens4.shape
    steps, block = 2 * frames, 2 * cells
    row = pl.BlockSpec((None, block, width), lambda s, *_: (s, 0, 0))
    shape = jax.ShapeDtypeStruct((steps, block, width), BF16)
    return pl.pallas_call(
        functools.partial(attend_kernel, frames, columns, height, groups * HALF),
        out_shape=[shape] * 5,
        grid_spec=pltpu.PrefetchScalarGridSpec(
            num_scalar_prefetch=1,
            grid=(steps,),
            in_specs=grid_specs(frames, cells, width) + [ANYWHERE] * len(blocks),
            out_specs=[row] * 5,
            scratch_shapes=[
                pltpu.VMEM((width, 3 * width), BF16),
                pltpu.VMEM((32, ROWS, LANE), BF16),
                pltpu.VMEM((4, width), F32),
                pltpu.SemaphoreType.DMA((2,)),
            ],
        ),
        compiler_params=params(),
        cost_estimate=pl.CostEstimate(flops=3 * 10**10, bytes_accessed=3 * 10**7, transcendentals=10**6),
        name="attend",
    )(info, tokens4, tokens4, halo, *blocks)


def middle(info, tokens4, halo, d4, o, blocks, hidden_width, columns, chunk=256, count=1):
    frames, groups, cells, width = tokens4.shape
    steps, block = 2 * frames, 2 * cells
    row = pl.BlockSpec((count, block, width), lambda s, *_: (s, 0, 0))
    ins = grid_specs(frames, cells, width, count=count)
    ins += grid_specs(frames, cells, width, which=1, count=count)
    mine = (16,) + blocks[0].shape[1:]
    return pl.pallas_call(
        functools.partial(middle_kernel, frames, columns, chunk),
        out_shape=[
            jax.ShapeDtypeStruct(tokens4.shape, BF16),
            jax.ShapeDtypeStruct(halo.shape[1:], BF16),
            jax.ShapeDtypeStruct((steps, block, width), F32),
            jax.ShapeDtypeStruct((steps, block, width), BF16),
            jax.ShapeDtypeStruct(mine, BF16),
            jax.ShapeDtypeStruct(mine, BF16),
        ],
        grid_spec=pltpu.PrefetchScalarGridSpec(
            num_scalar_prefetch=1,
            grid=(steps // count,),
            in_specs=ins + [row] + [ANYWHERE] * len(blocks),
            out_specs=[ANYWHERE, ANYWHERE, row, row, whole_out(mine), whole_out(mine)],
            scratch_shapes=[
                pltpu.VMEM((width, width), BF16),
                pltpu.VMEM((width, hidden_width), BF16),
                pltpu.VMEM((hidden_width, width), BF16),
                pltpu.VMEM((32, ROWS, 2 * LANE), BF16),
                pltpu.VMEM((4, width), F32),
                pltpu.VMEM((1, hidden_width), F32),
                pltpu.VMEM((width, width), F32),
                pltpu.VMEM((width, hidden_width), F32),
                pltpu.VMEM((width, hidden_width), F32),
                pltpu.VMEM((hidden_width, width), BF16),
                pltpu.VMEM((8, hidden_width), F32),
                pltpu.VMEM((2, count * block, chunk), BF16),
                pltpu.VMEM((2, count * block, chunk), BF16),
                pltpu.VMEM((2, count * block, width), BF16),
                pltpu.SemaphoreType.DMA((4,)),
                pltpu.SemaphoreType.DMA((2, 2 * count)),
            ],
        ),
        compiler_params=params(),
        cost_estimate=pl.CostEstimate(flops=9 * 10**10, bytes_accessed=4 * 10**7, transcendentals=10**7),
        name="middle",
    )(info, tokens4, tokens4, halo, d4, d4, halo, o, *blocks)


def back(info, tokens4, halo, q, k, v, p, do, dx, blocks, columns, before, first, count, ends):
    frames, groups, cells, width = tokens4.shape
    steps, block = 2 * frames, 2 * cells
    row = pl.BlockSpec((None, block, width), lambda s, *_: ((s + first) % steps, 0, 0))
    mine = (16,) + blocks[0].shape[1:]
    dw, small = (width, 3 * width), (8, 3 * width)
    handed = [jax.ShapeDtypeStruct(mine, BF16)] * 2
    sums = [jax.ShapeDtypeStruct(dw, F32), jax.ShapeDtypeStruct(small, F32)]
    in_vmem = [pltpu.VMEM(dw, F32), pltpu.VMEM(small, F32)]
    held = 10 + len(blocks)
    with_halo = first + count > frames
    g_shapes = [jax.ShapeDtypeStruct(tokens4.shape, BF16), jax.ShapeDtypeStruct(halo.shape[1:], BF16)]
    g_shapes = g_shapes[: 1 + with_halo]
    return pl.pallas_call(
        functools.partial(
            back_kernel, frames, columns, first, count, with_halo, len(blocks), len(before), ends
        ),
        out_shape=g_shapes + (handed if ends else sums),
        grid_spec=pltpu.PrefetchScalarGridSpec(
            num_scalar_prefetch=1,
            grid=(count,),
            in_specs=grid_specs(frames, cells, width, first)
            + [row] * 6
            + [ANYWHERE] * (len(blocks) + len(before)),
            out_specs=[ANYWHERE] * len(g_shapes)
            + ([whole_out(mine)] * 2 if ends else [whole_out(dw), whole_out(small)]),
            scratch_shapes=(in_vmem * ((len(before) - len(g_shapes)) // 2 + 1) if ends else [])
            + [
                pltpu.VMEM((block, 3 * width), BF16),
                pltpu.VMEM((width, 3 * width), BF16),
                pltpu.VMEM((32, ROWS, LANE), BF16),
                pltpu.VMEM((4, width), F32),
                pltpu.VMEM((2, block, width), BF16),
                pltpu.SemaphoreType.DMA((8,)),
                pltpu.SemaphoreType.DMA((2, 2)),
            ],
        ),
        input_output_aliases={held + i: i for i in range(len(g_shapes))} if before else {},
        compiler_params=params(),
        cost_estimate=pl.CostEstimate(
            flops=6 * 10**9 * count, bytes_accessed=5 * 10**6 * count, transcendentals=10**5
        ),
        name="back",
    )(info, tokens4, tokens4, halo, q, k, v, p, do, dx, *blocks, *before)


AXES = ("dp", "rows")


def flip_perm(axis, bits):
    return [(i, i ^ bits) for i in range(lax.axis_size(axis))]


def flipped(x, axis, bits):
    return lax.ppermute(x, axis, flip_perm(axis, bits))


def flipped_both(x, dp_bits, rows_bits):
    dp, rows = lax.axis_size("dp"), lax.axis_size("rows")
    pairs = [
        (d * rows + r, (d ^ dp_bits) * rows + (r ^ rows_bits)) for d in range(dp) for r in range(rows)
    ]
    return lax.ppermute(x, AXES, pairs)


def is_cube():
    return lax.axis_size("dp") == 8 and lax.axis_size("rows") == 4


def place_index():
    return lax.axis_index("dp") * lax.axis_size("rows") + lax.axis_index("rows")


def after(value, *others):
    return lax.optimization_barrier((value,) + others)[0]


def along_z(own):
    return [flipped(own, "dp", 2 * z) for z in (1, 2, 3)]


def over_plane(column):
    return [flipped(column, "rows", 2), flipped(column, "dp", 1), flipped_both(column, 1, 2)]


def gather_blocks(matrices, vectors):
    full = [lax.all_gather(m, AXES, axis=0, tiled=True) for m in matrices]
    lanes = []
    for m in full:
        per = m.shape[0] // 32
        blocks = m.reshape(32, per // ROWS, ROWS, m.shape[1]).transpose(0, 2, 1, 3)
        lanes.append(blocks.reshape(32, ROWS, -1))
    flat = jnp.concatenate([lax.all_gather(v, AXES, axis=0, tiled=True) for v in vectors])
    tail = flat.reshape(1, ROWS, -1)
    lanes.append(jnp.concatenate([tail, jnp.zeros((31,) + tail.shape[1:], tail.dtype)]))
    natural = jnp.concatenate(lanes, axis=2)
    relative = natural.reshape(4, 2, 2, 2, ROWS, -1).transpose(3, 1, 2, 0, 4, 5)
    relative = relative.reshape(2, 16, ROWS, -1)
    return relative[0], relative[1]


def own_rows(total, matrix_shapes, shards):
    matrices, lane = [], 0
    for rows, lanes in matrix_shapes:
        subs = rows // shards // ROWS
        pieces = [total[:, lane + i * lanes : lane + (i + 1) * lanes] for i in range(subs)]
        matrices.append(jnp.concatenate(pieces, axis=0))
        lane += subs * lanes
    return matrices, total[:, lane:].reshape(-1)


def wide(x):
    return x.astype(F32)


def sum_cores(keep, send):
    first = wide(keep) + wide(flipped(send, "rows", 1))
    return first[:4], first[4:].astype(BF16)


def sum_plane(kept, low):
    plane = (
        kept
        + wide(flipped(low[:4], "rows", 2))
        + wide(flipped(low[4:8], "dp", 1))
        + wide(flipped_both(low[8:], 1, 2))
    )
    return plane[0], plane[1:].astype(BF16)


def sum_line(kept, low):
    for z in (1, 2, 3):
        kept += wide(flipped(low[z - 1], "dp", 2 * z))
    return kept


def own_vectors(flat, vector_sizes):
    shards = lax.axis_size("dp") * lax.axis_size("rows")
    vectors, start = [], 0
    for size in vector_sizes:
        count = size // shards
        vectors.append(lax.dynamic_slice(flat, (start + place_index() * count,), (count,)))
        start += size
    return vectors


def scatter_sums(keep, send, matrix_shapes):
    matrices = []
    relative = jnp.stack([wide(keep), wide(send)]).reshape(2, 2, 2, 4, ROWS, -1)
    natural = relative.transpose(3, 1, 2, 0, 4, 5).reshape(32, ROWS, -1)
    lane = 0
    for rows, lanes in matrix_shapes:
        subs = rows // 32 // ROWS
        piece = natural[:, :, lane : lane + subs * lanes].reshape(32, ROWS, subs, lanes)
        whole_matrix = piece.transpose(0, 2, 1, 3).reshape(rows, lanes)
        matrices.append(lax.psum_scatter(whole_matrix, AXES, scatter_dimension=0, tiled=True))
        lane += subs * lanes
    flat = lax.psum(natural[0, :, lane:], AXES).reshape(-1)
    return matrices, flat


def per_device(
    tokens, frame_level, ln1_gain, ln1_bias, qkv_weight, qv_bias, proj_weight, proj_bias,
    ln2_gain, ln2_bias, fc1_weight, fc1_bias, fc2_weight, fc2_bias, d_out,
):
    frames, rows_here, columns, width = tokens.shape
    height = rows_here * lax.axis_size("rows")
    hidden_width = fc1_weight.shape[1]
    cells = HALF * columns
    grouped = (frames, rows_here // HALF, cells, width)
    tokens4, d4 = tokens.reshape(grouped), d_out.reshape(grouped)
    if is_cube():
        me = place_index().astype(jnp.int32)
        vectors = (
            ln1_gain, ln1_bias, qv_bias, proj_bias, ln2_gain, ln2_bias, fc2_bias, fc1_bias
        )
        own_a, own_b = pack(me[None], vectors, qkv_weight, proj_weight, fc1_weight, fc2_weight)
        z_a = along_z(own_a)
        halo = from_behind(jnp.stack([tokens4[:, 0], d4[:, 0]]), "rows", -1)
        column_a = join(own_a[None], *(z[None] for z in z_a))
        z_b = along_z(after(own_b, *z_a))
        mine_a = (column_a, *over_plane(column_a))
        z_b, halo = lax.optimization_barrier((z_b, halo))
        column_b = join(own_b[None], *(z[None] for z in z_b))
        *mine_a, column_b = lax.optimization_barrier((*mine_a, column_b))
        attend_blocks = (*mine_a, *(flipped(piece, "rows", 1) for piece in mine_a))
        mine_b = (column_b, *over_plane(column_b))
    else:
        me = jnp.int32(0)
        attend_blocks = gather_blocks((qkv_weight,), (ln1_gain, ln1_bias, qv_bias))
        middle_blocks = gather_blocks(
            (proj_weight, fc1_weight, fc2_weight), (proj_bias, ln2_gain, ln2_bias, fc2_bias, fc1_bias)
        )
        halo = from_behind(jnp.stack([tokens4[:, 0], d4[:, 0]]), "rows", -1)
    info = jnp.concatenate([frame_level, jnp.stack([lax.axis_index("rows").astype(jnp.int32), me])])
    q, k, v, p, o = attend(info, tokens4, halo, attend_blocks, height, columns)
    if is_cube():
        first_piece = flipped(mine_b[0], "rows", 1)
        *mine_b, o, first_piece = lax.optimization_barrier((*mine_b, o, first_piece))
        middle_blocks = (*mine_b, first_piece, *(flipped(piece, "rows", 1) for piece in mine_b[1:]))
    m_out, m_halo, dx, do, keep, send = middle(
        info, tokens4, halo, d4, o, middle_blocks, hidden_width, columns
    )
    m_back = from_behind(m_halo, "rows", 1)
    states = (info, tokens4, halo, q, k, v, p, do, dx, attend_blocks, columns)
    shapes_b = ((width, width), (width, hidden_width), (hidden_width, width))
    shapes_a = ((width, 3 * width),)
    if is_cube():
        shards = lax.axis_size("dp") * lax.axis_size("rows")
        cores_b = sum_cores(keep, send)
        part_a = back(*states, (), frames, 4, False)
        *part_a, cores_b, m_back = lax.optimization_barrier((*part_a, cores_b, m_back))
        plane_b = sum_plane(*cores_b)
        g_back = from_behind(part_a[1], "rows", 1)
        g_out, keep, send = back(*states, (part_a[0], *part_a[2:]), 0, 4, True)
        plane_b, send = lax.optimization_barrier((plane_b, send))
        plane_a = sum_plane(*sum_cores(keep, send))
        line_b = [flipped(plane_b[1][z - 1], "dp", 2 * z) for z in (1, 2, 3)]
        line_b, plane_a = lax.optimization_barrier((line_b, plane_a))
        sums_b, flat_b = own_rows(plane_b[0] + sum(wide(x) for x in line_b), shapes_b, shards)
        sums_a, flat_a = own_rows(sum_line(*plane_a), shapes_a, shards)
    else:
        sums_b, flat_b = scatter_sums(keep, send, shapes_b)
        before = back(*states, (), frames, frames, False)
        g_back = from_behind(before[1], "rows", 1)
        g_out, keep, send = back(*states, (before[0], *before[2:]), 0, frames, True)
        sums_a, flat_a = scatter_sums(keep, send, shapes_a)
    dw_proj, dw_up, dw_down = sums_b
    db_proj, dg_two, db_two, db_down, db_up = own_vectors(
        flat_b, (width, width, width, width, hidden_width)
    )
    (dw_qkv,) = sums_a
    dg_one, db_one, db_qv = own_vectors(flat_a, (width, width, 2 * width))
    return (
        m_out.at[:, 0].set(m_back).reshape(tokens.shape),
        g_out.at[:, 0].set(g_back).reshape(tokens.shape),
        dg_one, db_one, dw_qkv, db_qv, dw_proj, db_proj, dg_two, db_two, dw_up, db_up, dw_down, db_down,
    )


def solution(mesh):
    both = ("dp", "rows")
    frame, vector, matrix = P("dp", "rows", None, None), P(both), P(both, None)
    return jax.shard_map(
        per_device,
        mesh=mesh,
        in_specs=(
            frame, P("dp"), vector, vector, matrix, vector, matrix, vector,
            vector, vector, matrix, vector, matrix, vector, frame,
        ),
        out_specs=(
            frame, frame, vector, vector, matrix, vector, matrix, vector,
            vector, vector, matrix, vector, matrix, vector,
        ),
        check_vma=False,
    )
```

```python
import functools

import jax
import jax.numpy as jnp
from jax import lax
from jax.experimental import pallas as pl
from jax.experimental.pallas import tpu as pltpu
from jax.sharding import PartitionSpec as P

HEAD_DIM = 64
WIN = 8
HALF = WIN // 2
CELLS = WIN * WIN
LANES = 4 * HEAD_DIM
LANE = 128
ROWS = 16
EPSILON = 1e-05
INV_ROOT_TWO = 0.7071067811865476
INV_ROOT_TWO_PI = 0.3989422804014327
F32 = jnp.float32
BF16 = jnp.bfloat16
VMEM_LIMIT = 60 * 1024 * 1024


def from_behind(x, axis, by):
    devices = lax.axis_size(axis)
    return lax.ppermute(x, axis, [(i, (i + by) % devices) for i in range(devices)])


def dot(a, b):
    return jnp.dot(a, b, preferred_element_type=F32)


def dot_t(a, b):
    return lax.dot_general(a, b, (((1,), (1,)), ((), ())), preferred_element_type=F32)


def to_window_order(x, columns):
    depth = x.shape[-1]
    grid = pltpu.roll(x.reshape(WIN, columns, depth), columns - HALF, 1)
    grid = grid.reshape(WIN, columns // WIN, WIN, depth).swapaxes(0, 1)
    return grid.reshape(WIN * columns, depth)


def from_window_order(x, columns):
    depth = x.shape[-1]
    grid = x.reshape(columns // WIN, WIN, WIN, depth).swapaxes(0, 1)
    grid = pltpu.roll(grid.reshape(WIN, columns, depth), HALF, 1)
    return grid.reshape(WIN * columns, depth)


def normalize(values):
    center = values - jnp.mean(values, axis=-1, keepdims=True)
    inverse = lax.rsqrt(jnp.mean(center * center, axis=-1, keepdims=True) + EPSILON)
    return center * inverse, inverse


def norm_back(grad, normed, inverse):
    return inverse * (
        grad
        - jnp.mean(grad, axis=-1, keepdims=True)
        - normed * jnp.mean(grad * normed, axis=-1, keepdims=True)
    )


def block_diag(x):
    lane_head = lax.broadcasted_iota(jnp.int32, x.shape, 1) // HEAD_DIM
    zero = jnp.zeros_like(x)
    return jnp.concatenate(
        [jnp.where(lane_head == head, x, zero) for head in range(LANES // HEAD_DIM)], axis=0
    )


def dot_down(a, b):
    pair = 2 * HEAD_DIM
    first = lax.broadcasted_iota(jnp.int32, (CELLS, pair), 1) < HEAD_DIM
    out = []
    for lane in range(0, LANES, pair):
        both = lax.dot_general(
            a[:, lane : lane + pair],
            b[:, lane : lane + pair],
            (((0,), (0,)), ((), ())),
            preferred_element_type=F32,
        )
        out.append(jnp.where(first, both[:HEAD_DIM], both[HEAD_DIM:]))
    return jnp.concatenate(out, axis=1)


def window_bias(info, frames, step, win, columns, height, rows_here):
    frame = lax.rem(step, frames)
    level = info[frame]
    factor = jnp.where(level >= 2, 4, jnp.where(level >= 1, 2, 1))
    base = info[frames] * rows_here + (step // frames) * WIN
    row_limit, col_limit = height * factor // 4, columns * factor // 4
    last_row = (base + WIN >= height).astype(jnp.int32)
    last_col = jnp.int32(win == columns // WIN - 1)
    key = lax.broadcasted_iota(jnp.int32, (CELLS, LANES), 0)
    query = lax.broadcasted_iota(jnp.int32, (CELLS, LANES), 1) % CELLS
    row = base + key // WIN + HALF
    col = win * WIN + key % WIN + HALF
    row = jnp.where(row >= height, row - height, row)
    col = jnp.where(col >= columns, col - columns, col)
    differ = key ^ query
    bad = (differ // (HALF * WIN) % 2) * last_row + (differ // HALF % 2) * last_col
    bad = bad + (row >= row_limit).astype(jnp.int32) + (col >= col_limit).astype(jnp.int32)
    return jnp.where(bad > 0, -100.0, 0.0)


def place(info, at, pieces, targets, vec, vec_sem):
    blocks = [
        (source, k, core, i)
        for core, sources in enumerate(pieces)
        for i, (source, k) in enumerate((s, k) for s in sources for k in range(s.shape[0]))
    ]
    lanes = vec.shape[-1]
    start = 0
    for sources in pieces:
        for source in sources:
            count = source.shape[0]
            tail = source.at[:, :, pl.ds(source.shape[-1] - lanes, lanes)]
            pltpu.make_async_copy(tail, vec.at[pl.ds(start, count)], vec_sem).start()
            start += count
    for lane, lanes, rows, target, sem in targets:
        for source, k, core, i in blocks:
            block = info[at] ^ (bits_of(i) | core)
            for sub in range(rows // ROWS):
                row = pl.multiple_of(block * rows + sub * ROWS, ROWS)
                pltpu.make_async_copy(
                    source.at[k, :, pl.ds(lane + sub * lanes, lanes)], target.at[pl.ds(row, ROWS), :], sem
                ).start()


def halves(pieces):
    return pieces[: len(pieces) // 2], pieces[len(pieces) // 2 :]


def wait_bytes(target, sem):
    pltpu.make_async_copy(target, target, sem).wait()


def bits_of(j):
    return (j % 4) * 8 + (j // 8) * 4 + (j // 4 % 2) * 2


def natural_rows(vec):
    total = jnp.sum(vec[...].astype(F32), axis=0)
    return [total[r : r + 1, :] for r in range(total.shape[0])]


def hand_over(info, at, sources, tail, keep, send):
    for core, out in enumerate((keep, send)):
        for j in range(out.shape[0]):
            block = info[at] ^ (bits_of(j) | core)
            for lane, lanes, rows, source in sources:
                for sub in range(rows // ROWS):
                    row = pl.multiple_of(block * rows + sub * ROWS, ROWS)
                    start = lane + sub * lanes
                    out[j, :, start : start + lanes] = source[pl.ds(row, ROWS), :].astype(out.dtype)
            out[j, :, out.shape[-1] - tail.shape[-1] :] = tail.astype(out.dtype)


def store_rows(out, halo, held, sem, local, total, window_row, frame, value):
    slot = lax.rem(local, 2)
    half = out.shape[2]
    count = value.shape[0] // (2 * half)

    def finish(slot):
        for part in range(2 * count):
            rows = held.at[slot, pl.ds(part * half, half)]
            pltpu.make_async_copy(rows, rows, sem.at[slot, part]).wait()

    @pl.when(local >= 2)
    def _():
        finish(slot)

    held[slot] = value
    for i in range(count):
        at = frame + i
        top, bottom = (held.at[slot, pl.ds((2 * i + part) * half, half)] for part in range(2))
        top_sem, bottom_sem = sem.at[slot, 2 * i], sem.at[slot, 2 * i + 1]
        pltpu.make_async_copy(top, out.at[at, 1 + 2 * window_row], top_sem).start()

        @pl.when(window_row == 0)
        def _():
            pltpu.make_async_copy(bottom, out.at[at, 2], bottom_sem).start()

        if halo is not None:

            @pl.when(window_row == 1)
            def _():
                pltpu.make_async_copy(bottom, halo.at[at], bottom_sem).start()

    @pl.when(local == total - 1)
    def _():
        finish(slot)
        if total > 1:
            finish(1 - slot)


def attend_kernel(
    frames, columns, height, rows_here,
    info, top, own, halo, *rest,
):
    q_out, k_out, v_out, p_out, o_out, weight, vec, lines, sem = rest[-9:]
    step = pl.program_id(0)
    width = top.shape[-1]

    @pl.when(step == 0)
    def _():
        place(
            info, frames + 1, halves(rest[:-9]), [(0, 3 * width, ROWS, weight, sem.at[0])], vec, sem.at[1]
        )
        wait_bytes(weight, sem.at[0])
        wait_bytes(vec, sem.at[1])
        pieces = natural_rows(vec)
        per = width // LANE
        for line in range(lines.shape[0]):
            lines[line : line + 1, :] = jnp.concatenate(pieces[line * per : (line + 1) * per], axis=1)

    gain, bias, bias_q, bias_v = (lines.at[i : i + 1] for i in range(4))
    bottom = jnp.where(step < frames, own[...], halo[...])
    x = jnp.concatenate([top[...], bottom], axis=0).astype(F32)
    normed, _ = normalize(to_window_order(x, columns))
    hidden = (normed * gain[...] + bias[...]).astype(BF16)
    q_out[...] = (dot(hidden, weight[:, :width]) + bias_q[...]).astype(BF16) * 0.125
    k_out[...] = dot(hidden, weight[:, width : 2 * width]).astype(BF16)
    v_out[...] = (dot(hidden, weight[:, 2 * width :]) + bias_v[...]).astype(BF16)

    wins, groups = range(columns // WIN), range(width // LANES)
    items = [(w, slice(w * CELLS, (w + 1) * CELLS), slice(g * LANES, (g + 1) * LANES)) for w in wins for g in groups]
    masks = [window_bias(info, frames, step, w, columns, height, rows_here) for w in wins]
    scores = [dot_t(k_out[r, l], block_diag(q_out[r, l])) for _, r, l in items]
    exponents = []
    for (w, _, _), score in zip(items, scores):
        score = score + masks[w]
        exponents.append(jnp.exp(score - jnp.max(score, axis=0, keepdims=True)))
    probs = [(e * (1.0 / jnp.sum(e, axis=0, keepdims=True))).astype(BF16) for e in exponents]
    outs = [dot_down(p, v_out[r, l]).astype(BF16) for p, (_, r, l) in zip(probs, items)]
    for (_, r, l), p, out in zip(items, probs, outs):
        p_out[r, l] = p
        o_out[r, l] = out


def middle_kernel(
    frames, columns, chunk,
    info, top, own, halo, dtop, down, dhalo, o_in, *rest,
):
    (
        m_out, m_halo, dx_out, do_out, keep, send,
        w_proj, w_up, w_down, vec, lines, b_up, dw_proj, dw_up, dw_down_t, dw_down, small, g_s, du_s, held,
        sem, out_sem,
    ) = rest[-22:]
    step = pl.program_id(0)
    width = top.shape[-1]
    hidden_width = w_up.shape[-1]
    b_proj, g_two, b_two, b_down = (lines.at[i : i + 1] for i in range(4))

    @pl.when(step == 0)
    def _():
        targets = [
            (0, width, ROWS, w_proj, sem.at[0]),
            (width, hidden_width, ROWS, w_up, sem.at[1]),
            (width + hidden_width, width, w_down.shape[0] // 32, w_down, sem.at[2]),
        ]
        place(info, frames + 1, halves(rest[:-22]), targets, vec, sem.at[3])
        wait_bytes(vec, sem.at[3])
        pieces = natural_rows(vec)
        per = width // pieces[0].shape[-1]
        for line in range(4):
            lines[line : line + 1, :] = jnp.concatenate(pieces[line * per : (line + 1) * per], axis=1)
        b_up[...] = jnp.concatenate(pieces[4 * per :], axis=1)
        for target, copied in ((w_proj, sem.at[0]), (w_up, sem.at[1]), (w_down, sem.at[2])):
            wait_bytes(target, copied)
        dw_proj[...] = jnp.zeros_like(dw_proj)
        dw_up[...] = jnp.zeros_like(dw_up)
        dw_down_t[...] = jnp.zeros_like(dw_down_t)
        small[...] = jnp.zeros_like(small)

    count = top.shape[0]
    pairs = frames // count
    window_row = step // pairs

    def rows_of(top, own, halo):
        out = []
        for i in range(count):
            bottom = jnp.where(window_row == 0, own[i], halo[i])
            rows = jnp.concatenate([top[i], bottom], axis=0).astype(F32)
            out.append(to_window_order(rows, columns))
        return jnp.concatenate(out, axis=0)

    dy = rows_of(dtop, down, dhalo)
    dy_low = dy.astype(BF16)
    o_rows = o_in[...].reshape(-1, width)
    x2 = rows_of(top, own, halo) + dot(o_rows, w_proj[...]) + b_proj[...]
    parts = [slice(start, start + chunk) for start in range(0, hidden_width, chunk)]
    dgs = {0: dot_t(dy_low, w_down[parts[0], :])}
    normed, inverse = normalize(x2)
    h2 = (normed * g_two[...] + b_two[...]).astype(BF16)
    h2_t = h2.T
    dy_t = dy_low.T
    total = x2 + b_down[...]
    dh2 = jnp.zeros_like(x2)

    def enter(index):
        if index not in dgs:
            dgs[index] = dot_t(dy_low, w_down[parts[index], :])
        return dot(h2, w_up[:, parts[index]]) + b_up[:, parts[index]]

    ahead = enter(0)
    for index in range(len(parts) + 1):
        if index < len(parts):
            u, part = ahead, parts[index]
            if index + 1 < len(parts):
                ahead = enter(index + 1)
            phi = 0.5 * (1.0 + lax.erf(u * INV_ROOT_TWO))
            g_s[index % 2] = (u * phi).astype(BF16)
            du = dgs[index] * (phi + u * jnp.exp(-0.5 * u * u) * INV_ROOT_TWO_PI)
            du_s[index % 2] = du.astype(BF16)
            small[0:1, part] += jnp.sum(du, axis=0, keepdims=True)
        if index > 0:
            old, slot = parts[index - 1], (index - 1) % 2
            total += dot(g_s[slot], w_down[old, :])
            dh2 += dot_t(du_s[slot], w_up[:, old])
            dw_up[:, old] += dot(h2_t, du_s[slot])
            dw_down_t[:, old] += dot(dy_t, g_s[slot])
    block = total.shape[0] // count
    mixed = [from_window_order(total[i * block : (i + 1) * block], columns) for i in range(count)]
    mixed = jnp.concatenate(mixed, axis=0).astype(BF16)
    store_rows(
        m_out, m_halo, held, out_sem, step, pl.num_programs(0), window_row, lax.rem(step, pairs) * count, mixed
    )
    small[1:2, :width] += jnp.sum(dy, axis=0, keepdims=True)
    small[2:3, :width] += jnp.sum(dh2 * normed, axis=0, keepdims=True)
    small[3:4, :width] += jnp.sum(dh2, axis=0, keepdims=True)
    dx2 = dy + norm_back(dh2 * g_two[...], normed, inverse)
    da = dx2.astype(BF16)
    small[4:5, :width] += jnp.sum(dx2, axis=0, keepdims=True)
    dx_out[...] = dx2.reshape(dx_out.shape)
    dw_proj[...] += dot(o_rows.T, da)
    do_out[...] = dot_t(da, w_proj[...]).astype(BF16).reshape(do_out.shape)

    @pl.when(step == pl.num_programs(0) - 1)
    def _():
        for lane in range(0, hidden_width, LANE):
            dw_down[lane : lane + LANE, :] = dw_down_t[:, lane : lane + LANE].astype(BF16).T
        order = (4, 2, 3, 1)
        flat = jnp.concatenate([small[r : r + 1, :width] for r in order] + [small[0:1, :]], axis=1)
        lines_of = keep.shape[-1] - width - 2 * hidden_width
        tail = jnp.concatenate(
            [flat[:, i * lines_of : (i + 1) * lines_of] for i in range(ROWS)], axis=0
        )
        sources = [
            (0, width, ROWS, dw_proj),
            (width, hidden_width, ROWS, dw_up),
            (width + hidden_width, width, dw_down.shape[0] // 32, dw_down),
        ]
        hand_over(info, frames + 1, sources, tail, keep, send)


def back_kernel(
    frames, columns, first, count, with_halo, n_blocks, n_before, ends,
    info, top, own, halo, q_in, k_in, v_in, p_in, do_in, dx_in, *rest,
):
    blocks, rest = rest[:n_blocks], rest[n_blocks:]
    earlier = rest[1 + with_halo : n_before] if n_before else ()
    *outs, d_s, weight, vec, lines, held, sem, out_sem = rest[n_before:]
    g_out, g_halo = outs[0], outs[1] if with_halo else None
    if ends:
        keep, send, dw, small, *loaded = outs[1 + with_halo :]
    else:
        dw, small = outs[1 + with_halo :]
    local = pl.program_id(0)
    step = lax.rem(local + first, 2 * frames)
    width = top.shape[-1]
    gain, bias = (lines.at[i : i + 1] for i in range(2))

    @pl.when(local == 0)
    def _():
        place(
            info, frames + 1, halves(blocks), [(0, 3 * width, ROWS, weight, sem.at[0])], vec, sem.at[1]
        )
        dw[...] = jnp.zeros_like(dw)
        small[...] = jnp.zeros_like(small)
        if ends:
            for i, (source, target) in enumerate(zip(earlier, loaded)):
                pltpu.make_async_copy(source, target, sem.at[2 + i]).start()

    @pl.when(local == 0)
    def _():
        wait_bytes(weight, sem.at[0])
        wait_bytes(vec, sem.at[1])
        pieces = natural_rows(vec)
        per = width // LANE
        for line in range(lines.shape[0]):
            lines[line : line + 1, :] = jnp.concatenate(pieces[line * per : (line + 1) * per], axis=1)

    bottom = jnp.where(step < frames, own[...], halo[...])
    x = jnp.concatenate([top[...], bottom], axis=0).astype(F32)
    normed, inverse = normalize(to_window_order(x, columns))
    hidden = (normed * gain[...] + bias[...]).astype(BF16)
    hidden_t = hidden.T
    dh = jnp.zeros_like(normed)
    for at in range(0, width, LANES):
        l = slice(at, at + LANES)
        items = [slice(w * CELLS, (w + 1) * CELLS) for w in range(columns // WIN)]
        diags = [block_diag(do_in[r, l]) for r in items]
        dps = [dot_t(v_in[r, l], diag) for r, diag in zip(items, diags)]
        dvs = [dot(p_in[r, l], diag).astype(BF16) for r, diag in zip(items, diags)]
        dss = []
        for r, dp in zip(items, dps):
            full = p_in[r, l].astype(F32)
            dss.append((full * (dp - jnp.sum(dp * full, axis=0, keepdims=True))).astype(BF16))
        dks = [dot(ds, block_diag(q_in[r, l])).astype(BF16) for r, ds in zip(items, dss)]
        dqs = [(dot_down(ds, k_in[r, l]) * 0.125).astype(BF16) for r, ds in zip(items, dss)]
        for part, grads in enumerate((dqs, dks, dvs)):
            lane = slice(part * width + at, part * width + at + LANES)
            d = jnp.concatenate(grads, axis=0)
            dw[:, lane] += dot(hidden_t, d)
            small[0:1, lane] += jnp.sum(d.astype(F32), axis=0, keepdims=True)
            dh = dh + dot_t(d, weight[:, lane])

    small[1:2, :width] += jnp.sum(dh * normed, axis=0, keepdims=True)
    small[2:3, :width] += jnp.sum(dh, axis=0, keepdims=True)
    grad = dx_in[...] + norm_back(dh * gain[...], normed, inverse)
    grad = from_window_order(grad, columns).astype(BF16)
    store_rows(
        g_out, g_halo, held, out_sem, local, count, step // frames, lax.rem(step, frames), grad
    )

    if ends:

        @pl.when(local == count - 1)
        def _():
            for i, target in enumerate(loaded):
                wait_bytes(target, sem.at[2 + i])
                total = dw if i % 2 == 0 else small
                total[...] += target[...]
            pieces = [small[1:2, :width], small[2:3, :width], small[0:1, :width], small[0:1, 2 * width :]]
            flat = jnp.concatenate(pieces, axis=1)
            tail = jnp.concatenate([flat[:, i * LANE : (i + 1) * LANE] for i in range(ROWS)], axis=0)
            hand_over(info, frames + 1, [(0, 3 * width, ROWS, dw)], tail, keep, send)


def join_kernel(*refs):
    out = refs[-1]
    rows = refs[0].shape[0]
    for index, ref in enumerate(refs[:-1]):
        out[index * rows : (index + 1) * rows] = ref[...]


def join(*parts):
    shape = (len(parts) * parts[0].shape[0],) + parts[0].shape[1:]
    vmem = pl.BlockSpec(memory_space=pltpu.VMEM)
    return pl.pallas_call(
        join_kernel,
        out_shape=jax.ShapeDtypeStruct(shape, parts[0].dtype),
        in_specs=[vmem] * len(parts),
        out_specs=vmem,
        compiler_params=pltpu.CompilerParams(vmem_limit_bytes=VMEM_LIMIT),
        name="join",
    )(*parts)


def pack_kernel(index_ref, *refs):
    vectors, (qkv, proj, up, down, a_out, b_out) = refs[:-6], refs[-6:]
    index = index_ref[0]
    wide = 2 * LANE

    def spread_rows(sections, lanes):
        row = lax.broadcasted_iota(jnp.int32, (ROWS, wide), 0)
        total = jnp.zeros((ROWS, wide), F32)
        for ref, base in sections:
            count = ref.shape[0]
            at = base + index * count
            own = ref[...].astype(F32)[None, :]
            own = jnp.concatenate([own, jnp.zeros((1, wide - count), F32)], axis=1)
            moved = pltpu.roll(own, lax.rem(at, lanes), 1)
            total = total + jnp.where(row == at // lanes, moved, 0.0)
        return total[:, :lanes].astype(BF16)

    width = proj.shape[1]
    full = qkv.shape[1]
    a_out[:, :full] = qkv[...]
    sections = [(vectors[i], i * width) for i in range(3)]
    a_out[:, full:] = spread_rows(sections, a_out.shape[1] - full)
    hidden = up.shape[1]
    b_out[:, :width] = proj[...]
    b_out[:, width : width + hidden] = up[...]
    for i in range(down.shape[0] // ROWS):
        at = width + hidden + i * width
        b_out[:, at : at + width] = down[i * ROWS : (i + 1) * ROWS]
    full = width + 2 * hidden
    sections = [(vectors[3 + i], i * width) for i in range(5)]
    b_out[:, full:] = spread_rows(sections, b_out.shape[1] - full)


def pack(index, vectors, qkv, proj, up, down):
    lanes_a = qkv.shape[1] + LANE
    lanes_b = proj.shape[1] + 2 * up.shape[1] + 2 * LANE
    vmem = pl.BlockSpec(memory_space=pltpu.VMEM)
    return pl.pallas_call(
        pack_kernel,
        out_shape=[
            jax.ShapeDtypeStruct((ROWS, lanes_a), BF16),
            jax.ShapeDtypeStruct((ROWS, lanes_b), BF16),
        ],
        in_specs=[pl.BlockSpec(memory_space=pltpu.SMEM)] + [vmem] * (len(vectors) + 4),
        out_specs=[vmem, vmem],
        name="pack",
    )(index, *vectors, qkv, proj, up, down)


def grid_specs(frames, cells, width, first=0, which=0, count=None):
    turns = frames // (count or 1)
    at = lambda s: (s + first) % (2 * turns)
    top = pl.BlockSpec(
        (count, None, cells, width), lambda s, *_: (at(s) % turns, 1 + 2 * (at(s) // turns), 0, 0)
    )
    own = pl.BlockSpec(
        (count, None, cells, width), lambda s, *_: (jnp.minimum(at(s), turns - 1), 2, 0, 0)
    )
    halo = pl.BlockSpec(
        (None, count, cells, width), lambda s, *_: (which, jnp.maximum(at(s) - turns, 0), 0, 0)
    )
    return [top, own, halo]


def whole_out(shape):
    zeros = (0,) * len(shape)
    return pl.BlockSpec(shape, lambda s, *_: zeros, pipeline_mode=pl.Buffered(1))


ANYWHERE = pl.BlockSpec(memory_space=pl.ANY)


def params():
    return pltpu.CompilerParams(vmem_limit_bytes=VMEM_LIMIT, dimension_semantics=("arbitrary",))


def attend(info, tokens4, halo, blocks, height, columns):
    frames, groups, cells, width = tokens4.shape
    steps, block = 2 * frames, 2 * cells
    row = pl.BlockSpec((None, block, width), lambda s, *_: (s, 0, 0))
    shape = jax.ShapeDtypeStruct((steps, block, width), BF16)
    return pl.pallas_call(
        functools.partial(attend_kernel, frames, columns, height, groups * HALF),
        out_shape=[shape] * 5,
        grid_spec=pltpu.PrefetchScalarGridSpec(
            num_scalar_prefetch=1,
            grid=(steps,),
            in_specs=grid_specs(frames, cells, width) + [ANYWHERE] * len(blocks),
            out_specs=[row] * 5,
            scratch_shapes=[
                pltpu.VMEM((width, 3 * width), BF16),
                pltpu.VMEM((32, ROWS, LANE), BF16),
                pltpu.VMEM((4, width), F32),
                pltpu.SemaphoreType.DMA((2,)),
            ],
        ),
        compiler_params=params(),
        cost_estimate=pl.CostEstimate(flops=3 * 10**10, bytes_accessed=3 * 10**7, transcendentals=10**6),
        name="attend",
    )(info, tokens4, tokens4, halo, *blocks)


def middle(info, tokens4, halo, d4, o, blocks, hidden_width, columns, chunk=256, count=1):
    frames, groups, cells, width = tokens4.shape
    steps, block = 2 * frames, 2 * cells
    row = pl.BlockSpec((count, block, width), lambda s, *_: (s, 0, 0))
    ins = grid_specs(frames, cells, width, count=count)
    ins += grid_specs(frames, cells, width, which=1, count=count)
    mine = (16,) + blocks[0].shape[1:]
    return pl.pallas_call(
        functools.partial(middle_kernel, frames, columns, chunk),
        out_shape=[
            jax.ShapeDtypeStruct(tokens4.shape, BF16),
            jax.ShapeDtypeStruct(halo.shape[1:], BF16),
            jax.ShapeDtypeStruct((steps, block, width), F32),
            jax.ShapeDtypeStruct((steps, block, width), BF16),
            jax.ShapeDtypeStruct(mine, BF16),
            jax.ShapeDtypeStruct(mine, BF16),
        ],
        grid_spec=pltpu.PrefetchScalarGridSpec(
            num_scalar_prefetch=1,
            grid=(steps // count,),
            in_specs=ins + [row] + [ANYWHERE] * len(blocks),
            out_specs=[ANYWHERE, ANYWHERE, row, row, whole_out(mine), whole_out(mine)],
            scratch_shapes=[
                pltpu.VMEM((width, width), BF16),
                pltpu.VMEM((width, hidden_width), BF16),
                pltpu.VMEM((hidden_width, width), BF16),
                pltpu.VMEM((32, ROWS, 2 * LANE), BF16),
                pltpu.VMEM((4, width), F32),
                pltpu.VMEM((1, hidden_width), F32),
                pltpu.VMEM((width, width), F32),
                pltpu.VMEM((width, hidden_width), F32),
                pltpu.VMEM((width, hidden_width), F32),
                pltpu.VMEM((hidden_width, width), BF16),
                pltpu.VMEM((8, hidden_width), F32),
                pltpu.VMEM((2, count * block, chunk), BF16),
                pltpu.VMEM((2, count * block, chunk), BF16),
                pltpu.VMEM((2, count * block, width), BF16),
                pltpu.SemaphoreType.DMA((4,)),
                pltpu.SemaphoreType.DMA((2, 2 * count)),
            ],
        ),
        compiler_params=params(),
        cost_estimate=pl.CostEstimate(flops=9 * 10**10, bytes_accessed=4 * 10**7, transcendentals=10**7),
        name="middle",
    )(info, tokens4, tokens4, halo, d4, d4, halo, o, *blocks)


def back(info, tokens4, halo, q, k, v, p, do, dx, blocks, columns, before, first, count, ends):
    frames, groups, cells, width = tokens4.shape
    steps, block = 2 * frames, 2 * cells
    row = pl.BlockSpec((None, block, width), lambda s, *_: ((s + first) % steps, 0, 0))
    mine = (16,) + blocks[0].shape[1:]
    dw, small = (width, 3 * width), (8, 3 * width)
    handed = [jax.ShapeDtypeStruct(mine, BF16)] * 2
    sums = [jax.ShapeDtypeStruct(dw, F32), jax.ShapeDtypeStruct(small, F32)]
    in_vmem = [pltpu.VMEM(dw, F32), pltpu.VMEM(small, F32)]
    held = 10 + len(blocks)
    with_halo = first + count > frames
    g_shapes = [jax.ShapeDtypeStruct(tokens4.shape, BF16), jax.ShapeDtypeStruct(halo.shape[1:], BF16)]
    g_shapes = g_shapes[: 1 + with_halo]
    return pl.pallas_call(
        functools.partial(
            back_kernel, frames, columns, first, count, with_halo, len(blocks), len(before), ends
        ),
        out_shape=g_shapes + (handed if ends else sums),
        grid_spec=pltpu.PrefetchScalarGridSpec(
            num_scalar_prefetch=1,
            grid=(count,),
            in_specs=grid_specs(frames, cells, width, first)
            + [row] * 6
            + [ANYWHERE] * (len(blocks) + len(before)),
            out_specs=[ANYWHERE] * len(g_shapes)
            + ([whole_out(mine)] * 2 if ends else [whole_out(dw), whole_out(small)]),
            scratch_shapes=(in_vmem * ((len(before) - len(g_shapes)) // 2 + 1) if ends else [])
            + [
                pltpu.VMEM((block, 3 * width), BF16),
                pltpu.VMEM((width, 3 * width), BF16),
                pltpu.VMEM((32, ROWS, LANE), BF16),
                pltpu.VMEM((4, width), F32),
                pltpu.VMEM((2, block, width), BF16),
                pltpu.SemaphoreType.DMA((8,)),
                pltpu.SemaphoreType.DMA((2, 2)),
            ],
        ),
        input_output_aliases={held + i: i for i in range(len(g_shapes))} if before else {},
        compiler_params=params(),
        cost_estimate=pl.CostEstimate(
            flops=6 * 10**9 * count, bytes_accessed=5 * 10**6 * count, transcendentals=10**5
        ),
        name="back",
    )(info, tokens4, tokens4, halo, q, k, v, p, do, dx, *blocks, *before)


AXES = ("dp", "rows")


def flip_perm(axis, bits):
    return [(i, i ^ bits) for i in range(lax.axis_size(axis))]


def flipped(x, axis, bits):
    return lax.ppermute(x, axis, flip_perm(axis, bits))


def flipped_both(x, dp_bits, rows_bits):
    dp, rows = lax.axis_size("dp"), lax.axis_size("rows")
    pairs = [
        (d * rows + r, (d ^ dp_bits) * rows + (r ^ rows_bits)) for d in range(dp) for r in range(rows)
    ]
    return lax.ppermute(x, AXES, pairs)


def is_cube():
    return lax.axis_size("dp") == 8 and lax.axis_size("rows") == 4


def place_index():
    return lax.axis_index("dp") * lax.axis_size("rows") + lax.axis_index("rows")


def after(value, *others):
    return lax.optimization_barrier((value,) + others)[0]


def along_z(own):
    return [flipped(own, "dp", 2 * z) for z in (1, 2, 3)]


def over_plane(column):
    return [flipped(column, "rows", 2), flipped(column, "dp", 1), flipped_both(column, 1, 2)]


def gather_blocks(matrices, vectors):
    full = [lax.all_gather(m, AXES, axis=0, tiled=True) for m in matrices]
    lanes = []
    for m in full:
        per = m.shape[0] // 32
        blocks = m.reshape(32, per // ROWS, ROWS, m.shape[1]).transpose(0, 2, 1, 3)
        lanes.append(blocks.reshape(32, ROWS, -1))
    flat = jnp.concatenate([lax.all_gather(v, AXES, axis=0, tiled=True) for v in vectors])
    tail = flat.reshape(1, ROWS, -1)
    lanes.append(jnp.concatenate([tail, jnp.zeros((31,) + tail.shape[1:], tail.dtype)]))
    natural = jnp.concatenate(lanes, axis=2)
    relative = natural.reshape(4, 2, 2, 2, ROWS, -1).transpose(3, 1, 2, 0, 4, 5)
    relative = relative.reshape(2, 16, ROWS, -1)
    return relative[0], relative[1]


def own_rows(total, matrix_shapes, shards):
    matrices, lane = [], 0
    for rows, lanes in matrix_shapes:
        subs = rows // shards // ROWS
        pieces = [total[:, lane + i * lanes : lane + (i + 1) * lanes] for i in range(subs)]
        matrices.append(jnp.concatenate(pieces, axis=0))
        lane += subs * lanes
    return matrices, total[:, lane:].reshape(-1)


def wide(x):
    return x.astype(F32)


def sum_cores(keep, send):
    first = wide(keep) + wide(flipped(send, "rows", 1))
    return first[:4], first[4:].astype(BF16)


def sum_plane(kept, low):
    plane = (
        kept
        + wide(flipped(low[:4], "rows", 2))
        + wide(flipped(low[4:8], "dp", 1))
        + wide(flipped_both(low[8:], 1, 2))
    )
    return plane[0], plane[1:].astype(BF16)


def sum_line(kept, low):
    for z in (1, 2, 3):
        kept += wide(flipped(low[z - 1], "dp", 2 * z))
    return kept


def own_vectors(flat, vector_sizes):
    shards = lax.axis_size("dp") * lax.axis_size("rows")
    vectors, start = [], 0
    for size in vector_sizes:
        count = size // shards
        vectors.append(lax.dynamic_slice(flat, (start + place_index() * count,), (count,)))
        start += size
    return vectors


def scatter_sums(keep, send, matrix_shapes):
    matrices = []
    relative = jnp.stack([wide(keep), wide(send)]).reshape(2, 2, 2, 4, ROWS, -1)
    natural = relative.transpose(3, 1, 2, 0, 4, 5).reshape(32, ROWS, -1)
    lane = 0
    for rows, lanes in matrix_shapes:
        subs = rows // 32 // ROWS
        piece = natural[:, :, lane : lane + subs * lanes].reshape(32, ROWS, subs, lanes)
        whole_matrix = piece.transpose(0, 2, 1, 3).reshape(rows, lanes)
        matrices.append(lax.psum_scatter(whole_matrix, AXES, scatter_dimension=0, tiled=True))
        lane += subs * lanes
    flat = lax.psum(natural[0, :, lane:], AXES).reshape(-1)
    return matrices, flat


def per_device(
    tokens, frame_level, ln1_gain, ln1_bias, qkv_weight, qv_bias, proj_weight, proj_bias,
    ln2_gain, ln2_bias, fc1_weight, fc1_bias, fc2_weight, fc2_bias, d_out,
):
    frames, rows_here, columns, width = tokens.shape
    height = rows_here * lax.axis_size("rows")
    hidden_width = fc1_weight.shape[1]
    cells = HALF * columns
    grouped = (frames, rows_here // HALF, cells, width)
    tokens4, d4 = tokens.reshape(grouped), d_out.reshape(grouped)
    if is_cube():
        me = place_index().astype(jnp.int32)
        vectors = (
            ln1_gain, ln1_bias, qv_bias, proj_bias, ln2_gain, ln2_bias, fc2_bias, fc1_bias
        )
        own_a, own_b = pack(me[None], vectors, qkv_weight, proj_weight, fc1_weight, fc2_weight)
        z_a = along_z(own_a)
        halo = from_behind(jnp.stack([tokens4[:, 0], d4[:, 0]]), "rows", -1)
        column_a = join(own_a[None], *(z[None] for z in z_a))
        z_b = along_z(after(own_b, *z_a))
        mine_a = (column_a, *over_plane(column_a))
        z_b, halo = lax.optimization_barrier((z_b, halo))
        column_b = join(own_b[None], *(z[None] for z in z_b))
        *mine_a, column_b = lax.optimization_barrier((*mine_a, column_b))
        attend_blocks = (*mine_a, *(flipped(piece, "rows", 1) for piece in mine_a))
        mine_b = (column_b, *over_plane(column_b))
    else:
        me = jnp.int32(0)
        attend_blocks = gather_blocks((qkv_weight,), (ln1_gain, ln1_bias, qv_bias))
        middle_blocks = gather_blocks(
            (proj_weight, fc1_weight, fc2_weight), (proj_bias, ln2_gain, ln2_bias, fc2_bias, fc1_bias)
        )
        halo = from_behind(jnp.stack([tokens4[:, 0], d4[:, 0]]), "rows", -1)
    info = jnp.concatenate([frame_level, jnp.stack([lax.axis_index("rows").astype(jnp.int32), me])])
    q, k, v, p, o = attend(info, tokens4, halo, attend_blocks, height, columns)
    if is_cube():
        first_piece = flipped(mine_b[0], "rows", 1)
        *mine_b, o, first_piece = lax.optimization_barrier((*mine_b, o, first_piece))
        middle_blocks = (*mine_b, first_piece, *(flipped(piece, "rows", 1) for piece in mine_b[1:]))
    m_out, m_halo, dx, do, keep, send = middle(
        info, tokens4, halo, d4, o, middle_blocks, hidden_width, columns
    )
    m_back = from_behind(m_halo, "rows", 1)
    states = (info, tokens4, halo, q, k, v, p, do, dx, attend_blocks, columns)
    shapes_b = ((width, width), (width, hidden_width), (hidden_width, width))
    shapes_a = ((width, 3 * width),)
    if is_cube():
        shards = lax.axis_size("dp") * lax.axis_size("rows")
        cores_b = sum_cores(keep, send)
        part_a = back(*states, (), frames, 4, False)
        *part_a, cores_b, m_back = lax.optimization_barrier((*part_a, cores_b, m_back))
        plane_b = sum_plane(*cores_b)
        g_back = from_behind(part_a[1], "rows", 1)
        g_out, keep, send = back(*states, (part_a[0], *part_a[2:]), 0, 4, True)
        plane_b, send = lax.optimization_barrier((plane_b, send))
        plane_a = sum_plane(*sum_cores(keep, send))
        line_b = [flipped(plane_b[1][z - 1], "dp", 2 * z) for z in (1, 2, 3)]
        line_b, plane_a = lax.optimization_barrier((line_b, plane_a))
        sums_b, flat_b = own_rows(plane_b[0] + sum(wide(x) for x in line_b), shapes_b, shards)
        sums_a, flat_a = own_rows(sum_line(*plane_a), shapes_a, shards)
    else:
        sums_b, flat_b = scatter_sums(keep, send, shapes_b)
        before = back(*states, (), frames, frames, False)
        g_back = from_behind(before[1], "rows", 1)
        g_out, keep, send = back(*states, (before[0], *before[2:]), 0, frames, True)
        sums_a, flat_a = scatter_sums(keep, send, shapes_a)
    dw_proj, dw_up, dw_down = sums_b
    db_proj, dg_two, db_two, db_down, db_up = own_vectors(
        flat_b, (width, width, width, width, hidden_width)
    )
    (dw_qkv,) = sums_a
    dg_one, db_one, db_qv = own_vectors(flat_a, (width, width, 2 * width))
    return (
        m_out.at[:, 0].set(m_back).reshape(tokens.shape),
        g_out.at[:, 0].set(g_back).reshape(tokens.shape),
        dg_one, db_one, dw_qkv, db_qv, dw_proj, db_proj, dg_two, db_two, dw_up, db_up, dw_down, db_down,
    )


def solution(mesh):
    both = ("dp", "rows")
    frame, vector, matrix = P("dp", "rows", None, None), P(both), P(both, None)
    return jax.shard_map(
        per_device,
        mesh=mesh,
        in_specs=(
            frame, P("dp"), vector, vector, matrix, vector, matrix, vector,
            vector, vector, matrix, vector, matrix, vector, frame,
        ),
        out_specs=(
            frame, frame, vector, vector, matrix, vector, matrix, vector,
            vector, vector, matrix, vector, matrix, vector,
        ),
        check_vma=False,
    )
```
